256 devices in a mesh: clu: 64 (over y, z, core), rk: 4 (over x).
Axes of the slice: x: 4, y: 4, z: 8, core: 2. Of those that a mesh axis runs over, the one named last changes fastest.
Arguments:
- bases: float32 [64, 32, 256, 64], P('clu', None, None, 'rk'), may hold values from -0.4 to 0.4
- leaf_transfer: float32 [64, 32, 64, 64], P('clu')
- node_transfer: float32 [64, 64, 64], P('clu'), as said below
- pair_transfer: float32 [64, 64, 64], P('clu'), as said below
- quad_transfer: float32 [64, 64, 64], P('clu'), as said below
- coupling: float32 [64, 32, 32, 64, 64], P('clu', None, None, 'rk'), may hold values from -1.2 to 1.2
- row_device: int32 [64, 32, 32, 1], P('clu'), may hold values from 0 to 63; in each aligned block of 1024 rows (0 to 1023, 1024 to 2047, ..., all dimensions but the last counted through in order) at most 24 rows name the same one
- row_slot: int32 [64, 32, 32], P('clu'), may hold values from 0 to 31
- block_count: int32 [64, 32], P('clu'), may hold values from 16 to 32
Outputs:
- leaf_weights: float32 [64, 32, 64, 64], P('clu', None, None, 'rk')
- node_weights: float32 [4, 64, 64, 64], P(None, 'clu', None, 'rk')
- coupled: float32 [64, 32, 64, 64], P('clu', None, None, 'rk')
The draws below stay inside these ranges and needn't reach their ends.
Inputs may be any that keep to these rules, and one draw needn't show every extreme that they name: node_transfer[c] is drawn anew for every clu index. pair_transfer[c] equals pair_transfer[c xor 1]: one matrix for each node over two clu indices. quad_transfer[c] is the same for the four clu indices c of one node (equal c // 4). Among the 1024 listed blocks of one clu index, at most 24 name the same row_device.
All inputs are finite; a program needn't handle non-finite values.
Results may differ from the reference program's by a relative error of at most 0.00014.
Values sent between devices are 32-bit elements; how exact they have to be, the bound alone decides.
No kernel may reach another device: no remote copies, remote signals or barrier semaphores. Data moves between devices by JAX's collectives and lax.ppermute only.
A program may use at most 128 MiB of HBM per device.

```python
import math
import jax
import jax.numpy as jnp
import numpy as np
from jax import lax

K = 64
LEAFN = 256
BLK = 32
LEAF_DEV = 32
CAP = 24
N_CLU = 64


def transfer_block(key, shape, factor):
    spread = 0.3 * 3.0 ** 0.5 / K ** 0.5
    noise = jax.random.uniform(key, shape, jnp.float32, -spread, spread)
    return factor * (noise + 0.8 * jnp.eye(K, dtype=jnp.float32))


def draw_leaf_transfer(key, part):
    key = jax.random.fold_in(key, 11)
    return transfer_block(key, (N_CLU, LEAF_DEV, K, K), float(LEAF_DEV) ** (-0.5))


def draw_node_transfer(key, part):
    key = jax.random.fold_in(key, 12)
    return transfer_block(key, (N_CLU, K, K), 1.0)


def draw_pair_transfer(key, part):
    key = jax.random.fold_in(key, 13)
    return jnp.repeat(transfer_block(key, (N_CLU // 2, K, K), 1.0), 2, axis=0)


def draw_quad_transfer(key, part):
    key = jax.random.fold_in(key, 14)
    return jnp.repeat(transfer_block(key, (N_CLU // 4, K, K), 1.0), 4, axis=0)


def plant(array, stream_key, smallest, high):
    place = [jax.random.randint(jax.random.fold_in(stream_key, axis), (), 0, length) for axis, length in enumerate(array.shape)]
    main_axis = array.shape.index(max(array.shape))
    neighbour = place[:main_axis] + [(place[main_axis] + 1) % array.shape[main_axis]] + place[main_axis + 1:]
    return array.at[tuple(place)].set(smallest).at[tuple(neighbour)].set(high)


def levels(stream_key, shape, split, smallest, high):
    loudness = 1.0
    for axis_at, blocks in split:
        steps = jax.random.uniform(jax.random.fold_in(jax.random.fold_in(stream_key, 6), axis_at), (blocks,), jnp.float32, smallest / len(split), high / len(split))
        loudness = loudness * jnp.repeat(jnp.exp(steps), shape[axis_at] // blocks).reshape((-1,) + (1,) * (len(shape) - 1 - axis_at))
    return loudness


def routed_block(key, own, number, rows, number_of, top, most, slope):
    sequence = jax.random.permutation(key, number_of)
    heavy_load, ordinary = shares(number_of, rows * top, most, slope, True), shares(number_of, rows * top, most, slope, False)
    places = jnp.arange(number_of)

    def named(sizes, rotation):
        used = int((sizes > 0).sum())
        fixed = max(1, used // 4)
        shifted = fixed + (places - fixed + rotation * (used - fixed)) % max(1, number_of - fixed)
        return jnp.zeros((number_of,), jnp.int32).at[sequence[jnp.where(places < fixed, places, shifted)]].set(jnp.asarray(sizes, jnp.int32))

    sizes = jnp.where(number % 4 == 0, named(heavy_load, number // 4), named(ordinary, number - number // 4 - 1))
    mixed = jax.random.permutation(jax.random.fold_in(own, 3), number_of)
    source_of, sink = mixed[0:number_of // 2 * 2:2], mixed[1:number_of // 2 * 2:2]
    slack = jnp.minimum(sizes[source_of] - 1, most - sizes[sink]) // 2
    slack = jnp.where((source_of == sequence[0]) | (sink == sequence[0]) | (sizes[sink] == 0), 0, jnp.maximum(slack, 0))
    shifted = jax.random.randint(jax.random.fold_in(own, 4), (number_of // 2,), 0, 1 << 20) % (slack + 1)
    sizes = sizes.at[source_of].add(-shifted).at[sink].add(shifted)
    items = jnp.searchsorted(jnp.cumsum(sizes), jnp.arange(rows * top), side="right").astype(jnp.int32)
    listing = items.reshape(top, rows).T
    listing = listing[jax.random.permutation(jax.random.fold_in(own, 1), rows)]
    rotation = jax.random.randint(jax.random.fold_in(own, 2), (rows, 1), 0, top)
    return jnp.take_along_axis(listing, (jnp.arange(top)[None, :] + rotation) % top, axis=1)


def shares(amount, total, limit, slope, full):
    portions = [(1 << 20) // math.isqrt(rank ** slope) + 1 for rank in range(1, amount + 1)]
    largest = limit if full else min(limit, max(-(-total // amount), total * portions[0] // sum(portions)))
    least = 1 if total - largest >= amount - 1 else 0
    given, rest = [largest] + [least] * (amount - 1), total - largest - least * (amount - 1)
    while rest > 0:
        free = [i for i in range(1, amount) if given[i] < largest] or [i for i in range(1, amount) if given[i] < limit]
        whole, left = sum([portions[i] for i in free]), rest
        for i in free:
            extra = min(limit - given[i], max(1, left * portions[i] // whole), rest)
            given[i] = given[i] + extra
            rest = rest - extra
    return np.array(given)


def gaussian(key, dims, deviation, limit, cuts=(), kind=jnp.bfloat16):
    factor_of = levels(key, dims, cuts, -0.22, 0.18) if cuts else 1.0
    values = jax.random.normal(key, dims, jnp.float32) * deviation * factor_of
    return jnp.minimum(jnp.maximum(values, -limit), limit).astype(kind)


def setup_inputs(seed: int = 0) -> dict:
    seeds = jax.random.split(jax.random.key(seed), 10)
    bases = gaussian(seeds[0], (N_CLU, LEAF_DEV, LEAFN, K), 0.0625, 0.4, ((0, 64), (3, 4)), jnp.float32)
    leaf_transfer = draw_leaf_transfer(jax.random.fold_in(seeds[9], 71), 0)
    node_transfer = draw_node_transfer(jax.random.fold_in(seeds[9], 71), 0)
    pair_transfer = draw_pair_transfer(jax.random.fold_in(seeds[9], 71), 0)
    quad_transfer = draw_quad_transfer(jax.random.fold_in(seeds[9], 71), 0)
    coupling = gaussian(seeds[5], (N_CLU, LEAF_DEV, BLK, K, K), 0.2, 1.2, ((0, 64), (3, 4)), jnp.float32)
    row_device_keys = jax.random.split(jax.random.fold_in(seeds[6], 1), N_CLU * LEAF_DEV * BLK // (LEAF_DEV * BLK))
    row_device_turns = jax.random.permutation(jax.random.fold_in(seeds[6], 3), N_CLU * LEAF_DEV * BLK // (LEAF_DEV * BLK))
    row_device = jax.vmap(lambda own, number: routed_block(jax.random.fold_in(seeds[6], 2), own, number, LEAF_DEV * BLK, N_CLU, 1, CAP, 1))(row_device_keys, row_device_turns).reshape((N_CLU, LEAF_DEV, BLK, 1))
    row_slot = plant(jax.random.randint(seeds[7], (N_CLU, LEAF_DEV, BLK), 0, LEAF_DEV), jax.random.fold_in(seeds[7], 1), 0, LEAF_DEV - 1).astype(jnp.int32)
    block_count = plant(jax.random.randint(seeds[8], (N_CLU, LEAF_DEV), BLK // 2, BLK + 1), jax.random.fold_in(seeds[8], 1), BLK // 2, BLK).astype(jnp.int32)
    return {"bases": bases, "leaf_transfer": leaf_transfer, "node_transfer": node_transfer, "pair_transfer": pair_transfer, "quad_transfer": quad_transfer, "coupling": coupling, "row_device": row_device, "row_slot": row_slot, "block_count": block_count}


def upper_factor(gram):
    return jnp.swapaxes(jnp.linalg.cholesky(gram), -1, -2)

def reference(bases, leaf_transfer, node_transfer, pair_transfer, quad_transfer, coupling, row_device, row_slot, block_count):
    highest = lax.Precision.HIGHEST
    leaf_gram = jnp.einsum('cjpa,cjpb->cjab', bases, bases, precision=highest)
    moved = jnp.einsum('cjab,cjbe->cjae', leaf_gram, leaf_transfer, precision=highest)
    term = jnp.einsum('cjaf,cjae->cjfe', leaf_transfer, moved, precision=highest)
    level = jnp.sum(term, axis=1)
    grams = [level]
    clusters = jnp.arange(N_CLU, dtype=jnp.int32)
    for bit, transfer in enumerate((node_transfer, pair_transfer, quad_transfer)):
        moved = jnp.einsum('cab,cbe->cae', level, transfer, precision=highest)
        term = jnp.einsum('caf,cae->cfe', transfer, moved, precision=highest)
        level = term + term[clusters ^ 1 << bit]
        grams.append(level)
    node_weights = jnp.stack([upper_factor(g) for g in grams])
    leaf_factor = upper_factor(leaf_gram)
    target = (row_device[..., 0] * LEAF_DEV + row_slot).astype(jnp.int32)
    valid = jnp.arange(BLK, dtype=jnp.int32)[None, None, :] < block_count[:, :, None]
    target = jnp.where(valid, target, N_CLU * LEAF_DEV).astype(jnp.int32)

    def step(total, item):
        blocks, factor, dest = item
        prod = jnp.einsum('jkab,jcb->jkac', blocks, factor, precision=highest)
        total = total + jax.ops.segment_sum(prod.reshape(-1, K, K), dest.reshape(-1), num_segments=N_CLU * LEAF_DEV + 1)
        return (total, None)
    start = jnp.zeros((N_CLU * LEAF_DEV + 1, K, K), jnp.float32)
    total, unused = lax.scan(step, start, (coupling, leaf_factor, target))
    gathered = total[:-1].reshape(N_CLU, LEAF_DEV, K, K)
    coupled = jnp.einsum('cjab,cjbe->cjae', leaf_factor, gathered, precision=highest)
    return (leaf_factor, node_weights, coupled)
```

```python
import functools

import jax
import jax.numpy as jnp
from jax import lax
from jax.experimental import pallas as pl
from jax.experimental.pallas import tpu as pltpu
from jax.sharding import Mesh
from jax.sharding import PartitionSpec as P

HIGHEST = lax.Precision.HIGHEST
RANK = 64
TILE = 8
TILES = RANK // TILE


def shift(value, axis, step):
    size = lax.axis_size(axis)
    return lax.ppermute(value, axis, [(i, (i + step) % size) for i in range(size)])


def swap(value, axis, mask):
    return lax.ppermute(value, axis, [(i, i ^ mask) for i in range(lax.axis_size(axis))])


def factor_in_place(s_ref):
    batch = s_ref.shape[2]
    sub = lax.broadcasted_iota(jnp.int32, (TILE, batch), 0)
    for jb in range(TILES):
        count = TILES - jb
        base = jb * TILE
        rows = [
            [s_ref[base + k, pl.ds((jb + t) * TILE, TILE), :] for t in range(count)]
            for k in range(TILE)
        ]
        for k in range(TILE):
            scale = lax.rsqrt(rows[k][0][k : k + 1, :])
            row = [v * scale for v in rows[k]]
            row[0] = jnp.where(sub >= k, row[0], 0.0)
            rows[k] = row
            for t in range(count):
                s_ref[base + k, pl.ds((jb + t) * TILE, TILE), :] = row[t]
            for t in range(jb):
                s_ref[base + k, pl.ds(t * TILE, TILE), :] = jnp.zeros((TILE, batch), jnp.float32)
            for k2 in range(k + 1, TILE):
                s = row[0][k2 : k2 + 1, :]
                rows[k2] = [v - s * u for v, u in zip(rows[k2], row)]
        for rb in range(jb + 1, TILES):
            for r in range(rb * TILE, (rb + 1) * TILE):
                heads = [s_ref[base + k, pl.ds(r, 1), :] for k in range(TILE)]
                for ct in range(rb, TILES):
                    total = s_ref[r, pl.ds(ct * TILE, TILE), :]
                    for k in range(TILE):
                        total = total - heads[k] * rows[k][ct - jb]
                    s_ref[r, pl.ds(ct * TILE, TILE), :] = total


def to_lanes(g_ref, s_ref):
    for a in range(RANK):
        s_ref[a] = g_ref[:, a, :].T


def column_of(s_ref, c):
    return s_ref[:, c, :].T


def leaf_kernel(x_ref, gram_ref, packed_ref, s_ref):
    sources, leaves = x_ref.shape[0], x_ref.shape[1]
    for m in range(leaves):
        x = jnp.concatenate([x_ref[s, m] for s in range(sources)], axis=0)
        gram_ref[m] = lax.dot_general(
            x, x, (((1,), (1,)), ((), ())), precision=HIGHEST, preferred_element_type=jnp.float32
        )
    to_lanes(gram_ref, s_ref)
    factor_in_place(s_ref)
    half = RANK // 2
    for c in range(half):
        packed_ref[:, c, :] = jnp.concatenate(
            [column_of(s_ref, c), column_of(s_ref, c + half)], axis=1
        )


def leaf_factors(x):
    leaves = x.shape[1]
    return pl.pallas_call(
        leaf_kernel,
        out_shape=(
            jax.ShapeDtypeStruct((leaves, RANK, RANK), jnp.float32),
            jax.ShapeDtypeStruct((leaves, RANK // 2, 2 * RANK), jnp.float32),
        ),
        in_specs=[pl.BlockSpec(memory_space=pltpu.VMEM)],
        out_specs=(pl.BlockSpec(memory_space=pltpu.VMEM),) * 2,
        scratch_shapes=[pltpu.VMEM((RANK, RANK, leaves), jnp.float32)],
        compiler_params=pltpu.CompilerParams(vmem_limit_bytes=32 * 2**20),
        name="leaf_factors",
    )(x)


def node_kernel(g_ref, out_ref, s_ref):
    to_lanes(g_ref, s_ref)
    factor_in_place(s_ref)
    for c in range(RANK):
        out_ref[:, c, :] = column_of(s_ref, c)


def node_lower(grams):
    return pl.pallas_call(
        node_kernel,
        out_shape=jax.ShapeDtypeStruct(grams.shape, jnp.float32),
        in_specs=[pl.BlockSpec(memory_space=pltpu.VMEM)],
        out_specs=pl.BlockSpec(memory_space=pltpu.VMEM),
        scratch_shapes=[pltpu.VMEM((RANK, RANK, grams.shape[0]), jnp.float32)],
        compiler_params=pltpu.CompilerParams(vmem_limit_bytes=32 * 2**20),
        name="node_factors",
    )(grams)


def split(value):
    high = value.astype(jnp.bfloat16)
    return high, (value - high.astype(jnp.float32)).astype(jnp.bfloat16)


def product_kernel(half, place_ref, c_ref, l_ref, away_ref, keep_ref, acc_ref, sems):
    step = pl.program_id(0)
    per_step, listed, width, rank = c_ref.shape
    top = width // 2

    @pl.when(step == 0)
    def _():
        acc_ref[...] = jnp.zeros_like(acc_ref)

    zero = jnp.zeros((rank, rank), jnp.float32)
    for jj in range(per_step):
        packed = l_ref[jj]
        lower = jnp.concatenate([packed[:, :rank], packed[:, rank:]], axis=0)
        blocks = c_ref[jj]
        total = None
        for part, weight in (
            (blocks[:, :top, :], jnp.concatenate([lower, zero], axis=1)),
            (blocks[:, top:, :], jnp.concatenate([zero, lower], axis=1)),
        ):
            a_high, a_low = split(part.reshape(listed * top, rank))
            w_high, w_low = split(weight)
            for a, w in ((a_high, w_high), (a_low, w_high), (a_high, w_low)):
                term = jnp.dot(a, w, preferred_element_type=jnp.float32)
                total = term if total is None else total + term
        for k in range(listed):
            place = place_ref[(step * per_step + jj) * listed + k]
            acc_ref[place] = acc_ref[place] + total[k * top : (k + 1) * top, :]

    @pl.when(step == pl.num_programs(0) - 1)
    def _():
        first = pltpu.make_async_copy(acc_ref.at[pl.ds(0, half)], away_ref, sems.at[0])
        second = pltpu.make_async_copy(acc_ref.at[pl.ds(half, half)], keep_ref, sems.at[1])
        first.start()
        second.start()
        first.wait()
        second.wait()


def weighted_sums(place, blocks, packed, half):
    leaves, listed, width, rank = blocks.shape
    per_step = 4
    top = width // 2
    out = jax.ShapeDtypeStruct((half, top, 2 * rank), jnp.float32)
    return pl.pallas_call(
        functools.partial(product_kernel, half),
        grid_spec=pltpu.PrefetchScalarGridSpec(
            num_scalar_prefetch=1,
            grid=(leaves // per_step,),
            in_specs=[
                pl.BlockSpec((per_step, listed, width, rank), lambda i, p: (i, 0, 0, 0)),
                pl.BlockSpec((per_step, rank // 2, 2 * rank), lambda i, p: (i, 0, 0)),
            ],
            out_specs=(pl.BlockSpec(memory_space=pl.ANY),) * 2,
            scratch_shapes=[
                pltpu.VMEM((2 * half + TILE, top, 2 * rank), jnp.float32),
                pltpu.SemaphoreType.DMA((2,)),
            ],
        ),
        out_shape=(out, out),
        compiler_params=pltpu.CompilerParams(vmem_limit_bytes=48 * 2**20),
        name="weighted_sums",
    )(place, blocks, packed)


def shards(
    bases,
    leaf_transfer,
    node_transfer,
    pair_transfer,
    quad_transfer,
    coupling,
    row_device,
    row_slot,
    block_count,
):
    n_rank = lax.axis_size("rk")
    rank_index = lax.axis_index("rk")
    n_z = lax.axis_size("z")
    n_core = lax.axis_size("core")
    core = lax.axis_index("core")
    n_clu = lax.axis_size("y") * n_z * n_core
    local = jnp.swapaxes(bases[0], 1, 2)
    leaves, width, points = local.shape
    full_rank = width * n_rank
    share = leaves // n_rank

    blocks = coupling[0]
    listed = blocks.shape[1]
    half = (n_clu // n_core) * leaves
    dest = row_device[0, :, :, 0]
    valid = jnp.arange(listed, dtype=jnp.int32)[None, :] < block_count[0][:, None]
    own = (dest % n_core) == core
    place = jnp.where(own, half, 0) + (dest // n_core) * leaves + row_slot[0]
    place = jnp.where(valid, place, n_core * half).reshape(-1).astype(jnp.int32)

    pieces = lax.all_to_all(local, "rk", split_axis=0, concat_axis=0, tiled=True)
    gram, mine = leaf_factors(pieces.reshape(n_rank, share, width, points))
    packed = lax.all_gather(mine, "rk", axis=0, tiled=True)

    away, keep = weighted_sums(place, blocks, packed, half)
    dense = keep + swap(away, "core", 1)
    dense = lax.psum_scatter(dense, "y", scatter_dimension=0, tiled=True)
    gathered = lax.psum_scatter(dense, "z", scatter_dimension=0, tiled=True)

    lower = jnp.concatenate([packed[:, :, :full_rank], packed[:, :, full_rank:]], axis=1)
    gathered = gathered.reshape(leaves, width // 2, 2, full_rank)
    gathered = jnp.transpose(gathered, (0, 2, 1, 3)).reshape(leaves, width, full_rank)
    wide = lax.all_to_all(gathered, "rk", split_axis=2, concat_axis=1, tiled=True)
    coupled = jnp.einsum("jbe,jba->jea", wide, lower, precision=HIGHEST)

    moves = lax.dynamic_slice_in_dim(leaf_transfer[0], rank_index * share, share, 0)
    moved = jnp.einsum("jab,jbe->jae", gram, moves, precision=HIGHEST)
    level = jnp.einsum("jaf,jae->fe", moves, moved, precision=HIGHEST)
    level = level + swap(level, "rk", 1)
    level = level + swap(level, "rk", 2)
    grams = [level]
    partners = (("core", 1), ("z", 1), ("z", 2))
    for (axis, mask), transfer in zip(
        partners, (node_transfer[0], pair_transfer[0], quad_transfer[0])
    ):
        moved = jnp.dot(level, transfer, precision=HIGHEST)
        term = jnp.dot(transfer.T, moved, precision=HIGHEST)
        level = term + swap(term, axis, mask)
        grams.append(level)
    nodes = node_lower(jnp.stack(grams))

    node_weights = lax.dynamic_slice_in_dim(nodes, rank_index * width, width, 1)
    leaf_weights = lax.dynamic_slice_in_dim(lower, rank_index * width, width, 1)
    return (
        jnp.swapaxes(leaf_weights, 1, 2)[None],
        jnp.swapaxes(node_weights, 1, 2)[:, None],
        jnp.swapaxes(coupled, 1, 2)[None],
    )


def solution(mesh):
    devices = mesh.devices
    fine = Mesh(devices.reshape(4, 8, 2, devices.shape[1]), ("y", "z", "core", "rk"))
    clu = ("y", "z", "core")
    placed = (
        P(clu, None, None, "rk"),
        P(clu, None, None, None),
        P(clu, None, None),
        P(clu, None, None),
        P(clu, None, None),
        P(clu, None, None, "rk", None),
        P(clu, None, None, None),
        P(clu, None, None),
        P(clu, None),
    )
    return jax.shard_map(
        shards,
        mesh=fine,
        in_specs=placed,
        out_specs=(
            P(clu, None, None, "rk"),
            P(None, clu, None, "rk"),
            P(clu, None, None, "rk"),
        ),
        check_vma=False,
    )
```

```python
import functools

import jax
import jax.numpy as jnp
from jax import lax
from jax.experimental import pallas as pl
from jax.experimental.pallas import tpu as pltpu
from jax.sharding import Mesh
from jax.sharding import PartitionSpec as P

HIGHEST = lax.Precision.HIGHEST
RANK = 64
TILE = 8
TILES = RANK // TILE


def shift(value, axis, step):
    size = lax.axis_size(axis)
    return lax.ppermute(value, axis, [(i, (i + step) % size) for i in range(size)])


def swap(value, axis, mask):
    return lax.ppermute(value, axis, [(i, i ^ mask) for i in range(lax.axis_size(axis))])


def factor_in_place(s_ref):
    batch = s_ref.shape[2]
    sub = lax.broadcasted_iota(jnp.int32, (TILE, batch), 0)
    for jb in range(TILES):
        count = TILES - jb
        base = jb * TILE
        rows = [
            [s_ref[base + k, pl.ds((jb + t) * TILE, TILE), :] for t in range(count)]
            for k in range(TILE)
        ]
        for k in range(TILE):
            scale = lax.rsqrt(rows[k][0][k : k + 1, :])
            row = [v * scale for v in rows[k]]
            row[0] = jnp.where(sub >= k, row[0], 0.0)
            rows[k] = row
            for t in range(count):
                s_ref[base + k, pl.ds((jb + t) * TILE, TILE), :] = row[t]
            for t in range(jb):
                s_ref[base + k, pl.ds(t * TILE, TILE), :] = jnp.zeros((TILE, batch), jnp.float32)
            for k2 in range(k + 1, TILE):
                s = row[0][k2 : k2 + 1, :]
                rows[k2] = [v - s * u for v, u in zip(rows[k2], row)]
        for rb in range(jb + 1, TILES):
            for r in range(rb * TILE, (rb + 1) * TILE):
                heads = [s_ref[base + k, pl.ds(r, 1), :] for k in range(TILE)]
                for ct in range(rb, TILES):
                    total = s_ref[r, pl.ds(ct * TILE, TILE), :]
                    for k in range(TILE):
                        total = total - heads[k] * rows[k][ct - jb]
                    s_ref[r, pl.ds(ct * TILE, TILE), :] = total


def to_lanes(g_ref, s_ref):
    for a in range(RANK):
        s_ref[a] = g_ref[:, a, :].T


def column_of(s_ref, c):
    return s_ref[:, c, :].T


def leaf_kernel(x_ref, gram_ref, packed_ref, s_ref):
    sources, leaves = x_ref.shape[0], x_ref.shape[1]
    for m in range(leaves):
        x = jnp.concatenate([x_ref[s, m] for s in range(sources)], axis=0)
        gram_ref[m] = lax.dot_general(
            x, x, (((1,), (1,)), ((), ())), precision=HIGHEST, preferred_element_type=jnp.float32
        )
    to_lanes(gram_ref, s_ref)
    factor_in_place(s_ref)
    half = RANK // 2
    for c in range(half):
        packed_ref[:, c, :] = jnp.concatenate(
            [column_of(s_ref, c), column_of(s_ref, c + half)], axis=1
        )


def leaf_factors(x):
    leaves = x.shape[1]
    return pl.pallas_call(
        leaf_kernel,
        out_shape=(
            jax.ShapeDtypeStruct((leaves, RANK, RANK), jnp.float32),
            jax.ShapeDtypeStruct((leaves, RANK // 2, 2 * RANK), jnp.float32),
        ),
        in_specs=[pl.BlockSpec(memory_space=pltpu.VMEM)],
        out_specs=(pl.BlockSpec(memory_space=pltpu.VMEM),) * 2,
        scratch_shapes=[pltpu.VMEM((RANK, RANK, leaves), jnp.float32)],
        compiler_params=pltpu.CompilerParams(vmem_limit_bytes=32 * 2**20),
        name="leaf_factors",
    )(x)


def node_kernel(g_ref, out_ref, s_ref):
    to_lanes(g_ref, s_ref)
    factor_in_place(s_ref)
    for c in range(RANK):
        out_ref[:, c, :] = column_of(s_ref, c)


def node_lower(grams):
    return pl.pallas_call(
        node_kernel,
        out_shape=jax.ShapeDtypeStruct(grams.shape, jnp.float32),
        in_specs=[pl.BlockSpec(memory_space=pltpu.VMEM)],
        out_specs=pl.BlockSpec(memory_space=pltpu.VMEM),
        scratch_shapes=[pltpu.VMEM((RANK, RANK, grams.shape[0]), jnp.float32)],
        compiler_params=pltpu.CompilerParams(vmem_limit_bytes=32 * 2**20),
        name="node_factors",
    )(grams)


def split(value):
    high = value.astype(jnp.bfloat16)
    return high, (value - high.astype(jnp.float32)).astype(jnp.bfloat16)


def product_kernel(near, away, place_ref, c_ref, l_ref, first_ref, second_ref, keep_ref, acc_ref):
    leaves, listed, width, rank = c_ref.shape
    top = width // 2
    zero = jnp.zeros((rank, rank), jnp.bfloat16)
    acc_ref[...] = jnp.zeros_like(acc_ref)

    def leaf(j, carry):
        packed = l_ref[j]
        high, low = split(jnp.concatenate([packed[:, :rank], packed[:, rank:]], axis=0))
        blocks = c_ref[j]
        wide = jnp.concatenate(
            [
                blocks[:, :top, :].reshape(listed * top, rank),
                blocks[:, top:, :].reshape(listed * top, rank),
            ],
            axis=1,
        )
        w_high = jnp.concatenate(
            [jnp.concatenate([high, zero], axis=1), jnp.concatenate([zero, high], axis=1)], axis=0
        )
        w_low = jnp.concatenate(
            [jnp.concatenate([low, zero], axis=1), jnp.concatenate([zero, low], axis=1)], axis=0
        )
        c_high, c_low = split(wide)
        total = jnp.dot(
            jnp.concatenate([c_high, c_low], axis=1),
            jnp.concatenate([w_high, w_high], axis=0),
            preferred_element_type=jnp.float32,
        )
        total = total + jnp.dot(c_high, w_low, preferred_element_type=jnp.float32)
        for k in range(listed):
            place = place_ref[j * listed + k]
            acc_ref[place] = acc_ref[place] + total[k * top : (k + 1) * top, :]
        return carry

    lax.fori_loop(0, leaves, leaf, 0)
    first_ref[...] = acc_ref[:near]
    second_ref[...] = acc_ref[near:away]
    keep_ref[...] = acc_ref[away : 2 * away]


def weighted_sums(place, blocks, packed, near, away):
    leaves, listed, width, rank = blocks.shape
    top = width // 2
    vmem = pl.BlockSpec(memory_space=pltpu.VMEM)

    def out(rows):
        return jax.ShapeDtypeStruct((rows, top, 2 * rank), jnp.float32)

    return pl.pallas_call(
        functools.partial(product_kernel, near, away),
        in_specs=[pl.BlockSpec(memory_space=pltpu.SMEM), vmem, vmem],
        out_specs=(vmem, vmem, vmem),
        scratch_shapes=[pltpu.VMEM((2 * away + TILE, top, 2 * rank), jnp.float32)],
        out_shape=(out(near), out(away - near), out(away)),
        compiler_params=pltpu.CompilerParams(vmem_limit_bytes=32 * 2**20),
        name="weighted_sums",
    )(place, blocks, packed)


class Plan:
    def __init__(self, n_y, n_z, slots):
        self.cut = slots // 2
        self.rest = slots - self.cut
        self.order = (3, 1, 5, 7, 4, 2, 6, 0)
        self.spot = tuple(self.order.index(r) for r in range(n_z))
        self.y_rows = n_z * self.cut
        self.z_rows = n_y * self.rest
        self.base = {}
        at = 0
        for group in ("y2", "z4", "y1", "y3", "z3", "z1", "z5", "z7", "z2", "z6", "y0", "z0"):
            if group == "y1":
                self.near = at
            self.base[group] = at
            at += self.y_rows if group[0] == "y" else self.z_rows
        self.total = at
        self.n_y, self.n_z = n_y, n_z

    def rows(self, rel_y, rel_z, slot):
        base_y = sum(jnp.where(rel_y == r, self.base["y%d" % r], 0) for r in range(self.n_y))
        base_z = sum(jnp.where(rel_z == r, self.base["z%d" % r], 0) for r in range(self.n_z))
        spot = sum(jnp.where(rel_z == r, self.spot[r], 0) for r in range(self.n_z))
        by_y = base_y + spot * self.cut + slot
        by_z = base_z + rel_y * self.rest + slot - self.cut
        return jnp.where(slot < self.cut, by_y, by_z)


def sum_over_grid(plan, keep, first, second):
    near = plan.near

    def part(group, count=1, skip=0, rows=None):
        size = (plan.y_rows if group[0] == "y" else plan.z_rows) * count if rows is None else rows
        at = plan.base[group] + skip
        other = first[at : at + size] if at < near else second[at - near : at - near + size]
        return keep[at : at + size] + other

    half = plan.z_rows // 2
    y_far = shift(part("y2"), "y", 2)
    z_up2 = shift(part("z4", rows=half), "z", 2)
    z_down2 = shift(part("z4", skip=half, rows=half), "z", -2)
    y_up = shift(part("y1"), "y", 1)
    y_down = shift(part("y3"), "y", -1)
    z_up = shift(part("z3", 2), "z", 1)
    z_down = shift(part("z5", 2), "z", -1)
    rows = plan.z_rows
    pad = ((0, half), (0, 0), (0, 0))
    pad_low = ((half, 0), (0, 0), (0, 0))
    z_two = shift(part("z2") + z_up[:rows] + jnp.pad(z_up2, pad), "z", 2)
    z_six = shift(part("z6") + z_down[:rows] + jnp.pad(z_down2, pad_low), "z", -2)

    by_y = part("y0") + y_far + y_up + y_down
    cut = plan.cut
    up = shift(by_y[: 2 * cut], "z", 1)
    down = shift(by_y[2 * cut : 4 * cut], "z", -1)
    far = shift(by_y[4 * cut : 5 * cut], "z", 4)
    two = shift(by_y[5 * cut : 6 * cut] + up[:cut], "z", 2)
    six = shift(by_y[6 * cut : 7 * cut] + down[:cut], "z", -2)
    out_y = by_y[7 * cut :] + up[cut:] + down[cut:] + far + two + six

    by_z = part("z0") + z_up[rows:] + z_down[rows:] + z_two + z_six
    rest = plan.rest
    r1 = shift(by_z[rest : 2 * rest], "y", 1)
    r2 = shift(by_z[2 * rest : 3 * rest], "y", 2)
    r3 = shift(by_z[3 * rest :], "y", -1)
    out_z = by_z[:rest] + r1 + r2 + r3
    return jnp.concatenate([out_y, out_z], axis=0)


def shards(
    bases,
    leaf_transfer,
    node_transfer,
    pair_transfer,
    quad_transfer,
    coupling,
    row_device,
    row_slot,
    block_count,
):
    n_rank = lax.axis_size("rk")
    rank_index = lax.axis_index("rk")
    n_y, n_z, n_core = (lax.axis_size(axis) for axis in ("y", "z", "core"))
    core = lax.axis_index("core")
    local = jnp.swapaxes(bases[0], 1, 2)
    leaves, width, points = local.shape
    full_rank = width * n_rank
    share = leaves // n_rank

    blocks = coupling[0]
    listed = blocks.shape[1]
    plan = Plan(n_y, n_z, leaves)
    dest = row_device[0, :, :, 0]
    valid = jnp.arange(listed, dtype=jnp.int32)[None, :] < block_count[0][:, None]
    rel_z = (dest // n_core - lax.axis_index("z")) % n_z
    rel_y = (dest // (n_core * n_z) - lax.axis_index("y")) % n_y
    place = plan.rows(rel_y, rel_z, row_slot[0])
    place = place + jnp.where(dest % n_core == core, plan.total, 0)
    place = jnp.where(valid, place, 2 * plan.total).reshape(-1).astype(jnp.int32)

    pieces = lax.all_to_all(local, "rk", split_axis=0, concat_axis=0, tiled=True)
    gram, mine = leaf_factors(pieces.reshape(n_rank, share, width, points))
    packed = lax.all_gather(mine, "rk", axis=0, tiled=True)

    first, second, keep = weighted_sums(place, blocks, packed, plan.near, plan.total)
    first = swap(first, "core", 1)
    second = swap(second, "core", 1)
    gathered = sum_over_grid(plan, keep, first, second)

    lower = jnp.concatenate([packed[:, :, :full_rank], packed[:, :, full_rank:]], axis=1)
    gathered = gathered.reshape(leaves, width // 2, 2, full_rank)
    gathered = jnp.transpose(gathered, (0, 2, 1, 3)).reshape(leaves, width, full_rank)
    wide = lax.all_to_all(gathered, "rk", split_axis=2, concat_axis=1, tiled=True)
    coupled = jnp.einsum("jbe,jba->jea", wide, lower, precision=HIGHEST)

    moves = lax.dynamic_slice_in_dim(leaf_transfer[0], rank_index * share, share, 0)
    moved = jnp.einsum("jab,jbe->jae", gram, moves, precision=HIGHEST)
    level = jnp.einsum("jaf,jae->fe", moves, moved, precision=HIGHEST)
    level = level + swap(level, "rk", 1)
    level = level + swap(level, "rk", 2)
    grams = [level]
    partners = (("core", 1), ("z", 1), ("z", 2))
    for (axis, mask), transfer in zip(
        partners, (node_transfer[0], pair_transfer[0], quad_transfer[0])
    ):
        moved = jnp.dot(level, transfer, precision=HIGHEST)
        term = jnp.dot(transfer.T, moved, precision=HIGHEST)
        level = term + swap(term, axis, mask)
        grams.append(level)
    nodes = node_lower(jnp.stack(grams))

    node_weights = lax.dynamic_slice_in_dim(nodes, rank_index * width, width, 1)
    leaf_weights = lax.dynamic_slice_in_dim(lower, rank_index * width, width, 1)
    return (
        jnp.swapaxes(leaf_weights, 1, 2)[None],
        jnp.swapaxes(node_weights, 1, 2)[:, None],
        jnp.swapaxes(coupled, 1, 2)[None],
    )


def solution(mesh):
    devices = mesh.devices
    fine = Mesh(devices.reshape(4, 8, 2, devices.shape[1]), ("y", "z", "core", "rk"))
    clu = ("y", "z", "core")
    placed = (
        P(clu, None, None, "rk"),
        P(clu, None, None, None),
        P(clu, None, None),
        P(clu, None, None),
        P(clu, None, None),
        P(clu, None, None, "rk", None),
        P(clu, None, None, None),
        P(clu, None, None),
        P(clu, None),
    )
    return jax.shard_map(
        shards,
        mesh=fine,
        in_specs=placed,
        out_specs=(
            P(clu, None, None, "rk"),
            P(None, clu, None, "rk"),
            P(clu, None, None, "rk"),
        ),
        check_vma=False,
    )
```

```python
import functools

import jax
import jax.numpy as jnp
from jax import lax
from jax.experimental import pallas as pl
from jax.experimental.pallas import tpu as pltpu
from jax.sharding import Mesh
from jax.sharding import PartitionSpec as P

HIGHEST = lax.Precision.HIGHEST
RANK = 64
TILE = 8
TILES = RANK // TILE


def shift(value, axis, step):
    size = lax.axis_size(axis)
    return lax.ppermute(value, axis, [(i, (i + step) % size) for i in range(size)])


def swap(value, axis, mask):
    return lax.ppermute(value, axis, [(i, i ^ mask) for i in range(lax.axis_size(axis))])


def factor_in_place(s_ref):
    batch = s_ref.shape[2]
    sub = lax.broadcasted_iota(jnp.int32, (TILE, batch), 0)
    for jb in range(TILES):
        count = TILES - jb
        base = jb * TILE
        rows = [
            [s_ref[base + k, pl.ds((jb + t) * TILE, TILE), :] for t in range(count)]
            for k in range(TILE)
        ]
        for k in range(TILE):
            scale = lax.rsqrt(rows[k][0][k : k + 1, :])
            row = [v * scale for v in rows[k]]
            row[0] = jnp.where(sub >= k, row[0], 0.0)
            rows[k] = row
            for t in range(count):
                s_ref[base + k, pl.ds((jb + t) * TILE, TILE), :] = row[t]
            for t in range(jb):
                s_ref[base + k, pl.ds(t * TILE, TILE), :] = jnp.zeros((TILE, batch), jnp.float32)
            for k2 in range(k + 1, TILE):
                s = row[0][k2 : k2 + 1, :]
                rows[k2] = [v - s * u for v, u in zip(rows[k2], row)]
        for rb in range(jb + 1, TILES):
            for r in range(rb * TILE, (rb + 1) * TILE):
                heads = [s_ref[base + k, pl.ds(r, 1), :] for k in range(TILE)]
                for ct in range(rb, TILES):
                    total = s_ref[r, pl.ds(ct * TILE, TILE), :]
                    for k in range(TILE):
                        total = total - heads[k] * rows[k][ct - jb]
                    s_ref[r, pl.ds(ct * TILE, TILE), :] = total


def to_lanes(g_ref, s_ref):
    for a in range(RANK):
        s_ref[a] = g_ref[:, a, :].T


def column_of(s_ref, c):
    return s_ref[:, c, :].T


def packed_rows(matrix):
    half = matrix.shape[0] // 2
    return jnp.concatenate([matrix[:half], matrix[half:]], axis=1)


def unpacked(rows):
    half = rows.shape[-1] // 2
    return jnp.concatenate([rows[..., :half], rows[..., half:]], axis=-2)


def leaf_kernel(x_ref, move_ref, packed_ref, gram_ref, s_ref):
    sources, leaves = x_ref.shape[0], x_ref.shape[1]
    term = None
    for m in range(leaves):
        x = jnp.concatenate([x_ref[s, m] for s in range(sources)], axis=0)
        gram_ref[m] = lax.dot_general(
            x, x, (((1,), (1,)), ((), ())), precision=HIGHEST, preferred_element_type=jnp.float32
        )
    to_lanes(gram_ref, s_ref)
    for m in range(leaves):
        move = move_ref[m]
        moved = jnp.dot(gram_ref[m], move, precision=HIGHEST, preferred_element_type=jnp.float32)
        last = jnp.dot(move.T, moved, precision=HIGHEST, preferred_element_type=jnp.float32)
        term = last if term is None else term + last
    packed_ref[leaves] = packed_rows(term)
    factor_in_place(s_ref)
    half = RANK // 2
    for c in range(half):
        packed_ref[:leaves, c, :] = jnp.concatenate(
            [column_of(s_ref, c), column_of(s_ref, c + half)], axis=1
        )


def leaf_factors(x, moves):
    leaves = x.shape[1]
    vmem = pl.BlockSpec(memory_space=pltpu.VMEM)
    return pl.pallas_call(
        leaf_kernel,
        out_shape=jax.ShapeDtypeStruct((leaves + 1, RANK // 2, 2 * RANK), jnp.float32),
        in_specs=[vmem, vmem],
        out_specs=vmem,
        scratch_shapes=[
            pltpu.VMEM((leaves, RANK, RANK), jnp.float32),
            pltpu.VMEM((RANK, RANK, leaves), jnp.float32),
        ],
        compiler_params=pltpu.CompilerParams(vmem_limit_bytes=32 * 2**20),
        name="leaf_factors",
    )(x, moves)


def node_kernel(g_ref, out_ref, s_ref):
    to_lanes(g_ref, s_ref)
    factor_in_place(s_ref)
    for c in range(RANK):
        out_ref[:, c, :] = column_of(s_ref, c)


def node_lower(grams):
    return pl.pallas_call(
        node_kernel,
        out_shape=jax.ShapeDtypeStruct(grams.shape, jnp.float32),
        in_specs=[pl.BlockSpec(memory_space=pltpu.VMEM)],
        out_specs=pl.BlockSpec(memory_space=pltpu.VMEM),
        scratch_shapes=[pltpu.VMEM((RANK, RANK, grams.shape[0]), jnp.float32)],
        compiler_params=pltpu.CompilerParams(vmem_limit_bytes=32 * 2**20),
        name="node_factors",
    )(grams)


def split(value):
    high = value.astype(jnp.bfloat16)
    return high, (value - high.astype(jnp.float32)).astype(jnp.bfloat16)


def block_products(blocks, packed):
    listed, width, rank = blocks.shape
    top = width // 2
    zero = jnp.zeros((rank, rank), jnp.bfloat16)
    high, low = split(unpacked(packed))
    wide = jnp.concatenate(
        [
            blocks[:, :top, :].reshape(listed * top, rank),
            blocks[:, top:, :].reshape(listed * top, rank),
        ],
        axis=1,
    )
    w_high = jnp.concatenate(
        [jnp.concatenate([high, zero], axis=1), jnp.concatenate([zero, high], axis=1)], axis=0
    )
    w_low = jnp.concatenate(
        [jnp.concatenate([low, zero], axis=1), jnp.concatenate([zero, low], axis=1)], axis=0
    )
    c_high, c_low = split(wide)
    total = jnp.dot(
        jnp.concatenate([c_high, c_low], axis=1),
        jnp.concatenate([w_high, w_high], axis=0),
        preferred_element_type=jnp.float32,
    )
    return total + jnp.dot(c_high, w_low, preferred_element_type=jnp.float32)


def product_kernel(
    near, away, place_ref, c_hbm, l_ref, first_ref, second_ref, keep_ref, acc_ref, c_ref, sems
):
    leaves, listed, width, _ = c_hbm.shape
    slots, group = c_ref.shape[0], c_ref.shape[1]
    steps = leaves // group
    top = width // 2
    share = l_ref.shape[1] - 1

    def fetch(step, slot):
        return pltpu.make_async_copy(
            c_hbm.at[pl.ds(step * group, group)], c_ref.at[slot], sems.at[slot]
        )

    for step in range(slots - 1):
        fetch(step, step).start()
    acc_ref[...] = jnp.zeros_like(acc_ref)

    def body(step, carry):
        slot = lax.rem(step, slots)
        ahead = step + slots - 1

        @pl.when(ahead < steps)
        def _():
            fetch(ahead, lax.rem(ahead, slots)).start()

        fetch(step, slot).wait()
        source = lax.div(step * group, share)
        first_leaf = step * group - source * share
        totals = [
            block_products(c_ref[slot, u], l_ref[source, first_leaf + u]) for u in range(group)
        ]
        for u in range(group):
            for k in range(listed):
                place = place_ref[(step * group + u) * listed + k]
                acc_ref[place] = acc_ref[place] + totals[u][k * top : (k + 1) * top, :]
        return carry

    lax.fori_loop(0, steps, body, 0)
    first_ref[...] = acc_ref[:near]
    second_ref[...] = acc_ref[near:away]
    keep_ref[...] = acc_ref[away : 2 * away]


def weighted_sums(place, blocks, packed, near, away):
    leaves, listed, width, rank = blocks.shape
    top = width // 2
    group, slots = 4, 4
    vmem = pl.BlockSpec(memory_space=pltpu.VMEM)

    def out(rows):
        return jax.ShapeDtypeStruct((rows, top, 2 * rank), jnp.float32)

    return pl.pallas_call(
        functools.partial(product_kernel, near, away),
        in_specs=[
            pl.BlockSpec(memory_space=pltpu.SMEM),
            pl.BlockSpec(memory_space=pl.ANY),
            vmem,
        ],
        out_specs=(vmem, vmem, vmem),
        scratch_shapes=[
            pltpu.VMEM((2 * away + TILE, top, 2 * rank), jnp.float32),
            pltpu.VMEM((slots, group, listed, width, rank), jnp.float32),
            pltpu.SemaphoreType.DMA((slots,)),
        ],
        out_shape=(out(near), out(away - near), out(away)),
        compiler_params=pltpu.CompilerParams(vmem_limit_bytes=32 * 2**20),
        name="weighted_sums",
    )(place, blocks, packed)


def pack_kernel(
    cut, me_ref, y_ref, up_ref, down_ref, far_ref, two_ref, six_ref,
    z_ref, r1_ref, r2_ref, r3_ref, o0_ref, o1_ref, o2_ref, o3_ref, g_ref, m_ref,
):
    slots = g_ref.shape[0]
    rest = slots - cut
    g_ref[:cut] = (
        y_ref[7 * cut :] + up_ref[cut:] + down_ref[cut:] + far_ref[...] + two_ref[...] + six_ref[...]
    )
    g_ref[cut:] = z_ref[:rest] + r1_ref[...] + r2_ref[...] + r3_ref[...]
    chunks = m_ref.shape[0]
    piece = RANK // chunks
    batch = 2 * RANK // piece
    for g in range(slots // batch):
        rows = [g_ref[g * batch + q] for q in range(batch)]
        for c in range(chunks):
            for h in range(2):
                at = h * RANK + c * piece
                m_ref[c, 2 * g + h] = jnp.concatenate([r[:, at : at + piece] for r in rows], axis=1)
    for step, o_ref in enumerate((o0_ref, o1_ref, o2_ref, o3_ref)):
        o_ref[...] = m_ref[lax.rem(me_ref[0] + step, chunks)]


def pack(me, cut, slots, arrays):
    vmem = pl.BlockSpec(memory_space=pltpu.VMEM)
    top, lanes = arrays[0].shape[1:]
    tiles = slots * RANK // 4 * top * 2 // (top * lanes)
    message = jax.ShapeDtypeStruct((tiles, top, lanes), jnp.float32)
    return pl.pallas_call(
        functools.partial(pack_kernel, cut),
        in_specs=[pl.BlockSpec(memory_space=pltpu.SMEM)] + [vmem] * len(arrays),
        out_specs=(vmem,) * 4,
        out_shape=(message,) * 4,
        scratch_shapes=[
            pltpu.VMEM((slots, top, lanes), jnp.float32),
            pltpu.VMEM((4, tiles, top, lanes), jnp.float32),
        ],
        compiler_params=pltpu.CompilerParams(vmem_limit_bytes=16 * 2**20),
        name="pack",
    )(me, *arrays)


def final_kernel(me_ref, l_ref, m0_ref, m1_ref, m2_ref, m3_ref, out_ref, m_ref):
    chunks, tiles = m_ref.shape[0], m_ref.shape[1]
    for step, ref in enumerate((m0_ref, m1_ref, m2_ref, m3_ref)):
        m_ref[lax.rem(me_ref[0] + chunks - step, chunks)] = ref[...]
    share = l_ref.shape[1] - 1
    piece = RANK // chunks
    batch = 2 * RANK // piece
    for g in range(tiles // 2):
        rows = [m_ref[c, 2 * g + h] for c in range(chunks) for h in range(2)]
        turned = jnp.concatenate(rows, axis=0).T
        for q in range(batch):
            j = g * batch + q
            out_ref[j] = jnp.dot(
                turned[q * piece : (q + 1) * piece, :],
                unpacked(l_ref[j // share, j % share]),
                precision=HIGHEST,
                preferred_element_type=jnp.float32,
            )


def final(me, packed, messages, slots):
    vmem = pl.BlockSpec(memory_space=pltpu.VMEM)
    return pl.pallas_call(
        final_kernel,
        in_specs=[pl.BlockSpec(memory_space=pltpu.SMEM)] + [vmem] * 5,
        out_specs=vmem,
        out_shape=jax.ShapeDtypeStruct((slots, RANK // 4, RANK), jnp.float32),
        scratch_shapes=[pltpu.VMEM((4,) + messages[0].shape, jnp.float32)],
        compiler_params=pltpu.CompilerParams(vmem_limit_bytes=16 * 2**20),
        name="left_factor",
    )(me, packed, *messages)


class Plan:
    def __init__(self, n_y, n_z, slots):
        self.cut = 9 * slots // 16
        self.rest = slots - self.cut
        self.order = (3, 1, 5, 7, 4, 2, 6, 0)
        self.spot = tuple(self.order.index(r) for r in range(n_z))
        self.y_rows = n_z * self.cut
        self.z_rows = n_y * self.rest
        self.base = {}
        at = 0
        for group in ("y2", "z4", "y1", "y3", "z3", "z1", "z5", "z7", "z2", "z6", "y0", "z0"):
            if group == "y1":
                self.near = at
            self.base[group] = at
            at += self.y_rows if group[0] == "y" else self.z_rows
        self.total = at
        self.n_y, self.n_z = n_y, n_z

    def rows(self, rel_y, rel_z, slot):
        base_y = sum(jnp.where(rel_y == r, self.base["y%d" % r], 0) for r in range(self.n_y))
        base_z = sum(jnp.where(rel_z == r, self.base["z%d" % r], 0) for r in range(self.n_z))
        spot = sum(jnp.where(rel_z == r, self.spot[r], 0) for r in range(self.n_z))
        by_y = base_y + spot * self.cut + slot
        by_z = base_z + rel_y * self.rest + slot - self.cut
        return jnp.where(slot < self.cut, by_y, by_z)


def tie(*values):
    return lax.optimization_barrier(values)


def shards(
    bases,
    leaf_transfer,
    node_transfer,
    pair_transfer,
    quad_transfer,
    coupling,
    row_device,
    row_slot,
    block_count,
):
    n_rank = lax.axis_size("rk")
    rank_index = lax.axis_index("rk")
    me = rank_index.astype(jnp.int32).reshape(1)
    n_y, n_z, n_core = (lax.axis_size(axis) for axis in ("y", "z", "core"))
    core = lax.axis_index("core")
    local = jnp.swapaxes(bases[0], 1, 2)
    leaves, width, points = local.shape
    share = leaves // n_rank

    blocks = coupling[0]
    listed = blocks.shape[1]
    plan = Plan(n_y, n_z, leaves)
    dest = row_device[0, :, :, 0]
    valid = jnp.arange(listed, dtype=jnp.int32)[None, :] < block_count[0][:, None]
    rel_z = (dest // n_core - lax.axis_index("z")) % n_z
    rel_y = (dest // (n_core * n_z) - lax.axis_index("y")) % n_y
    place = plan.rows(rel_y, rel_z, row_slot[0])
    place = place + jnp.where(dest % n_core == core, plan.total, 0)
    place = jnp.where(valid, place, 2 * plan.total).reshape(-1).astype(jnp.int32)

    pieces = lax.all_to_all(local, "rk", split_axis=0, concat_axis=0, tiled=True)
    moves = lax.dynamic_slice_in_dim(leaf_transfer[0], rank_index * share, share, 0)
    mine = leaf_factors(pieces.reshape(n_rank, share, width, points), moves)
    packed = lax.all_gather(mine, "rk", axis=0, tiled=False)

    first, second, keep = weighted_sums(place, blocks, packed, plan.near, plan.total)
    first = swap(first, "core", 1)
    second = swap(second, "core", 1)
    near = plan.near

    def part(group, count=1, skip=0, rows=None):
        size = (plan.y_rows if group[0] == "y" else plan.z_rows) * count if rows is None else rows
        at = plan.base[group] + skip
        other = first[at : at + size] if at < near else second[at - near : at - near + size]
        return keep[at : at + size] + other

    def level_term(level, transfer):
        moved = jnp.dot(level, transfer, precision=HIGHEST)
        return jnp.dot(transfer.T, moved, precision=HIGHEST)

    rows = plan.z_rows
    half = rows // 2
    y_far, z_up2, z_down2, z_up, z_down, y_up, y_down, terms = tie(
        part("y2"),
        part("z4", rows=half),
        part("z4", skip=half, rows=half),
        part("z3", 2),
        part("z5", 2),
        part("y1"),
        part("y3"),
        packed[:, share],
    )
    y_far = shift(y_far, "y", 2)
    z_up2 = shift(z_up2, "z", 2)
    z_down2 = shift(z_down2, "z", -2)
    z_up = shift(z_up, "z", 1)
    z_down = shift(z_down, "z", -1)
    grams = [unpacked(jnp.sum(terms, axis=0))]
    term = level_term(grams[0], node_transfer[0])
    other = swap(term, "core", 1)

    y_far, z_up2, z_down2, z_up, z_down, y_up, y_down, other = tie(
        y_far, z_up2, z_down2, z_up, z_down, y_up, y_down, other
    )
    z_two = part("z2") + z_up[:rows] + jnp.pad(z_up2, ((0, half), (0, 0), (0, 0)))
    z_six = part("z6") + z_down[:rows] + jnp.pad(z_down2, ((half, 0), (0, 0), (0, 0)))
    y_up, y_down, z_two, z_six, other = tie(y_up, y_down, z_two, z_six, other)
    y_up = shift(y_up, "y", 1)
    y_down = shift(y_down, "y", -1)
    z_two = shift(z_two, "z", 2)
    z_six = shift(z_six, "z", -2)
    grams.append(term + other)
    term = level_term(grams[1], pair_transfer[0])
    other = swap(term, "z", 1)

    y_up, y_down, z_two, z_six, other = tie(y_up, y_down, z_two, z_six, other)
    by_y = part("y0") + y_far + y_up + y_down
    by_z = part("z0") + z_up[rows:] + z_down[rows:] + z_two + z_six
    cut, rest = plan.cut, plan.rest
    by_y, by_z, other = tie(by_y, by_z, other)
    up = shift(by_y[: 2 * cut], "z", 1)
    down = shift(by_y[2 * cut : 4 * cut], "z", -1)
    far = shift(by_y[4 * cut : 5 * cut], "z", 4)
    r1 = shift(by_z[rest : 2 * rest], "y", 1)
    r2 = shift(by_z[2 * rest : 3 * rest], "y", 2)
    r3 = shift(by_z[3 * rest :], "y", -1)
    grams.append(term + other)
    term = level_term(grams[2], quad_transfer[0])
    other = swap(term, "z", 2)

    up, down, other = tie(up, down, other)
    two = shift(by_y[5 * cut : 6 * cut] + up[:cut], "z", 2)
    six = shift(by_y[6 * cut : 7 * cut] + down[:cut], "z", -2)
    grams.append(term + other)
    nodes = node_lower(jnp.stack(grams))

    messages = pack(
        me, cut, leaves, (by_y, up, down, far, two, six, by_z, r1, r2, r3)
    )
    arrived = [messages[0]] + [shift(messages[s], "rk", s) for s in range(1, n_rank)]
    coupled = final(me, packed, arrived, leaves)

    lower = unpacked(packed[:, :share]).reshape(leaves, RANK, RANK)
    node_weights = lax.dynamic_slice_in_dim(nodes, rank_index * width, width, 1)
    leaf_weights = lax.dynamic_slice_in_dim(lower, rank_index * width, width, 1)
    return (
        jnp.swapaxes(leaf_weights, 1, 2)[None],
        jnp.swapaxes(node_weights, 1, 2)[:, None],
        jnp.swapaxes(coupled, 1, 2)[None],
    )


def solution(mesh):
    devices = mesh.devices
    fine = Mesh(devices.reshape(4, 8, 2, devices.shape[1]), ("y", "z", "core", "rk"))
    clu = ("y", "z", "core")
    placed = (
        P(clu, None, None, "rk"),
        P(clu, None, None, None),
        P(clu, None, None),
        P(clu, None, None),
        P(clu, None, None),
        P(clu, None, None, "rk", None),
        P(clu, None, None, None),
        P(clu, None, None),
        P(clu, None),
    )
    return jax.shard_map(
        shards,
        mesh=fine,
        in_specs=placed,
        out_specs=(
            P(clu, None, None, "rk"),
            P(None, clu, None, "rk"),
            P(clu, None, None, "rk"),
        ),
        check_vma=False,
    )
```

```python
import functools

import jax
import jax.numpy as jnp
from jax import lax
from jax.experimental import pallas as pl
from jax.experimental.pallas import tpu as pltpu
from jax.sharding import Mesh
from jax.sharding import PartitionSpec as P

HIGHEST = lax.Precision.HIGHEST
RANK = 64
TILE = 8
TILES = RANK // TILE


def shift(value, axis, step):
    size = lax.axis_size(axis)
    return lax.ppermute(value, axis, [(i, (i + step) % size) for i in range(size)])


def swap(value, axis, mask):
    return lax.ppermute(value, axis, [(i, i ^ mask) for i in range(lax.axis_size(axis))])


def factor_in_place(s_ref):
    batch = s_ref.shape[2]
    sub = lax.broadcasted_iota(jnp.int32, (TILE, batch), 0)
    for jb in range(TILES):
        count = TILES - jb
        base = jb * TILE
        rows = [
            [s_ref[base + k, pl.ds((jb + t) * TILE, TILE), :] for t in range(count)]
            for k in range(TILE)
        ]
        for k in range(TILE):
            scale = lax.rsqrt(rows[k][0][k : k + 1, :])
            row = [v * scale for v in rows[k]]
            row[0] = jnp.where(sub >= k, row[0], 0.0)
            rows[k] = row
            for t in range(count):
                s_ref[base + k, pl.ds((jb + t) * TILE, TILE), :] = row[t]
            for t in range(jb):
                s_ref[base + k, pl.ds(t * TILE, TILE), :] = jnp.zeros((TILE, batch), jnp.float32)
            for k2 in range(k + 1, TILE):
                s = row[0][k2 : k2 + 1, :]
                rows[k2] = [v - s * u for v, u in zip(rows[k2], row)]
        for rb in range(jb + 1, TILES):
            for r in range(rb * TILE, (rb + 1) * TILE):
                heads = [s_ref[base + k, pl.ds(r, 1), :] for k in range(TILE)]
                for ct in range(rb, TILES):
                    total = s_ref[r, pl.ds(ct * TILE, TILE), :]
                    for k in range(TILE):
                        total = total - heads[k] * rows[k][ct - jb]
                    s_ref[r, pl.ds(ct * TILE, TILE), :] = total


def to_lanes(g_ref, s_ref):
    for a in range(RANK):
        s_ref[a] = g_ref[:, a, :].T


def column_of(s_ref, c):
    return s_ref[:, c, :].T


def packed_rows(matrix):
    half = matrix.shape[0] // 2
    return jnp.concatenate([matrix[:half], matrix[half:]], axis=1)


def unpacked(rows):
    half = rows.shape[-1] // 2
    return jnp.concatenate([rows[..., :half], rows[..., half:]], axis=-2)


def leaf_kernel(x_ref, move_ref, packed_ref, gram_ref, s_ref):
    sources, leaves = x_ref.shape[0], x_ref.shape[1]
    term = None
    for m in range(leaves):
        x = jnp.concatenate([x_ref[s, m] for s in range(sources)], axis=0)
        gram_ref[m] = lax.dot_general(
            x, x, (((1,), (1,)), ((), ())), precision=HIGHEST, preferred_element_type=jnp.float32
        )
    to_lanes(gram_ref, s_ref)
    for m in range(leaves):
        move = move_ref[m]
        moved = jnp.dot(gram_ref[m], move, precision=HIGHEST, preferred_element_type=jnp.float32)
        last = jnp.dot(move.T, moved, precision=HIGHEST, preferred_element_type=jnp.float32)
        term = last if term is None else term + last
    packed_ref[leaves] = packed_rows(term)
    factor_in_place(s_ref)
    half = RANK // 2
    for c in range(half):
        packed_ref[:leaves, c, :] = jnp.concatenate(
            [column_of(s_ref, c), column_of(s_ref, c + half)], axis=1
        )


def leaf_factors(x, moves):
    leaves = x.shape[1]
    vmem = pl.BlockSpec(memory_space=pltpu.VMEM)
    return pl.pallas_call(
        leaf_kernel,
        out_shape=jax.ShapeDtypeStruct((leaves + 1, RANK // 2, 2 * RANK), jnp.float32),
        in_specs=[vmem, vmem],
        out_specs=vmem,
        scratch_shapes=[
            pltpu.VMEM((leaves, RANK, RANK), jnp.float32),
            pltpu.VMEM((RANK, RANK, leaves), jnp.float32),
        ],
        compiler_params=pltpu.CompilerParams(vmem_limit_bytes=32 * 2**20),
        name="leaf_factors",
    )(x, moves)


def node_kernel(g_ref, out_ref, s_ref):
    to_lanes(g_ref, s_ref)
    factor_in_place(s_ref)
    for c in range(RANK):
        out_ref[:, c, :] = column_of(s_ref, c)


def node_lower(grams):
    return pl.pallas_call(
        node_kernel,
        out_shape=jax.ShapeDtypeStruct(grams.shape, jnp.float32),
        in_specs=[pl.BlockSpec(memory_space=pltpu.VMEM)],
        out_specs=pl.BlockSpec(memory_space=pltpu.VMEM),
        scratch_shapes=[pltpu.VMEM((RANK, RANK, grams.shape[0]), jnp.float32)],
        compiler_params=pltpu.CompilerParams(vmem_limit_bytes=32 * 2**20),
        name="node_factors",
    )(grams)


def split(value):
    high = value.astype(jnp.bfloat16)
    return high, (value - high.astype(jnp.float32)).astype(jnp.bfloat16)


def block_products(blocks, packed):
    listed, width, rank = blocks.shape
    top = width // 2
    zero = jnp.zeros((rank, rank), jnp.bfloat16)
    high, low = split(unpacked(packed))
    wide = jnp.concatenate(
        [
            blocks[:, :top, :].reshape(listed * top, rank),
            blocks[:, top:, :].reshape(listed * top, rank),
        ],
        axis=1,
    )
    w_high = jnp.concatenate(
        [jnp.concatenate([high, zero], axis=1), jnp.concatenate([zero, high], axis=1)], axis=0
    )
    w_low = jnp.concatenate(
        [jnp.concatenate([low, zero], axis=1), jnp.concatenate([zero, low], axis=1)], axis=0
    )
    c_high, c_low = split(wide)
    total = jnp.dot(
        jnp.concatenate([c_high, c_low], axis=1),
        jnp.concatenate([w_high, w_high], axis=0),
        preferred_element_type=jnp.float32,
    )
    return total + jnp.dot(c_high, w_low, preferred_element_type=jnp.float32)


def product_kernel(place_ref, c_hbm, l_ref, o0_ref, o1_ref, o2_ref, o3_ref, acc_ref, c_ref, sems):
    leaves, listed, width, _ = c_hbm.shape
    slots, group = c_ref.shape[0], c_ref.shape[1]
    steps = leaves // group
    top = width // 2
    share = l_ref.shape[1] - 1

    def fetch(step, slot):
        return pltpu.make_async_copy(
            c_hbm.at[pl.ds(step * group, group)], c_ref.at[slot], sems.at[slot]
        )

    for step in range(slots - 1):
        fetch(step, step).start()
    acc_ref[...] = jnp.zeros_like(acc_ref)

    def body(step, carry):
        slot = lax.rem(step, slots)
        ahead = step + slots - 1

        @pl.when(ahead < steps)
        def _():
            fetch(ahead, lax.rem(ahead, slots)).start()

        fetch(step, slot).wait()
        source = lax.div(step * group, share)
        first_leaf = step * group - source * share
        totals = [
            block_products(c_ref[slot, u], l_ref[source, first_leaf + u]) for u in range(group)
        ]
        for u in range(group):
            for k in range(listed):
                place = place_ref[(step * group + u) * listed + k]
                acc_ref[place] = acc_ref[place] + totals[u][k * top : (k + 1) * top, :]
        return carry

    lax.fori_loop(0, steps, body, 0)
    at = 0
    for ref in (o0_ref, o1_ref, o2_ref, o3_ref):
        ref[...] = acc_ref[at : at + ref.shape[0]]
        at += ref.shape[0]


def weighted_sums(place, blocks, packed, parts):
    leaves, listed, width, rank = blocks.shape
    top = width // 2
    group, slots = 4, 4
    vmem = pl.BlockSpec(memory_space=pltpu.VMEM)

    def out(rows):
        return jax.ShapeDtypeStruct((rows, top, 2 * rank), jnp.float32)

    return pl.pallas_call(
        product_kernel,
        in_specs=[
            pl.BlockSpec(memory_space=pltpu.SMEM),
            pl.BlockSpec(memory_space=pltpu.HBM),
            vmem,
        ],
        out_specs=(vmem,) * len(parts),
        scratch_shapes=[
            pltpu.VMEM((sum(parts) + TILE, top, 2 * rank), jnp.float32),
            pltpu.VMEM((slots, group, listed, width, rank), jnp.float32),
            pltpu.SemaphoreType.DMA((slots,)),
        ],
        out_shape=tuple(out(rows) for rows in parts),
        compiler_params=pltpu.CompilerParams(vmem_limit_bytes=24 * 2**20),
        name="weighted_sums",
    )(place, blocks, packed)


def pack_kernel(me_ref, y_ref, z_ref, o0_ref, o1_ref, o2_ref, o3_ref, g_ref, m_ref):
    slots = g_ref.shape[0]
    cut = y_ref.shape[1]
    g_ref[:cut] = jnp.sum(y_ref[...], axis=0)
    g_ref[cut:] = jnp.sum(z_ref[...], axis=0)
    chunks = m_ref.shape[0]
    piece = RANK // chunks
    batch = 2 * RANK // piece
    for g in range(slots // batch):
        rows = [g_ref[g * batch + q] for q in range(batch)]
        for c in range(chunks):
            for h in range(2):
                at = h * RANK + c * piece
                m_ref[c, 2 * g + h] = jnp.concatenate([r[:, at : at + piece] for r in rows], axis=1)
    for step, o_ref in enumerate((o0_ref, o1_ref, o2_ref, o3_ref)):
        o_ref[...] = m_ref[lax.rem(me_ref[0] + step, chunks)]


def pack(me, *arrays):
    vmem = pl.BlockSpec(memory_space=pltpu.VMEM)
    slots = sum(array.shape[1] for array in arrays)
    top, lanes = arrays[0].shape[2:]
    tiles = slots * RANK // 4 * top * 2 // (top * lanes)
    message = jax.ShapeDtypeStruct((tiles, top, lanes), jnp.float32)
    return pl.pallas_call(
        pack_kernel,
        in_specs=[pl.BlockSpec(memory_space=pltpu.SMEM)] + [vmem] * len(arrays),
        out_specs=(vmem,) * 4,
        out_shape=(message,) * 4,
        scratch_shapes=[
            pltpu.VMEM((slots, top, lanes), jnp.float32),
            pltpu.VMEM((4, tiles, top, lanes), jnp.float32),
        ],
        compiler_params=pltpu.CompilerParams(vmem_limit_bytes=16 * 2**20),
        name="pack",
    )(me, *arrays)


def final_kernel(me_ref, l_ref, m0_ref, m1_ref, m2_ref, m3_ref, out_ref, m_ref):
    chunks, tiles = m_ref.shape[0], m_ref.shape[1]
    for step, ref in enumerate((m0_ref, m1_ref, m2_ref, m3_ref)):
        m_ref[lax.rem(me_ref[0] + chunks - step, chunks)] = ref[...]
    share = l_ref.shape[1] - 1
    piece = RANK // chunks
    batch = 2 * RANK // piece
    for g in range(tiles // 2):
        rows = [m_ref[c, 2 * g + h] for c in range(chunks) for h in range(2)]
        turned = jnp.concatenate(rows, axis=0).T
        for q in range(batch):
            j = g * batch + q
            out_ref[j] = jnp.dot(
                turned[q * piece : (q + 1) * piece, :],
                unpacked(l_ref[j // share, j % share]),
                precision=HIGHEST,
                preferred_element_type=jnp.float32,
            )


def final(me, packed, messages, slots):
    vmem = pl.BlockSpec(memory_space=pltpu.VMEM)
    return pl.pallas_call(
        final_kernel,
        in_specs=[pl.BlockSpec(memory_space=pltpu.SMEM)] + [vmem] * 5,
        out_specs=vmem,
        out_shape=jax.ShapeDtypeStruct((slots, RANK // 4, RANK), jnp.float32),
        scratch_shapes=[pltpu.VMEM((4,) + messages[0].shape, jnp.float32)],
        compiler_params=pltpu.CompilerParams(vmem_limit_bytes=16 * 2**20),
        name="left_factor",
    )(me, packed, *messages)


def tie(*values):
    return lax.optimization_barrier(values)


def shards(
    bases,
    leaf_transfer,
    node_transfer,
    pair_transfer,
    quad_transfer,
    coupling,
    row_device,
    row_slot,
    block_count,
):
    n_rank = lax.axis_size("rk")
    rank_index = lax.axis_index("rk")
    me = rank_index.astype(jnp.int32).reshape(1)
    n_y, n_z, n_core = (lax.axis_size(axis) for axis in ("y", "z", "core"))
    core = lax.axis_index("core")
    local = jnp.swapaxes(bases[0], 1, 2)
    leaves, width, points = local.shape
    share = leaves // n_rank

    blocks = coupling[0]
    listed = blocks.shape[1]
    cut = 21 * leaves // 32
    rest = leaves - cut
    cells = n_y * n_z
    dest = row_device[0, :, :, 0]
    valid = jnp.arange(listed, dtype=jnp.int32)[None, :] < block_count[0][:, None]
    to_core = dest % n_core
    to_z = (dest // n_core) % n_z
    to_y = dest // (n_core * n_z)
    slot = row_slot[0]
    by_z = (to_z * n_y + to_y) * rest + slot - cut
    by_y = cells * rest + (to_y * n_z + to_z) * cut + slot
    place = jnp.where(slot < cut, by_y, by_z)
    place = place + jnp.where(to_core == core, cells * leaves, 0)
    place = jnp.where(valid, place, n_core * cells * leaves).reshape(-1).astype(jnp.int32)

    pieces = lax.all_to_all(local, "rk", split_axis=0, concat_axis=0, tiled=True)
    moves = lax.dynamic_slice_in_dim(leaf_transfer[0], rank_index * share, share, 0)
    mine = leaf_factors(pieces.reshape(n_rank, share, width, points), moves)
    packed = lax.all_gather(mine, "rk", axis=0, tiled=False)

    away_z, away_y, keep_z, keep_y = weighted_sums(
        place, blocks, packed, (cells * rest, cells * cut) * 2
    )
    away_z = swap(away_z, "core", 1)
    away_y = swap(away_y, "core", 1)

    def exchange(value, axis):
        return lax.all_to_all(value, axis, split_axis=0, concat_axis=0, tiled=True)

    def level_term(level, transfer):
        moved = jnp.dot(level, transfer, precision=HIGHEST)
        return jnp.dot(transfer.T, moved, precision=HIGHEST)

    tail = away_z.shape[1:]
    by_z = (keep_z + away_z).reshape((n_z, n_y, rest) + tail)
    by_y = (keep_y + away_y).reshape((n_y, n_z, cut) + tail)
    by_z, by_y, terms = tie(by_z, by_y, packed[:, share])
    by_z = exchange(by_z, "z")
    by_y = exchange(by_y, "y")
    grams = [unpacked(jnp.sum(terms, axis=0))]
    for (axis, mask), transfer in zip(
        (("core", 1), ("z", 1), ("z", 2)), (node_transfer[0], pair_transfer[0], quad_transfer[0])
    ):
        term = level_term(grams[-1], transfer)
        grams.append(term + swap(term, axis, mask))

    by_z, by_y, grams = tie(by_z, by_y, jnp.stack(grams))
    by_z = exchange(jnp.sum(by_z, axis=0), "y")
    by_y = exchange(jnp.sum(by_y, axis=0), "z")
    nodes = node_lower(grams)
    by_z, by_y = tie(by_z, by_y)

    messages = pack(me, by_y, by_z)
    arrived = [messages[0]] + [shift(messages[s], "rk", s) for s in range(1, n_rank)]
    coupled = final(me, packed, arrived, leaves)

    lower = unpacked(packed[:, :share]).reshape(leaves, RANK, RANK)
    node_weights = lax.dynamic_slice_in_dim(nodes, rank_index * width, width, 1)
    leaf_weights = lax.dynamic_slice_in_dim(lower, rank_index * width, width, 1)
    return (
        jnp.swapaxes(leaf_weights, 1, 2)[None],
        jnp.swapaxes(node_weights, 1, 2)[:, None],
        jnp.swapaxes(coupled, 1, 2)[None],
    )


def solution(mesh):
    devices = mesh.devices
    fine = Mesh(devices.reshape(4, 8, 2, devices.shape[1]), ("y", "z", "core", "rk"))
    clu = ("y", "z", "core")
    placed = (
        P(clu, None, None, "rk"),
        P(clu, None, None, None),
        P(clu, None, None),
        P(clu, None, None),
        P(clu, None, None),
        P(clu, None, None, "rk", None),
        P(clu, None, None, None),
        P(clu, None, None),
        P(clu, None),
    )
    return jax.shard_map(
        shards,
        mesh=fine,
        in_specs=placed,
        out_specs=(
            P(clu, None, None, "rk"),
            P(None, clu, None, "rk"),
            P(clu, None, None, "rk"),
        ),
        check_vma=False,
    )
```

```python
import functools

import jax
import jax.numpy as jnp
from jax import lax
from jax.experimental import pallas as pl
from jax.experimental.pallas import tpu as pltpu
from jax.sharding import Mesh
from jax.sharding import PartitionSpec as P

HIGHEST = lax.Precision.HIGHEST
RANK = 64
TILE = 8
TILES = RANK // TILE


def shift(value, axis, step):
    size = lax.axis_size(axis)
    return lax.ppermute(value, axis, [(i, (i + step) % size) for i in range(size)])


def swap(value, axis, mask):
    return lax.ppermute(value, axis, [(i, i ^ mask) for i in range(lax.axis_size(axis))])


def factor_in_place(s_ref):
    batch = s_ref.shape[2]
    sub = lax.broadcasted_iota(jnp.int32, (TILE, batch), 0)
    for jb in range(TILES):
        count = TILES - jb
        base = jb * TILE
        rows = [
            [s_ref[base + k, pl.ds((jb + t) * TILE, TILE), :] for t in range(count)]
            for k in range(TILE)
        ]
        for k in range(TILE):
            scale = lax.rsqrt(rows[k][0][k : k + 1, :])
            row = [v * scale for v in rows[k]]
            row[0] = jnp.where(sub >= k, row[0], 0.0)
            rows[k] = row
            for t in range(count):
                s_ref[base + k, pl.ds((jb + t) * TILE, TILE), :] = row[t]
            for t in range(jb):
                s_ref[base + k, pl.ds(t * TILE, TILE), :] = jnp.zeros((TILE, batch), jnp.float32)
            for k2 in range(k + 1, TILE):
                s = row[0][k2 : k2 + 1, :]
                rows[k2] = [v - s * u for v, u in zip(rows[k2], row)]
        for rb in range(jb + 1, TILES):
            for r in range(rb * TILE, (rb + 1) * TILE):
                heads = [s_ref[base + k, pl.ds(r, 1), :] for k in range(TILE)]
                for ct in range(rb, TILES):
                    total = s_ref[r, pl.ds(ct * TILE, TILE), :]
                    for k in range(TILE):
                        total = total - heads[k] * rows[k][ct - jb]
                    s_ref[r, pl.ds(ct * TILE, TILE), :] = total


def to_lanes(g_ref, s_ref):
    for a in range(RANK):
        s_ref[a] = g_ref[:, a, :].T


def column_of(s_ref, c):
    return s_ref[:, c, :].T


def packed_rows(matrix):
    half = matrix.shape[0] // 2
    return jnp.concatenate([matrix[:half], matrix[half:]], axis=1)


def unpacked(rows):
    half = rows.shape[-1] // 2
    return jnp.concatenate([rows[..., :half], rows[..., half:]], axis=-2)


def leaf_kernel(x_ref, move_ref, packed_ref, gram_ref, s_ref):
    sources, leaves = x_ref.shape[0], x_ref.shape[1]
    term = None
    for m in range(leaves):
        x = jnp.concatenate([x_ref[s, m] for s in range(sources)], axis=0)
        gram_ref[m] = lax.dot_general(
            x, x, (((1,), (1,)), ((), ())), precision=HIGHEST, preferred_element_type=jnp.float32
        )
    to_lanes(gram_ref, s_ref)
    for m in range(leaves):
        move = move_ref[m]
        moved = jnp.dot(gram_ref[m], move, precision=HIGHEST, preferred_element_type=jnp.float32)
        last = jnp.dot(move.T, moved, precision=HIGHEST, preferred_element_type=jnp.float32)
        term = last if term is None else term + last
    packed_ref[leaves] = packed_rows(term)
    factor_in_place(s_ref)
    half = RANK // 2
    for c in range(half):
        packed_ref[:leaves, c, :] = jnp.concatenate(
            [column_of(s_ref, c), column_of(s_ref, c + half)], axis=1
        )


def leaf_factors(x, moves):
    leaves = x.shape[1]
    vmem = pl.BlockSpec(memory_space=pltpu.VMEM)
    return pl.pallas_call(
        leaf_kernel,
        out_shape=jax.ShapeDtypeStruct((leaves + 1, RANK // 2, 2 * RANK), jnp.float32),
        in_specs=[vmem, vmem],
        out_specs=vmem,
        scratch_shapes=[
            pltpu.VMEM((leaves, RANK, RANK), jnp.float32),
            pltpu.VMEM((RANK, RANK, leaves), jnp.float32),
        ],
        compiler_params=pltpu.CompilerParams(vmem_limit_bytes=32 * 2**20),
        name="leaf_factors",
    )(x, moves)


def node_kernel(g_ref, out_ref, s_ref):
    to_lanes(g_ref, s_ref)
    factor_in_place(s_ref)
    for c in range(RANK):
        out_ref[:, c, :] = column_of(s_ref, c)


def node_lower(grams):
    return pl.pallas_call(
        node_kernel,
        out_shape=jax.ShapeDtypeStruct(grams.shape, jnp.float32),
        in_specs=[pl.BlockSpec(memory_space=pltpu.VMEM)],
        out_specs=pl.BlockSpec(memory_space=pltpu.VMEM),
        scratch_shapes=[pltpu.VMEM((RANK, RANK, grams.shape[0]), jnp.float32)],
        compiler_params=pltpu.CompilerParams(vmem_limit_bytes=32 * 2**20),
        name="node_factors",
    )(grams)


def split(value):
    high = value.astype(jnp.bfloat16)
    return high, (value - high.astype(jnp.float32)).astype(jnp.bfloat16)


def block_products(blocks, packed):
    listed, width, rank = blocks.shape
    top = width // 2
    zero = jnp.zeros((rank, rank), jnp.bfloat16)
    high, low = split(unpacked(packed))
    wide = jnp.concatenate(
        [
            blocks[:, :top, :].reshape(listed * top, rank),
            blocks[:, top:, :].reshape(listed * top, rank),
        ],
        axis=1,
    )
    w_high = jnp.concatenate(
        [jnp.concatenate([high, zero], axis=1), jnp.concatenate([zero, high], axis=1)], axis=0
    )
    w_low = jnp.concatenate(
        [jnp.concatenate([low, zero], axis=1), jnp.concatenate([zero, low], axis=1)], axis=0
    )
    c_high, c_low = split(wide)
    total = jnp.dot(
        jnp.concatenate([c_high, c_low], axis=1),
        jnp.concatenate([w_high, w_high], axis=0),
        preferred_element_type=jnp.float32,
    )
    return total + jnp.dot(c_high, w_low, preferred_element_type=jnp.float32)


def product_kernel(place_ref, c_hbm, l_ref, o0_ref, o1_ref, o2_ref, o3_ref, acc_ref, c_ref, sems):
    leaves, listed, width, _ = c_hbm.shape
    slots, group = c_ref.shape[0], c_ref.shape[1]
    steps = leaves // group
    top = width // 2
    share = l_ref.shape[1] - 1

    def fetch(step, slot):
        return pltpu.make_async_copy(
            c_hbm.at[pl.ds(step * group, group)], c_ref.at[slot], sems.at[slot]
        )

    for step in range(slots - 1):
        fetch(step, step).start()
    acc_ref[...] = jnp.zeros_like(acc_ref)

    def body(step, carry):
        slot = lax.rem(step, slots)
        ahead = step + slots - 1

        @pl.when(ahead < steps)
        def _():
            fetch(ahead, lax.rem(ahead, slots)).start()

        fetch(step, slot).wait()
        source = lax.div(step * group, share)
        first_leaf = step * group - source * share
        totals = [
            block_products(c_ref[slot, u], l_ref[source, first_leaf + u]) for u in range(group)
        ]
        for u in range(group):
            for k in range(listed):
                place = place_ref[(step * group + u) * listed + k]
                acc_ref[place] = acc_ref[place] + totals[u][k * top : (k + 1) * top, :]
        return carry

    lax.fori_loop(0, steps, body, 0)
    at = 0
    for ref in (o0_ref, o1_ref, o2_ref, o3_ref):
        ref[...] = acc_ref[at : at + ref.shape[0]]
        at += ref.shape[0]


def weighted_sums(place, blocks, packed, parts):
    leaves, listed, width, rank = blocks.shape
    top = width // 2
    group, slots = 4, 4
    vmem = pl.BlockSpec(memory_space=pltpu.VMEM)

    def out(rows):
        return jax.ShapeDtypeStruct((rows, top, 2 * rank), jnp.float32)

    return pl.pallas_call(
        product_kernel,
        in_specs=[
            pl.BlockSpec(memory_space=pltpu.SMEM),
            pl.BlockSpec(memory_space=pltpu.HBM),
            vmem,
        ],
        out_specs=(vmem,) * len(parts),
        scratch_shapes=[
            pltpu.VMEM((sum(parts) + TILE, top, 2 * rank), jnp.float32),
            pltpu.VMEM((slots, group, listed, width, rank), jnp.float32),
            pltpu.SemaphoreType.DMA((slots,)),
        ],
        out_shape=tuple(out(rows) for rows in parts),
        compiler_params=pltpu.CompilerParams(vmem_limit_bytes=24 * 2**20),
        name="weighted_sums",
    )(place, pltpu.with_memory_space_constraint(blocks, pltpu.HBM), packed)


class Plan:
    def __init__(self, n_y, n_z, slots):
        self.n_y, self.n_z = n_y, n_z
        self.cut = 3 * slots // 8
        self.rest = slots - self.cut
        self.rows = {"y": n_z * self.cut, "z": n_y * self.rest}
        self.base = {}
        at = 0
        for group in (
            ("y", 2), ("z", 4), ("y", 1), ("y", 3), ("z", 3), ("z", 5), ("y", 0), ("z", 2),
            ("z", 6), ("z", 1), ("z", 7), ("z", 0),
        ):
            if group == ("y", 1):
                self.near = at
            self.base[group] = at
            at += self.rows[group[0]]
        self.total = at

    def places(self, rel_y, rel_z, slot):
        base_y = sum(jnp.where(rel_y == r, self.base["y", r], 0) for r in range(self.n_y))
        base_z = sum(jnp.where(rel_z == r, self.base["z", r], 0) for r in range(self.n_z))
        by_y = base_y + rel_z * self.cut + slot
        by_z = base_z + rel_y * self.rest + slot - self.cut
        return jnp.where(slot < self.cut, by_y, by_z)

    def part(self, ref, group):
        at = self.base[group] - (0 if self.base[group] < self.near else self.near)
        return ref[at : at + self.rows[group[0]]]


def low_add(whole, extra):
    rows = extra.shape[0]
    return jnp.concatenate([whole[:rows] + extra, whole[rows:]], axis=0)


def high_add(whole, extra):
    rows = whole.shape[0] - extra.shape[0]
    return jnp.concatenate([whole[:rows], whole[rows:] + extra], axis=0)


def round1_kernel(plan, keep, swapped, y_up, y_down, z_up, z_down):
    y = plan.part(keep, ("y", 2)) + plan.part(swapped, ("y", 2))
    z = plan.part(keep, ("z", 4)) + plan.part(swapped, ("z", 4))
    half = y.shape[0] // 2
    y_up[...] = y[:half]
    y_down[...] = y[half:]
    half = z.shape[0] // 2
    z_up[...] = z[:half]
    z_down[...] = z[half:]


def round2_kernel(plan, d, ry_up, ry_down, rz_up, rz_down, y_up, y_down, z_up, z_down):
    y_up[...] = low_add(plan.part(d, ("y", 1)), ry_up[...])
    y_down[...] = high_add(plan.part(d, ("y", 3)), ry_down[...])
    z_up[...] = low_add(plan.part(d, ("z", 3)), rz_up[...])
    z_down[...] = high_add(plan.part(d, ("z", 5)), rz_down[...])


def round3_kernel(plan, d, ry_up, ry_down, rz_up, rz_down, ey, z_up, z_down):
    ey[...] = plan.part(d, ("y", 0)) + ry_up[...] + ry_down[...]
    rows, cut = plan.rows["z"], plan.cut
    half = cut // 2
    z_up[:rows] = plan.part(d, ("z", 2)) + rz_up[...]
    z_up[rows:] = ey[4 * cut : 4 * cut + half]
    z_down[:rows] = plan.part(d, ("z", 6)) + rz_down[...]
    z_down[rows:] = ey[4 * cut + half : 5 * cut]


def round4_kernel(plan, d, ey, rz_up, rz_down, z_up, z_down):
    rows, cut = plan.rows["z"], plan.cut
    z_up[:rows] = plan.part(d, ("z", 1)) + rz_up[:rows]
    z_up[rows:] = low_add(ey[3 * cut : 4 * cut], rz_up[rows:])
    z_down[:rows] = plan.part(d, ("z", 7)) + rz_down[:rows]
    z_down[rows:] = high_add(ey[5 * cut : 6 * cut], rz_down[rows:])


def round5_kernel(plan, d, ey, rz_up, rz_down, ez, y_up, y_down, z_up, z_down):
    rows, cut, rest = plan.rows["z"], plan.cut, plan.rest
    half = rest // 2
    ez[...] = plan.part(d, ("z", 0)) + rz_up[:rows] + rz_down[:rows]
    y_up[...] = ez[2 * rest : 2 * rest + half]
    y_down[...] = ez[2 * rest + half : 3 * rest]
    z_up[...] = ey[2 * cut : 3 * cut] + rz_up[rows:]
    z_down[...] = ey[6 * cut : 7 * cut] + rz_down[rows:]


def round6_kernel(plan, ey, ez, ry_up, ry_down, rz_up, rz_down, y_up, y_down, z_up, z_down):
    cut, rest = plan.cut, plan.rest
    y_up[...] = low_add(ez[rest : 2 * rest], ry_up[...])
    y_down[...] = high_add(ez[3 * rest :], ry_down[...])
    z_up[...] = ey[cut : 2 * cut] + rz_up[...]
    z_down[...] = ey[7 * cut :] + rz_down[...]


def run_round(kernel, plan, rows, *arrays):
    vmem = pl.BlockSpec(memory_space=pltpu.VMEM)
    tail = arrays[0].shape[1:]
    return pl.pallas_call(
        functools.partial(kernel, plan),
        in_specs=[vmem] * len(arrays),
        out_specs=(vmem,) * len(rows),
        out_shape=tuple(jax.ShapeDtypeStruct((r,) + tail, jnp.float32) for r in rows),
        compiler_params=pltpu.CompilerParams(vmem_limit_bytes=12 * 2**20),
        name=kernel.__name__,
    )(*arrays)


def pack_kernel(
    me_ref, ey, ez, ry_up, ry_down, rz_up, rz_down, o0_ref, o1_ref, o2_ref, o3_ref, g_ref, m_ref
):
    slots = g_ref.shape[0]
    cut = rz_up.shape[0]
    g_ref[:cut] = ey[:cut] + rz_up[...] + rz_down[...]
    g_ref[cut:] = ez[: slots - cut] + ry_up[...] + ry_down[...]
    chunks = m_ref.shape[0]
    piece = RANK // chunks
    batch = 2 * RANK // piece
    for g in range(slots // batch):
        rows = [g_ref[g * batch + q] for q in range(batch)]
        for c in range(chunks):
            for h in range(2):
                at = h * RANK + c * piece
                m_ref[c, 2 * g + h] = jnp.concatenate([r[:, at : at + piece] for r in rows], axis=1)
    for step, o_ref in enumerate((o0_ref, o1_ref, o2_ref, o3_ref)):
        o_ref[...] = m_ref[lax.rem(me_ref[0] + step, chunks)]


def pack(me, *arrays):
    vmem = pl.BlockSpec(memory_space=pltpu.VMEM)
    slots = arrays[2].shape[0] + arrays[4].shape[0]
    top, lanes = arrays[0].shape[1:]
    tiles = slots * RANK // 4 * top * 2 // (top * lanes)
    message = jax.ShapeDtypeStruct((tiles, top, lanes), jnp.float32)
    return pl.pallas_call(
        pack_kernel,
        in_specs=[pl.BlockSpec(memory_space=pltpu.SMEM)] + [vmem] * len(arrays),
        out_specs=(vmem,) * 4,
        out_shape=(message,) * 4,
        scratch_shapes=[
            pltpu.VMEM((slots, top, lanes), jnp.float32),
            pltpu.VMEM((4, tiles, top, lanes), jnp.float32),
        ],
        compiler_params=pltpu.CompilerParams(vmem_limit_bytes=16 * 2**20),
        name="pack",
    )(me, *arrays)


def final_kernel(me_ref, l_ref, m0_ref, m1_ref, m2_ref, m3_ref, out_ref, m_ref):
    chunks, tiles = m_ref.shape[0], m_ref.shape[1]
    for step, ref in enumerate((m0_ref, m1_ref, m2_ref, m3_ref)):
        m_ref[lax.rem(me_ref[0] + chunks - step, chunks)] = ref[...]
    share = l_ref.shape[1] - 1
    piece = RANK // chunks
    batch = 2 * RANK // piece
    for g in range(tiles // 2):
        rows = [m_ref[c, 2 * g + h] for c in range(chunks) for h in range(2)]
        turned = jnp.concatenate(rows, axis=0).T
        for q in range(batch):
            j = g * batch + q
            out_ref[j] = jnp.dot(
                turned[q * piece : (q + 1) * piece, :],
                unpacked(l_ref[j // share, j % share]),
                precision=HIGHEST,
                preferred_element_type=jnp.float32,
            )


def final(me, packed, messages, slots):
    vmem = pl.BlockSpec(memory_space=pltpu.VMEM)
    return pl.pallas_call(
        final_kernel,
        in_specs=[pl.BlockSpec(memory_space=pltpu.SMEM)] + [vmem] * 5,
        out_specs=vmem,
        out_shape=jax.ShapeDtypeStruct((slots, RANK // 4, RANK), jnp.float32),
        scratch_shapes=[pltpu.VMEM((4,) + messages[0].shape, jnp.float32)],
        compiler_params=pltpu.CompilerParams(vmem_limit_bytes=16 * 2**20),
        name="left_factor",
    )(me, packed, *messages)


def tie(*values):
    return lax.optimization_barrier(values)


def shards(
    bases,
    leaf_transfer,
    node_transfer,
    pair_transfer,
    quad_transfer,
    coupling,
    row_device,
    row_slot,
    block_count,
):
    n_rank = lax.axis_size("rk")
    rank_index = lax.axis_index("rk")
    me = rank_index.astype(jnp.int32).reshape(1)
    n_y, n_z, n_core = (lax.axis_size(axis) for axis in ("y", "z", "core"))
    core = lax.axis_index("core")
    local = jnp.swapaxes(bases[0], 1, 2)
    leaves, width, points = local.shape
    share = leaves // n_rank

    blocks = coupling[0]
    listed = blocks.shape[1]
    plan = Plan(n_y, n_z, leaves)
    dest = row_device[0, :, :, 0]
    valid = jnp.arange(listed, dtype=jnp.int32)[None, :] < block_count[0][:, None]
    rel_z = (dest // n_core - lax.axis_index("z")) % n_z
    rel_y = (dest // (n_core * n_z) - lax.axis_index("y")) % n_y
    place = plan.places(rel_y, rel_z, row_slot[0])
    place = place + jnp.where(dest % n_core == core, plan.total, 0)
    place = jnp.where(valid, place, n_core * plan.total).reshape(-1).astype(jnp.int32)

    pieces = lax.all_to_all(local, "rk", split_axis=0, concat_axis=0, tiled=True)
    moves = lax.dynamic_slice_in_dim(leaf_transfer[0], rank_index * share, share, 0)
    mine = leaf_factors(pieces.reshape(n_rank, share, width, points), moves)
    packed = lax.all_gather(mine, "rk", axis=0, tiled=False)

    near, far = plan.near, plan.total - plan.near
    away_near, away_far, keep_near, keep_far = weighted_sums(
        place, blocks, packed, (near, far, near, far)
    )
    got_near = swap(away_near, "core", 1)
    got_far = swap(away_far, "core", 1)

    def level_term(level, transfer):
        moved = jnp.dot(level, transfer, precision=HIGHEST)
        return jnp.dot(transfer.T, moved, precision=HIGHEST)

    def along(axis, up, down):
        return shift(up, axis, 1), shift(down, axis, -1)

    def send(messages):
        y_up, y_down, z_up, z_down = messages
        return along("z", z_up, z_down) + along("y", y_up, y_down)

    y_rows, z_rows, cut, rest = plan.rows["y"], plan.rows["z"], plan.cut, plan.rest
    sent = run_round(
        round1_kernel, plan, (y_rows // 2,) * 2 + (z_rows // 2,) * 2, keep_near, got_near
    )
    sent, terms = tie(sent, packed[:, share])
    rz_up, rz_down, ry_up, ry_down = send(sent)
    grams = [unpacked(jnp.sum(terms, axis=0))]
    term = level_term(grams[0], node_transfer[0])
    other = swap(term, "core", 1)
    d = keep_far + got_far
    ry_up, ry_down, rz_up, rz_down, d, other = tie(ry_up, ry_down, rz_up, rz_down, d, other)

    sent = run_round(
        round2_kernel, plan, (y_rows,) * 2 + (z_rows,) * 2, d, ry_up, ry_down, rz_up, rz_down
    )
    sent, other = tie(sent, other)
    rz_up, rz_down, ry_up, ry_down = send(sent)
    grams.append(term + other)
    term = level_term(grams[1], pair_transfer[0])
    other = swap(term, "z", 1)
    ry_up, ry_down, rz_up, rz_down, other = tie(ry_up, ry_down, rz_up, rz_down, other)

    both = z_rows + cut // 2
    ey, up, down = run_round(
        round3_kernel, plan, (y_rows, both, both), d, ry_up, ry_down, rz_up, rz_down
    )
    up, down, other, lower = tie(up, down, other, packed[:, :share])
    rz_up, rz_down = along("z", up, down)
    grams.append(term + other)
    term = level_term(grams[2], quad_transfer[0])
    other = swap(term, "z", 2)
    lower = unpacked(lower).reshape(leaves, RANK, RANK)
    leaf_weights = lax.dynamic_slice_in_dim(lower, rank_index * width, width, 1)
    rz_up, rz_down, other, leaf_weights = tie(rz_up, rz_down, other, leaf_weights)

    both = z_rows + cut
    up, down = run_round(round4_kernel, plan, (both, both), d, ey, rz_up, rz_down)
    up, down, other = tie(up, down, other)
    rz_up, rz_down = along("z", up, down)
    grams.append(term + other)
    nodes = node_lower(jnp.stack(grams))
    node_weights = lax.dynamic_slice_in_dim(nodes, rank_index * width, width, 1)
    rz_up, rz_down, node_weights = tie(rz_up, rz_down, node_weights)

    ez, *sent = run_round(
        round5_kernel, plan, (z_rows, rest // 2, rest // 2, cut, cut), d, ey, rz_up, rz_down
    )
    rz_up, rz_down, ry_up, ry_down = send(sent)
    sent = run_round(
        round6_kernel, plan, (rest, rest, cut, cut), ey, ez, ry_up, ry_down, rz_up, rz_down
    )
    rz_up, rz_down, ry_up, ry_down = send(sent)
    messages = pack(me, ey, ez, ry_up, ry_down, rz_up, rz_down)
    arrived = [messages[0]] + [shift(messages[s], "rk", s) for s in range(1, n_rank)]
    coupled = final(me, packed, arrived, leaves)

    return (
        jnp.swapaxes(leaf_weights, 1, 2)[None],
        jnp.swapaxes(node_weights, 1, 2)[:, None],
        jnp.swapaxes(coupled, 1, 2)[None],
    )


def solution(mesh):
    devices = mesh.devices
    fine = Mesh(devices.reshape(4, 8, 2, devices.shape[1]), ("y", "z", "core", "rk"))
    clu = ("y", "z", "core")
    placed = (
        P(clu, None, None, "rk"),
        P(clu, None, None, None),
        P(clu, None, None),
        P(clu, None, None),
        P(clu, None, None),
        P(clu, None, None, "rk", None),
        P(clu, None, None, None),
        P(clu, None, None),
        P(clu, None),
    )
    return jax.shard_map(
        shards,
        mesh=fine,
        in_specs=placed,
        out_specs=(
            P(clu, None, None, "rk"),
            P(None, clu, None, "rk"),
            P(clu, None, None, "rk"),
        ),
        check_vma=False,
    )
```

```python
import functools

import jax
import jax.numpy as jnp
from jax import lax
from jax.experimental import pallas as pl
from jax.experimental.pallas import tpu as pltpu
from jax.sharding import Mesh
from jax.sharding import PartitionSpec as P

HIGHEST = lax.Precision.HIGHEST
RANK = 64
TILE = 8
TILES = RANK // TILE


def shift(value, axis, step):
    size = lax.axis_size(axis)
    return lax.ppermute(value, axis, [(i, (i + step) % size) for i in range(size)])


def swap(value, axis, mask):
    return lax.ppermute(value, axis, [(i, i ^ mask) for i in range(lax.axis_size(axis))])


def factor_in_place(s_ref):
    batch = s_ref.shape[2]
    sub = lax.broadcasted_iota(jnp.int32, (TILE, batch), 0)
    for jb in range(TILES):
        count = TILES - jb
        base = jb * TILE
        rows = [
            [s_ref[base + k, pl.ds((jb + t) * TILE, TILE), :] for t in range(count)]
            for k in range(TILE)
        ]
        for k in range(TILE):
            scale = lax.rsqrt(rows[k][0][k : k + 1, :])
            row = [v * scale for v in rows[k]]
            row[0] = jnp.where(sub >= k, row[0], 0.0)
            rows[k] = row
            for t in range(count):
                s_ref[base + k, pl.ds((jb + t) * TILE, TILE), :] = row[t]
            for t in range(jb):
                s_ref[base + k, pl.ds(t * TILE, TILE), :] = jnp.zeros((TILE, batch), jnp.float32)
            for k2 in range(k + 1, TILE):
                s = row[0][k2 : k2 + 1, :]
                rows[k2] = [v - s * u for v, u in zip(rows[k2], row)]
        for rb in range(jb + 1, TILES):
            for r in range(rb * TILE, (rb + 1) * TILE):
                heads = [s_ref[base + k, pl.ds(r, 1), :] for k in range(TILE)]
                for ct in range(rb, TILES):
                    total = s_ref[r, pl.ds(ct * TILE, TILE), :]
                    for k in range(TILE):
                        total = total - heads[k] * rows[k][ct - jb]
                    s_ref[r, pl.ds(ct * TILE, TILE), :] = total


def to_lanes(g_ref, s_ref):
    for a in range(RANK):
        s_ref[a] = g_ref[:, a, :].T


def column_of(s_ref, c):
    return s_ref[:, c, :].T


def packed_rows(matrix):
    half = matrix.shape[0] // 2
    return jnp.concatenate([matrix[:half], matrix[half:]], axis=1)


def unpacked(rows):
    half = rows.shape[-1] // 2
    return jnp.concatenate([rows[..., :half], rows[..., half:]], axis=-2)


def leaf_kernel(x_ref, move_ref, packed_ref, gram_ref, s_ref):
    sources, leaves = x_ref.shape[0], x_ref.shape[1]
    term = None
    for m in range(leaves):
        x = jnp.concatenate([x_ref[s, m] for s in range(sources)], axis=0)
        gram_ref[m] = lax.dot_general(
            x, x, (((1,), (1,)), ((), ())), precision=HIGHEST, preferred_element_type=jnp.float32
        )
    to_lanes(gram_ref, s_ref)
    for m in range(leaves):
        move = move_ref[m]
        moved = jnp.dot(gram_ref[m], move, precision=HIGHEST, preferred_element_type=jnp.float32)
        last = jnp.dot(move.T, moved, precision=HIGHEST, preferred_element_type=jnp.float32)
        term = last if term is None else term + last
    packed_ref[leaves] = packed_rows(term)
    factor_in_place(s_ref)
    half = RANK // 2
    for c in range(half):
        packed_ref[:leaves, c, :] = jnp.concatenate(
            [column_of(s_ref, c), column_of(s_ref, c + half)], axis=1
        )


def leaf_factors(x, moves):
    leaves = x.shape[1]
    vmem = pl.BlockSpec(memory_space=pltpu.VMEM)
    return pl.pallas_call(
        leaf_kernel,
        out_shape=jax.ShapeDtypeStruct((leaves + 1, RANK // 2, 2 * RANK), jnp.float32),
        in_specs=[vmem, vmem],
        out_specs=vmem,
        scratch_shapes=[
            pltpu.VMEM((leaves, RANK, RANK), jnp.float32),
            pltpu.VMEM((RANK, RANK, leaves), jnp.float32),
        ],
        compiler_params=pltpu.CompilerParams(vmem_limit_bytes=10 * 2**20),
        name="leaf_factors",
    )(x, moves)


def node_kernel(me_ref, g_ref, out_ref, s_ref, l_ref):
    to_lanes(g_ref, s_ref)
    factor_in_place(s_ref)
    for c in range(RANK):
        l_ref[:, c, :] = column_of(s_ref, c)
    width = out_ref.shape[1]
    out_ref[...] = l_ref[:, pl.ds(pl.multiple_of(me_ref[0] * width, width), width), :]


def node_lower(me, grams, width):
    vmem = pl.BlockSpec(memory_space=pltpu.VMEM)
    return pl.pallas_call(
        node_kernel,
        out_shape=jax.ShapeDtypeStruct((grams.shape[0], width, RANK), jnp.float32),
        in_specs=[pl.BlockSpec(memory_space=pltpu.SMEM), vmem],
        out_specs=vmem,
        scratch_shapes=[
            pltpu.VMEM((RANK, RANK, grams.shape[0]), jnp.float32),
            pltpu.VMEM(grams.shape, jnp.float32),
        ],
        compiler_params=pltpu.CompilerParams(vmem_limit_bytes=10 * 2**20),
        name="node_factors",
    )(me, grams)


def split(value):
    high = value.astype(jnp.bfloat16)
    return high, (value - high.astype(jnp.float32)).astype(jnp.bfloat16)


def block_products(blocks, packed):
    listed, width, rank = blocks.shape
    top = width // 2
    zero = jnp.zeros((rank, rank), jnp.bfloat16)
    high, low = split(unpacked(packed))
    wide = jnp.concatenate(
        [
            blocks[:, :top, :].reshape(listed * top, rank),
            blocks[:, top:, :].reshape(listed * top, rank),
        ],
        axis=1,
    )
    w_high = jnp.concatenate(
        [jnp.concatenate([high, zero], axis=1), jnp.concatenate([zero, high], axis=1)], axis=0
    )
    w_low = jnp.concatenate(
        [jnp.concatenate([low, zero], axis=1), jnp.concatenate([zero, low], axis=1)], axis=0
    )
    c_high, c_low = split(wide)
    total = jnp.dot(
        jnp.concatenate([c_high, c_low], axis=1),
        jnp.concatenate([w_high, w_high], axis=0),
        preferred_element_type=jnp.float32,
    )
    return total + jnp.dot(c_high, w_low, preferred_element_type=jnp.float32)


def product_kernel(
    me_ref, place_ref, c_hbm, l_ref, o0_ref, o1_ref, o2_ref, o3_ref, rows_ref,
    acc_ref, c_ref, sems, out_sems,
):
    leaves, listed, width, _ = c_hbm.shape
    slots, group = c_ref.shape[0], c_ref.shape[1]
    steps = leaves // group
    top = width // 2
    share = l_ref.shape[1] - 1

    def fetch(step, slot):
        return pltpu.make_async_copy(
            c_hbm.at[pl.ds(step * group, group)], c_ref.at[slot], sems.at[slot]
        )

    for step in range(slots - 1):
        fetch(step, step).start()
    acc_ref[...] = jnp.zeros_like(acc_ref)

    me = me_ref[0]
    at = pl.multiple_of(lax.rem(me, 2) * width, width)
    for j in range(leaves):
        rows = l_ref[j // share, j % share, pl.ds(at, width), :]
        rows_ref[j] = jnp.where(me < 2, rows[:, :RANK], rows[:, RANK:])

    def body(step, carry):
        slot = lax.rem(step, slots)
        ahead = step + slots - 1

        @pl.when(ahead < steps)
        def _():
            fetch(ahead, lax.rem(ahead, slots)).start()

        fetch(step, slot).wait()
        source = lax.div(step * group, share)
        first_leaf = step * group - source * share
        totals = [
            block_products(c_ref[slot, u], l_ref[source, first_leaf + u]) for u in range(group)
        ]
        for u in range(group):
            for k in range(listed):
                place = place_ref[(step * group + u) * listed + k]
                acc_ref[place] = acc_ref[place] + totals[u][k * top : (k + 1) * top, :]
        return carry

    lax.fori_loop(0, steps, body, 0)
    near, far = o0_ref.shape[0], o1_ref.shape[0]
    total = near + far
    copies = [
        pltpu.make_async_copy(acc_ref.at[pl.ds(at, far)], ref, sem)
        for at, ref, sem in ((near, o1_ref, out_sems.at[0]), (total + near, o3_ref, out_sems.at[1]))
    ]
    for copy in copies:
        copy.start()
    o0_ref[...] = acc_ref[:near]
    o2_ref[...] = acc_ref[total : total + near]
    for copy in copies:
        copy.wait()


def weighted_sums(me, place, blocks, packed, parts):
    leaves, listed, width, rank = blocks.shape
    top = width // 2
    group, slots = 4, 4
    vmem = pl.BlockSpec(memory_space=pltpu.VMEM)
    hbm = pl.BlockSpec(memory_space=pltpu.HBM)

    def out(rows):
        return jax.ShapeDtypeStruct((rows, top, 2 * rank), jnp.float32)

    return pl.pallas_call(
        product_kernel,
        in_specs=[
            pl.BlockSpec(memory_space=pltpu.SMEM),
            pl.BlockSpec(memory_space=pltpu.SMEM),
            hbm,
            vmem,
        ],
        out_specs=(vmem, hbm, vmem, hbm, vmem),
        scratch_shapes=[
            pltpu.VMEM((sum(parts) + TILE, top, 2 * rank), jnp.float32),
            pltpu.VMEM((slots, group, listed, width, rank), jnp.float32),
            pltpu.SemaphoreType.DMA((slots,)),
            pltpu.SemaphoreType.DMA((2,)),
        ],
        out_shape=tuple(out(rows) for rows in parts)
        + (jax.ShapeDtypeStruct((leaves, width, rank), jnp.float32),),
        compiler_params=pltpu.CompilerParams(vmem_limit_bytes=16 * 2**20),
        name="weighted_sums",
    )(me, place, pltpu.with_memory_space_constraint(blocks, pltpu.HBM), packed)


class Plan:
    def __init__(self, n_y, n_z, slots):
        self.n_y, self.n_z = n_y, n_z
        self.cut = 3 * slots // 8
        self.rest = slots - self.cut
        self.rows = {"y": n_z * self.cut, "z": n_y * self.rest}
        self.base = {}
        at = 0
        for group in (
            ("y", 2), ("z", 4), ("y", 1), ("y", 3), ("z", 3), ("z", 5), ("y", 0), ("z", 2),
            ("z", 6), ("z", 1), ("z", 7), ("z", 0),
        ):
            if group == ("y", 1):
                self.near = at
            self.base[group] = at
            at += self.rows[group[0]]
        self.total = at

    def places(self, rel_y, rel_z, slot):
        base_y = sum(jnp.where(rel_y == r, self.base["y", r], 0) for r in range(self.n_y))
        base_z = sum(jnp.where(rel_z == r, self.base["z", r], 0) for r in range(self.n_z))
        by_y = base_y + rel_z * self.cut + slot
        by_z = base_z + rel_y * self.rest + slot - self.cut
        return jnp.where(slot < self.cut, by_y, by_z)

    def part(self, ref, group):
        at = self.base[group] - (0 if self.base[group] < self.near else self.near)
        return ref[at : at + self.rows[group[0]]]

    def both(self, keep, got, group):
        return self.part(keep, group) + self.part(got, group)


def low_add(whole, extra):
    rows = extra.shape[0]
    return jnp.concatenate([whole[:rows] + extra, whole[rows:]], axis=0)


def high_add(whole, extra):
    rows = whole.shape[0] - extra.shape[0]
    return jnp.concatenate([whole[:rows], whole[rows:] + extra], axis=0)


def round1_kernel(plan, keep, got, y_up, y_down, z_up, z_down):
    y = plan.both(keep, got, ("y", 2))
    z = plan.both(keep, got, ("z", 4))
    half = y.shape[0] // 2
    y_up[...] = y[:half]
    y_down[...] = y[half:]
    half = z.shape[0] // 2
    z_up[...] = z[:half]
    z_down[...] = z[half:]


def round2_kernel(plan, keep, got, ry_up, ry_down, rz_up, rz_down, y_up, y_down, z_up, z_down):
    y_up[...] = low_add(plan.both(keep, got, ("y", 1)), ry_up[...])
    y_down[...] = high_add(plan.both(keep, got, ("y", 3)), ry_down[...])
    z_up[...] = low_add(plan.both(keep, got, ("z", 3)), rz_up[...])
    z_down[...] = high_add(plan.both(keep, got, ("z", 5)), rz_down[...])


def round3_kernel(plan, keep, got, ry_up, ry_down, rz_up, rz_down, ey, z_up, z_down):
    ey[...] = plan.both(keep, got, ("y", 0)) + ry_up[...] + ry_down[...]
    rows, cut = plan.rows["z"], plan.cut
    half = cut // 2
    z_up[:rows] = plan.both(keep, got, ("z", 2)) + rz_up[...]
    z_up[rows : rows + half] = ey[4 * cut : 4 * cut + half]
    z_up[rows + half :] = ey[cut : 2 * cut]
    z_down[:rows] = plan.both(keep, got, ("z", 6)) + rz_down[...]
    z_down[rows : rows + half] = ey[4 * cut + half : 5 * cut]
    z_down[rows + half :] = ey[7 * cut :]


def round4_kernel(plan, keep, got, ey, rz_up, rz_down, z_up, z_down):
    rows, cut = plan.rows["z"], plan.cut
    half = cut // 2
    z_up[:rows] = plan.both(keep, got, ("z", 1)) + rz_up[:rows]
    z_up[rows:] = low_add(ey[3 * cut : 4 * cut], rz_up[rows : rows + half])
    z_down[:rows] = plan.both(keep, got, ("z", 7)) + rz_down[:rows]
    z_down[rows:] = high_add(ey[5 * cut : 6 * cut], rz_down[rows : rows + half])


def round5_kernel(plan, keep, got, ey, rz_up, rz_down, own, y_one, y_two, y_three, z_two, z_six):
    rows, cut, rest = plan.rows["z"], plan.cut, plan.rest
    ez = plan.both(keep, got, ("z", 0)) + rz_up[:rows] + rz_down[:rows]
    for r, ref in enumerate((own, y_one, y_two, y_three)):
        ref[...] = ez[r * rest : (r + 1) * rest]
    z_two[...] = ey[2 * cut : 3 * cut] + rz_up[rows:]
    z_six[...] = ey[6 * cut : 7 * cut] + rz_down[rows:]


def run_round(kernel, plan, rows, *arrays):
    vmem = pl.BlockSpec(memory_space=pltpu.VMEM)
    tail = arrays[0].shape[1:]
    return pl.pallas_call(
        functools.partial(kernel, plan),
        in_specs=[vmem] * len(arrays),
        out_specs=(vmem,) * len(rows),
        out_shape=tuple(jax.ShapeDtypeStruct((r,) + tail, jnp.float32) for r in rows),
        compiler_params=pltpu.CompilerParams(vmem_limit_bytes=12 * 2**20),
        name=kernel.__name__,
    )(*arrays)


def pack_kernel(
    me_ref, ey, z_up, z_down, z_two, z_six, ez, y_one, y_two, y_three,
    o0_ref, o1_ref, o2_ref, o3_ref, g_ref, m_ref,
):
    slots = g_ref.shape[0]
    cut = z_two.shape[0]
    skip = z_up.shape[0] - cut
    g_ref[:cut] = ey[:cut] + z_up[skip:] + z_down[skip:] + z_two[...] + z_six[...]
    g_ref[cut:] = ez[...] + y_one[...] + y_two[...] + y_three[...]
    chunks = m_ref.shape[0]
    piece = RANK // chunks
    batch = 2 * RANK // piece
    for g in range(slots // batch):
        rows = [g_ref[g * batch + q] for q in range(batch)]
        for c in range(chunks):
            for h in range(2):
                at = h * RANK + c * piece
                m_ref[c, 2 * g + h] = jnp.concatenate([r[:, at : at + piece] for r in rows], axis=1)
    for step, o_ref in enumerate((o0_ref, o1_ref, o2_ref, o3_ref)):
        o_ref[...] = m_ref[lax.rem(me_ref[0] + step, chunks)]


def pack(me, *arrays):
    vmem = pl.BlockSpec(memory_space=pltpu.VMEM)
    slots = arrays[4].shape[0] + arrays[5].shape[0]
    top, lanes = arrays[0].shape[1:]
    tiles = slots * RANK // 4 * top * 2 // (top * lanes)
    message = jax.ShapeDtypeStruct((tiles, top, lanes), jnp.float32)
    return pl.pallas_call(
        pack_kernel,
        in_specs=[pl.BlockSpec(memory_space=pltpu.SMEM)] + [vmem] * len(arrays),
        out_specs=(vmem,) * 4,
        out_shape=(message,) * 4,
        scratch_shapes=[
            pltpu.VMEM((slots, top, lanes), jnp.float32),
            pltpu.VMEM((4, tiles, top, lanes), jnp.float32),
        ],
        compiler_params=pltpu.CompilerParams(vmem_limit_bytes=8 * 2**20),
        name="pack",
    )(me, *arrays)


def final_kernel(me_ref, l_ref, m0_ref, m1_ref, m2_ref, m3_ref, out_ref, m_ref):
    chunks, tiles = m_ref.shape[0], m_ref.shape[1]
    for step, ref in enumerate((m0_ref, m1_ref, m2_ref, m3_ref)):
        m_ref[lax.rem(me_ref[0] + chunks - step, chunks)] = ref[...]
    share = l_ref.shape[1] - 1
    piece = RANK // chunks
    batch = 2 * RANK // piece
    for g in range(tiles // 2):
        rows = [m_ref[c, 2 * g + h] for c in range(chunks) for h in range(2)]
        turned = jnp.concatenate(rows, axis=0).T
        for q in range(batch):
            j = g * batch + q
            out_ref[j] = jnp.dot(
                turned[q * piece : (q + 1) * piece, :],
                unpacked(l_ref[j // share, j % share]),
                precision=HIGHEST,
                preferred_element_type=jnp.float32,
            )


def final(me, packed, messages, slots):
    vmem = pl.BlockSpec(memory_space=pltpu.VMEM)
    return pl.pallas_call(
        final_kernel,
        in_specs=[pl.BlockSpec(memory_space=pltpu.SMEM)] + [vmem] * 5,
        out_specs=vmem,
        out_shape=jax.ShapeDtypeStruct((slots, RANK // 4, RANK), jnp.float32),
        scratch_shapes=[pltpu.VMEM((4,) + messages[0].shape, jnp.float32)],
        compiler_params=pltpu.CompilerParams(vmem_limit_bytes=8 * 2**20),
        name="left_factor",
    )(me, packed, *messages)


def tie(*values):
    return lax.optimization_barrier(values)


def shards(
    bases,
    leaf_transfer,
    node_transfer,
    pair_transfer,
    quad_transfer,
    coupling,
    row_device,
    row_slot,
    block_count,
):
    n_rank = lax.axis_size("rk")
    rank_index = lax.axis_index("rk")
    me = rank_index.astype(jnp.int32).reshape(1)
    n_y, n_z, n_core = (lax.axis_size(axis) for axis in ("y", "z", "core"))
    core = lax.axis_index("core")
    local = jnp.swapaxes(bases[0], 1, 2)
    leaves, width, points = local.shape
    share = leaves // n_rank

    blocks = coupling[0]
    listed = blocks.shape[1]
    plan = Plan(n_y, n_z, leaves)
    dest = row_device[0, :, :, 0]
    valid = jnp.arange(listed, dtype=jnp.int32)[None, :] < block_count[0][:, None]
    rel_z = (dest // n_core - lax.axis_index("z")) % n_z
    rel_y = (dest // (n_core * n_z) - lax.axis_index("y")) % n_y
    place = plan.places(rel_y, rel_z, row_slot[0])
    place = place + jnp.where(dest % n_core == core, plan.total, 0)
    place = jnp.where(valid, place, n_core * plan.total).reshape(-1).astype(jnp.int32)

    pieces = lax.all_to_all(local, "rk", split_axis=0, concat_axis=0, tiled=True)
    moves = lax.dynamic_slice_in_dim(leaf_transfer[0], rank_index * share, share, 0)
    mine = leaf_factors(pieces.reshape(n_rank, share, width, points), moves)
    packed = lax.all_gather(mine, "rk", axis=0, tiled=False)

    near, far = plan.near, plan.total - plan.near
    away_near, away_far, keep_near, keep_far, leaf_weights = weighted_sums(
        me, place, blocks, packed, (near, far, near, far)
    )
    got_near = swap(away_near, "core", 1)
    got_near, away_far = tie(got_near, away_far)
    got_far = swap(away_far, "core", 1)

    def level_term(level, transfer):
        moved = jnp.dot(level, transfer, precision=HIGHEST)
        return jnp.dot(transfer.T, moved, precision=HIGHEST)

    def along(axis, up, down):
        return shift(up, axis, 1), shift(down, axis, -1)

    def send(messages):
        y_up, y_down, z_up, z_down = messages
        return along("z", z_up, z_down) + along("y", y_up, y_down)

    y_rows, z_rows, cut, rest = plan.rows["y"], plan.rows["z"], plan.cut, plan.rest
    sent = run_round(
        round1_kernel, plan, (y_rows // 2,) * 2 + (z_rows // 2,) * 2, keep_near, got_near
    )
    sent, terms = tie(sent, packed[:, share])
    rz_up, rz_down, ry_up, ry_down = send(sent)
    grams = [unpacked(jnp.sum(terms, axis=0))]
    term = level_term(grams[0], node_transfer[0])
    other = swap(term, "core", 1)
    ry_up, ry_down, rz_up, rz_down, got_far, term = tie(
        ry_up, ry_down, rz_up, rz_down, got_far, term
    )
    sums = (keep_far, got_far)

    sent = run_round(
        round2_kernel, plan, (y_rows,) * 2 + (z_rows,) * 2, *sums, ry_up, ry_down, rz_up, rz_down
    )
    sent, term = tie(sent, term)
    rz_up, rz_down, ry_up, ry_down = send(sent)
    grams.append(term + other)
    term = level_term(grams[1], pair_transfer[0])
    other = swap(term, "z", 1)
    ry_up, ry_down, rz_up, rz_down, term = tie(ry_up, ry_down, rz_up, rz_down, term)

    ride = z_rows + cut // 2 + cut
    ey, up, down = run_round(
        round3_kernel, plan, (y_rows, ride, ride), *sums, ry_up, ry_down, rz_up, rz_down
    )
    up, down, term = tie(up, down, term)
    ride_up, ride_down = along("z", up, down)
    grams.append(term + other)
    term = level_term(grams[2], quad_transfer[0])
    other = swap(term, "z", 2)
    ride_up, ride_down, term = tie(ride_up, ride_down, term)

    both = z_rows + cut
    up, down = run_round(round4_kernel, plan, (both, both), *sums, ey, ride_up, ride_down)
    up, down, term = tie(up, down, term)
    rz_up, rz_down = along("z", up, down)
    grams.append(term + other)
    node_weights = node_lower(me, jnp.stack(grams), width)
    rz_up, rz_down, node_weights = tie(rz_up, rz_down, node_weights)

    ez, y_one, y_two, y_three, z_two, z_six = run_round(
        round5_kernel, plan, (rest,) * 4 + (cut,) * 2, *sums, ey, rz_up, rz_down
    )
    z_two = shift(z_two, "z", 2)
    z_six = shift(z_six, "z", -2)
    y_one, y_three = along("y", y_one, y_three)
    y_two = shift(y_two, "y", 2)
    messages = pack(me, ey, ride_up, ride_down, z_two, z_six, ez, y_one, y_two, y_three)
    arrived = [messages[0]] + [shift(messages[s], "rk", s) for s in range(1, n_rank)]
    coupled = final(me, packed, arrived, leaves)

    return (
        jnp.swapaxes(leaf_weights, 1, 2)[None],
        jnp.swapaxes(node_weights, 1, 2)[:, None],
        jnp.swapaxes(coupled, 1, 2)[None],
    )


def solution(mesh):
    devices = mesh.devices
    fine = Mesh(devices.reshape(4, 8, 2, devices.shape[1]), ("y", "z", "core", "rk"))
    clu = ("y", "z", "core")
    placed = (
        P(clu, None, None, "rk"),
        P(clu, None, None, None),
        P(clu, None, None),
        P(clu, None, None),
        P(clu, None, None),
        P(clu, None, None, "rk", None),
        P(clu, None, None, None),
        P(clu, None, None),
        P(clu, None),
    )
    return jax.shard_map(
        shards,
        mesh=fine,
        in_specs=placed,
        out_specs=(
            P(clu, None, None, "rk"),
            P(None, clu, None, "rk"),
            P(clu, None, None, "rk"),
        ),
        check_vma=False,
    )
```

```python
import functools

import jax
import jax.numpy as jnp
from jax import lax
from jax.experimental import pallas as pl
from jax.experimental.pallas import tpu as pltpu
from jax.sharding import Mesh
from jax.sharding import PartitionSpec as P

HIGHEST = lax.Precision.HIGHEST
RANK = 64
TILE = 8
TILES = RANK // TILE


def shift(value, axis, step):
    size = lax.axis_size(axis)
    return lax.ppermute(value, axis, [(i, (i + step) % size) for i in range(size)])


def swap(value, axis, mask):
    return lax.ppermute(value, axis, [(i, i ^ mask) for i in range(lax.axis_size(axis))])


def factor_in_place(s_ref):
    batch = s_ref.shape[2]
    sub = lax.broadcasted_iota(jnp.int32, (TILE, batch), 0)
    for jb in range(TILES):
        count = TILES - jb
        base = jb * TILE
        rows = [
            [s_ref[base + k, pl.ds((jb + t) * TILE, TILE), :] for t in range(count)]
            for k in range(TILE)
        ]
        for k in range(TILE):
            scale = lax.rsqrt(rows[k][0][k : k + 1, :])
            row = [v * scale for v in rows[k]]
            row[0] = jnp.where(sub >= k, row[0], 0.0)
            rows[k] = row
            for t in range(count):
                s_ref[base + k, pl.ds((jb + t) * TILE, TILE), :] = row[t]
            for t in range(jb):
                s_ref[base + k, pl.ds(t * TILE, TILE), :] = jnp.zeros((TILE, batch), jnp.float32)
            for k2 in range(k + 1, TILE):
                s = row[0][k2 : k2 + 1, :]
                rows[k2] = [v - s * u for v, u in zip(rows[k2], row)]
        for rb in range(jb + 1, TILES):
            for r in range(rb * TILE, (rb + 1) * TILE):
                heads = [s_ref[base + k, pl.ds(r, 1), :] for k in range(TILE)]
                for ct in range(rb, TILES):
                    total = s_ref[r, pl.ds(ct * TILE, TILE), :]
                    for k in range(TILE):
                        total = total - heads[k] * rows[k][ct - jb]
                    s_ref[r, pl.ds(ct * TILE, TILE), :] = total


def to_lanes(g_ref, s_ref):
    for a in range(RANK):
        s_ref[a] = g_ref[:, a, :].T


def column_of(s_ref, c):
    return s_ref[:, c, :].T


def packed_rows(matrix):
    half = matrix.shape[0] // 2
    return jnp.concatenate([matrix[:half], matrix[half:]], axis=1)


def unpacked(rows):
    half = rows.shape[-1] // 2
    return jnp.concatenate([rows[..., :half], rows[..., half:]], axis=-2)


def leaf_kernel(x_ref, move_ref, packed_ref, gram_ref, s_ref):
    sources, leaves = x_ref.shape[0], x_ref.shape[1]
    term = None
    for m in range(leaves):
        x = jnp.concatenate([x_ref[s, m] for s in range(sources)], axis=0)
        gram_ref[m] = lax.dot_general(
            x, x, (((1,), (1,)), ((), ())), precision=HIGHEST, preferred_element_type=jnp.float32
        )
    to_lanes(gram_ref, s_ref)
    for m in range(leaves):
        move = move_ref[m]
        moved = jnp.dot(gram_ref[m], move, precision=HIGHEST, preferred_element_type=jnp.float32)
        last = jnp.dot(move.T, moved, precision=HIGHEST, preferred_element_type=jnp.float32)
        term = last if term is None else term + last
    packed_ref[leaves] = packed_rows(term)
    factor_in_place(s_ref)
    half = RANK // 2
    for c in range(half):
        packed_ref[:leaves, c, :] = jnp.concatenate(
            [column_of(s_ref, c), column_of(s_ref, c + half)], axis=1
        )


def leaf_factors(x, moves):
    leaves = x.shape[1]
    vmem = pl.BlockSpec(memory_space=pltpu.VMEM)
    return pl.pallas_call(
        leaf_kernel,
        out_shape=jax.ShapeDtypeStruct((leaves + 1, RANK // 2, 2 * RANK), jnp.float32),
        in_specs=[vmem, vmem],
        out_specs=vmem,
        scratch_shapes=[
            pltpu.VMEM((leaves, RANK, RANK), jnp.float32),
            pltpu.VMEM((RANK, RANK, leaves), jnp.float32),
        ],
        compiler_params=pltpu.CompilerParams(vmem_limit_bytes=10 * 2**20),
        name="leaf_factors",
    )(x, moves)


def level_term(level, transfer):
    moved = jnp.dot(level, transfer, precision=HIGHEST, preferred_element_type=jnp.float32)
    return jnp.dot(transfer.T, moved, precision=HIGHEST, preferred_element_type=jnp.float32)


def first_level_kernel(packed_ref, move_ref, gram_ref, term_ref):
    leaves = packed_ref.shape[1] - 1
    gram = unpacked(jnp.sum(packed_ref[:, leaves], axis=0))
    gram_ref[...] = gram
    term_ref[...] = level_term(gram, move_ref[...])


def next_level_kernel(mine_ref, other_ref, move_ref, gram_ref, term_ref):
    gram = mine_ref[...] + other_ref[...]
    gram_ref[...] = gram
    term_ref[...] = level_term(gram, move_ref[...])


def level(kernel, *arrays):
    vmem = pl.BlockSpec(memory_space=pltpu.VMEM)
    return pl.pallas_call(
        kernel,
        in_specs=[vmem] * len(arrays),
        out_specs=(vmem, vmem),
        out_shape=(jax.ShapeDtypeStruct((RANK, RANK), jnp.float32),) * 2,
        compiler_params=pltpu.CompilerParams(vmem_limit_bytes=4 * 2**20),
        name=kernel.__name__,
    )(*arrays)


def node_kernel(me_ref, g1_ref, g2_ref, g3_ref, mine_ref, other_ref, out_ref, s_ref, l_ref):
    g_ref = l_ref
    for t, ref in enumerate((g1_ref, g2_ref, g3_ref)):
        g_ref[t] = ref[...]
    g_ref[3] = mine_ref[...] + other_ref[...]
    to_lanes(g_ref, s_ref)
    factor_in_place(s_ref)
    for c in range(RANK):
        l_ref[:, c, :] = column_of(s_ref, c)
    width = out_ref.shape[1]
    out_ref[...] = l_ref[:, pl.ds(pl.multiple_of(me_ref[0] * width, width), width), :]


def node_lower(me, grams, width):
    vmem = pl.BlockSpec(memory_space=pltpu.VMEM)
    count = len(grams) - 1
    return pl.pallas_call(
        node_kernel,
        out_shape=jax.ShapeDtypeStruct((count, width, RANK), jnp.float32),
        in_specs=[pl.BlockSpec(memory_space=pltpu.SMEM)] + [vmem] * len(grams),
        out_specs=vmem,
        scratch_shapes=[
            pltpu.VMEM((RANK, RANK, count), jnp.float32),
            pltpu.VMEM((count, RANK, RANK), jnp.float32),
        ],
        compiler_params=pltpu.CompilerParams(vmem_limit_bytes=10 * 2**20),
        name="node_factors",
    )(me, *grams)


def split(value):
    high = value.astype(jnp.bfloat16)
    return high, (value - high.astype(jnp.float32)).astype(jnp.bfloat16)


def block_products(blocks, packed):
    listed, width, rank = blocks.shape
    top = width // 2
    zero = jnp.zeros((rank, rank), jnp.bfloat16)
    high, low = split(unpacked(packed))
    wide = jnp.concatenate(
        [
            blocks[:, :top, :].reshape(listed * top, rank),
            blocks[:, top:, :].reshape(listed * top, rank),
        ],
        axis=1,
    )
    w_high = jnp.concatenate(
        [jnp.concatenate([high, zero], axis=1), jnp.concatenate([zero, high], axis=1)], axis=0
    )
    w_low = jnp.concatenate(
        [jnp.concatenate([low, zero], axis=1), jnp.concatenate([zero, low], axis=1)], axis=0
    )
    c_high, c_low = split(wide)
    total = jnp.dot(
        jnp.concatenate([c_high, c_low], axis=1),
        jnp.concatenate([w_high, w_high], axis=0),
        preferred_element_type=jnp.float32,
    )
    return total + jnp.dot(c_high, w_low, preferred_element_type=jnp.float32)


def product_kernel(
    me_ref, place_ref, c_hbm, l_ref, o0_ref, o1_ref, o2_ref, o3_ref, rows_ref,
    acc_ref, c_ref, sems,
):
    leaves, listed, width, _ = c_hbm.shape
    slots, group = c_ref.shape[0], c_ref.shape[1]
    steps = leaves // group
    top = width // 2
    share = l_ref.shape[1] - 1

    def fetch(step, slot):
        return pltpu.make_async_copy(
            c_hbm.at[pl.ds(step * group, group)], c_ref.at[slot], sems.at[slot]
        )

    for step in range(slots - 1):
        fetch(step, step).start()
    acc_ref[...] = jnp.zeros_like(acc_ref)

    me = me_ref[0]
    at = pl.multiple_of(lax.rem(me, 2) * width, width)
    for j in range(leaves):
        rows = l_ref[j // share, j % share, pl.ds(at, width), :]
        rows_ref[j] = jnp.where(me < 2, rows[:, :RANK], rows[:, RANK:])

    def body(step, carry):
        slot = lax.rem(step, slots)
        ahead = step + slots - 1

        @pl.when(ahead < steps)
        def _():
            fetch(ahead, lax.rem(ahead, slots)).start()

        fetch(step, slot).wait()
        source = lax.div(step * group, share)
        first_leaf = step * group - source * share
        totals = [
            block_products(c_ref[slot, u], l_ref[source, first_leaf + u]) for u in range(group)
        ]
        for u in range(group):
            for k in range(listed):
                place = place_ref[(step * group + u) * listed + k]
                acc_ref[place] = acc_ref[place] + totals[u][k * top : (k + 1) * top, :]
        return carry

    lax.fori_loop(0, steps, body, 0)
    at = 0
    for ref in (o0_ref, o1_ref, o2_ref, o3_ref):
        ref[...] = acc_ref[at : at + ref.shape[0]]
        at += ref.shape[0]


def weighted_sums(me, place, blocks, packed, parts):
    leaves, listed, width, rank = blocks.shape
    top = width // 2
    group, slots = 4, 4
    vmem = pl.BlockSpec(memory_space=pltpu.VMEM)
    hbm = pl.BlockSpec(memory_space=pltpu.HBM)

    def out(rows):
        return jax.ShapeDtypeStruct((rows, top, 2 * rank), jnp.float32)

    return pl.pallas_call(
        product_kernel,
        in_specs=[
            pl.BlockSpec(memory_space=pltpu.SMEM),
            pl.BlockSpec(memory_space=pltpu.SMEM),
            hbm,
            vmem,
        ],
        out_specs=(vmem,) * (len(parts) + 1),
        scratch_shapes=[
            pltpu.VMEM((sum(parts) + TILE, top, 2 * rank), jnp.float32),
            pltpu.VMEM((slots, group, listed, width, rank), jnp.float32),
            pltpu.SemaphoreType.DMA((slots,)),
        ],
        out_shape=tuple(out(rows) for rows in parts)
        + (jax.ShapeDtypeStruct((leaves, width, rank), jnp.float32),),
        compiler_params=pltpu.CompilerParams(vmem_limit_bytes=16 * 2**20),
        name="weighted_sums",
    )(me, place, pltpu.with_memory_space_constraint(blocks, pltpu.HBM), packed)


class Plan:
    def __init__(self, n_y, n_z, slots):
        self.n_y, self.n_z = n_y, n_z
        self.cut = 3 * slots // 8
        self.rest = slots - self.cut
        self.rows = {"y": n_z * self.cut, "z": n_y * self.rest}
        self.base = {}
        at = 0
        for group in (
            ("y", 2), ("z", 4), ("y", 1), ("y", 3), ("z", 3), ("z", 5), ("y", 0), ("z", 2),
            ("z", 6), ("z", 1), ("z", 7), ("z", 0),
        ):
            if group == ("y", 1):
                self.near = at
            self.base[group] = at
            at += self.rows[group[0]]
        self.total = at

    def places(self, rel_y, rel_z, slot):
        base_y = sum(jnp.where(rel_y == r, self.base["y", r], 0) for r in range(self.n_y))
        base_z = sum(jnp.where(rel_z == r, self.base["z", r], 0) for r in range(self.n_z))
        by_y = base_y + rel_z * self.cut + slot
        by_z = base_z + rel_y * self.rest + slot - self.cut
        return jnp.where(slot < self.cut, by_y, by_z)

    def part(self, ref, group):
        at = self.base[group] - (0 if self.base[group] < self.near else self.near)
        return ref[at : at + self.rows[group[0]]]

    def both(self, keep, got, group):
        return self.part(keep, group) + self.part(got, group)


def low_add(whole, extra):
    rows = extra.shape[0]
    return jnp.concatenate([whole[:rows] + extra, whole[rows:]], axis=0)


def high_add(whole, extra):
    rows = whole.shape[0] - extra.shape[0]
    return jnp.concatenate([whole[:rows], whole[rows:] + extra], axis=0)


def round1_kernel(plan, keep, got, y_up, y_down, z_up, z_down):
    y = plan.both(keep, got, ("y", 2))
    z = plan.both(keep, got, ("z", 4))
    half = y.shape[0] // 2
    y_up[...] = y[:half]
    y_down[...] = y[half:]
    half = z.shape[0] // 2
    z_up[...] = z[:half]
    z_down[...] = z[half:]


def round2_kernel(plan, keep, got, ry_up, ry_down, rz_up, rz_down, y_up, y_down, z_up, z_down):
    y_up[...] = low_add(plan.both(keep, got, ("y", 1)), ry_up[...])
    y_down[...] = high_add(plan.both(keep, got, ("y", 3)), ry_down[...])
    z_up[...] = low_add(plan.both(keep, got, ("z", 3)), rz_up[...])
    z_down[...] = high_add(plan.both(keep, got, ("z", 5)), rz_down[...])


def round3_kernel(plan, keep, got, ry_up, ry_down, rz_up, rz_down, ey, z_up, z_down):
    ey[...] = plan.both(keep, got, ("y", 0)) + ry_up[...] + ry_down[...]
    rows, cut = plan.rows["z"], plan.cut
    half = cut // 2
    z_up[:rows] = plan.both(keep, got, ("z", 2)) + rz_up[...]
    z_up[rows : rows + half] = ey[4 * cut : 4 * cut + half]
    z_up[rows + half :] = ey[cut : 2 * cut]
    z_down[:rows] = plan.both(keep, got, ("z", 6)) + rz_down[...]
    z_down[rows : rows + half] = ey[4 * cut + half : 5 * cut]
    z_down[rows + half :] = ey[7 * cut :]


def round4_kernel(plan, keep, got, ey, rz_up, rz_down, z_up, z_down):
    rows, cut = plan.rows["z"], plan.cut
    half = cut // 2
    z_up[:rows] = plan.both(keep, got, ("z", 1)) + rz_up[:rows]
    z_up[rows:] = low_add(ey[3 * cut : 4 * cut], rz_up[rows : rows + half])
    z_down[:rows] = plan.both(keep, got, ("z", 7)) + rz_down[:rows]
    z_down[rows:] = high_add(ey[5 * cut : 6 * cut], rz_down[rows : rows + half])


def round5_kernel(plan, keep, got, ey, rz_up, rz_down, own, y_one, y_two, y_three, z_two, z_six):
    rows, cut, rest = plan.rows["z"], plan.cut, plan.rest
    ez = plan.both(keep, got, ("z", 0)) + rz_up[:rows] + rz_down[:rows]
    for r, ref in enumerate((own, y_one, y_two, y_three)):
        ref[...] = ez[r * rest : (r + 1) * rest]
    z_two[...] = ey[2 * cut : 3 * cut] + rz_up[rows:]
    z_six[...] = ey[6 * cut : 7 * cut] + rz_down[rows:]


def run_round(kernel, plan, rows, *arrays):
    vmem = pl.BlockSpec(memory_space=pltpu.VMEM)
    tail = arrays[0].shape[1:]
    return pl.pallas_call(
        functools.partial(kernel, plan),
        in_specs=[vmem] * len(arrays),
        out_specs=(vmem,) * len(rows),
        out_shape=tuple(jax.ShapeDtypeStruct((r,) + tail, jnp.float32) for r in rows),
        compiler_params=pltpu.CompilerParams(vmem_limit_bytes=12 * 2**20),
        name=kernel.__name__,
    )(*arrays)


def pack_kernel(
    me_ref, ey, z_up, z_down, z_two, z_six, ez, y_one, y_two, y_three,
    o0_ref, o1_ref, o2_ref, o3_ref, g_ref, m_ref,
):
    slots = g_ref.shape[0]
    cut = z_two.shape[0]
    skip = z_up.shape[0] - cut
    g_ref[:cut] = ey[:cut] + z_up[skip:] + z_down[skip:] + z_two[...] + z_six[...]
    g_ref[cut:] = ez[...] + y_one[...] + y_two[...] + y_three[...]
    chunks = m_ref.shape[0]
    piece = RANK // chunks
    batch = 2 * RANK // piece
    for g in range(slots // batch):
        rows = [g_ref[g * batch + q] for q in range(batch)]
        for c in range(chunks):
            for h in range(2):
                at = h * RANK + c * piece
                m_ref[c, 2 * g + h] = jnp.concatenate([r[:, at : at + piece] for r in rows], axis=1)
    for step, o_ref in enumerate((o0_ref, o1_ref, o2_ref, o3_ref)):
        o_ref[...] = m_ref[lax.rem(me_ref[0] + step, chunks)]


def pack(me, *arrays):
    vmem = pl.BlockSpec(memory_space=pltpu.VMEM)
    slots = arrays[4].shape[0] + arrays[5].shape[0]
    top, lanes = arrays[0].shape[1:]
    tiles = slots * RANK // 4 * top * 2 // (top * lanes)
    message = jax.ShapeDtypeStruct((tiles, top, lanes), jnp.float32)
    return pl.pallas_call(
        pack_kernel,
        in_specs=[pl.BlockSpec(memory_space=pltpu.SMEM)] + [vmem] * len(arrays),
        out_specs=(vmem,) * 4,
        out_shape=(message,) * 4,
        scratch_shapes=[
            pltpu.VMEM((slots, top, lanes), jnp.float32),
            pltpu.VMEM((4, tiles, top, lanes), jnp.float32),
        ],
        compiler_params=pltpu.CompilerParams(vmem_limit_bytes=8 * 2**20),
        name="pack",
    )(me, *arrays)


def final_kernel(me_ref, l_ref, m0_ref, m1_ref, m2_ref, m3_ref, out_ref, m_ref):
    chunks, tiles = m_ref.shape[0], m_ref.shape[1]
    for step, ref in enumerate((m0_ref, m1_ref, m2_ref, m3_ref)):
        m_ref[lax.rem(me_ref[0] + chunks - step, chunks)] = ref[...]
    share = l_ref.shape[1] - 1
    piece = RANK // chunks
    batch = 2 * RANK // piece
    for g in range(tiles // 2):
        rows = [m_ref[c, 2 * g + h] for c in range(chunks) for h in range(2)]
        turned = jnp.concatenate(rows, axis=0).T
        for q in range(batch):
            j = g * batch + q
            out_ref[j] = jnp.dot(
                turned[q * piece : (q + 1) * piece, :],
                unpacked(l_ref[j // share, j % share]),
                precision=HIGHEST,
                preferred_element_type=jnp.float32,
            )


def final(me, packed, messages, slots):
    vmem = pl.BlockSpec(memory_space=pltpu.VMEM)
    return pl.pallas_call(
        final_kernel,
        in_specs=[pl.BlockSpec(memory_space=pltpu.SMEM)] + [vmem] * 5,
        out_specs=vmem,
        out_shape=jax.ShapeDtypeStruct((slots, RANK // 4, RANK), jnp.float32),
        scratch_shapes=[pltpu.VMEM((4,) + messages[0].shape, jnp.float32)],
        compiler_params=pltpu.CompilerParams(vmem_limit_bytes=8 * 2**20),
        name="left_factor",
    )(me, packed, *messages)


def tie(*values):
    return lax.optimization_barrier(values)


def shards(
    bases,
    leaf_transfer,
    node_transfer,
    pair_transfer,
    quad_transfer,
    coupling,
    row_device,
    row_slot,
    block_count,
):
    n_rank = lax.axis_size("rk")
    rank_index = lax.axis_index("rk")
    me = rank_index.astype(jnp.int32).reshape(1)
    n_y, n_z, n_core = (lax.axis_size(axis) for axis in ("y", "z", "core"))
    core = lax.axis_index("core")
    local = jnp.swapaxes(bases[0], 1, 2)
    leaves, width, points = local.shape
    share = leaves // n_rank

    blocks = coupling[0]
    listed = blocks.shape[1]
    plan = Plan(n_y, n_z, leaves)
    dest = row_device[0, :, :, 0]
    valid = jnp.arange(listed, dtype=jnp.int32)[None, :] < block_count[0][:, None]
    rel_z = (dest // n_core - lax.axis_index("z")) % n_z
    rel_y = (dest // (n_core * n_z) - lax.axis_index("y")) % n_y
    place = plan.places(rel_y, rel_z, row_slot[0])
    place = place + jnp.where(dest % n_core == core, plan.total, 0)
    place = jnp.where(valid, place, n_core * plan.total).reshape(-1).astype(jnp.int32)

    pieces = lax.all_to_all(local, "rk", split_axis=0, concat_axis=0, tiled=True)
    moves = lax.dynamic_slice_in_dim(leaf_transfer[0], rank_index * share, share, 0)
    mine = leaf_factors(pieces.reshape(n_rank, share, width, points), moves)
    packed = lax.all_gather(mine, "rk", axis=0, tiled=False)

    near, far = plan.near, plan.total - plan.near
    away_near, away_far, keep_near, keep_far, leaf_weights = weighted_sums(
        me, place, blocks, packed, (near, far, near, far)
    )
    got_near = swap(away_near, "core", 1)
    got_near, away_far = tie(got_near, away_far)
    got_far = swap(away_far, "core", 1)

    def along(axis, up, down):
        return shift(up, axis, 1), shift(down, axis, -1)

    def send(messages):
        y_up, y_down, z_up, z_down = messages
        return along("z", z_up, z_down) + along("y", y_up, y_down)

    y_rows, z_rows, cut, rest = plan.rows["y"], plan.rows["z"], plan.cut, plan.rest
    sent = run_round(
        round1_kernel, plan, (y_rows // 2,) * 2 + (z_rows // 2,) * 2, keep_near, got_near
    )
    sent, shared = tie(sent, packed)
    rz_up, rz_down, ry_up, ry_down = send(sent)
    gram1, term = level(first_level_kernel, shared, node_transfer[0])
    other = swap(term, "core", 1)
    ry_up, ry_down, rz_up, rz_down, got_far, term = tie(
        ry_up, ry_down, rz_up, rz_down, got_far, term
    )
    sums = (keep_far, got_far)

    sent = run_round(
        round2_kernel, plan, (y_rows,) * 2 + (z_rows,) * 2, *sums, ry_up, ry_down, rz_up, rz_down
    )
    sent, term = tie(sent, term)
    rz_up, rz_down, ry_up, ry_down = send(sent)
    gram2, term = level(next_level_kernel, term, other, pair_transfer[0])
    other = swap(term, "z", 1)
    ry_up, ry_down, rz_up, rz_down, term = tie(ry_up, ry_down, rz_up, rz_down, term)

    ride = z_rows + cut // 2 + cut
    ey, up, down = run_round(
        round3_kernel, plan, (y_rows, ride, ride), *sums, ry_up, ry_down, rz_up, rz_down
    )
    up, down, term = tie(up, down, term)
    ride_up, ride_down = along("z", up, down)
    gram3, term = level(next_level_kernel, term, other, quad_transfer[0])
    other = swap(term, "z", 2)
    ride_up, ride_down, term = tie(ride_up, ride_down, term)

    both = z_rows + cut
    up, down = run_round(round4_kernel, plan, (both, both), *sums, ey, ride_up, ride_down)
    up, down, term = tie(up, down, term)
    rz_up, rz_down = along("z", up, down)
    node_weights = node_lower(me, (gram1, gram2, gram3, term, other), width)
    rz_up, rz_down, node_weights = tie(rz_up, rz_down, node_weights)

    ez, y_one, y_two, y_three, z_two, z_six = run_round(
        round5_kernel, plan, (rest,) * 4 + (cut,) * 2, *sums, ey, rz_up, rz_down
    )
    z_two = shift(z_two, "z", 2)
    z_six = shift(z_six, "z", -2)
    y_one, y_three = along("y", y_one, y_three)
    y_two = shift(y_two, "y", 2)
    messages = pack(me, ey, ride_up, ride_down, z_two, z_six, ez, y_one, y_two, y_three)
    arrived = [messages[0]] + [shift(messages[s], "rk", s) for s in range(1, n_rank)]
    coupled = final(me, packed, arrived, leaves)

    return (
        jnp.swapaxes(leaf_weights, 1, 2)[None],
        jnp.swapaxes(node_weights, 1, 2)[:, None],
        jnp.swapaxes(coupled, 1, 2)[None],
    )


def solution(mesh):
    devices = mesh.devices
    fine = Mesh(devices.reshape(4, 8, 2, devices.shape[1]), ("y", "z", "core", "rk"))
    clu = ("y", "z", "core")
    placed = (
        P(clu, None, None, "rk"),
        P(clu, None, None, None),
        P(clu, None, None),
        P(clu, None, None),
        P(clu, None, None),
        P(clu, None, None, "rk", None),
        P(clu, None, None, None),
        P(clu, None, None),
        P(clu, None),
    )
    return jax.shard_map(
        shards,
        mesh=fine,
        in_specs=placed,
        out_specs=(
            P(clu, None, None, "rk"),
            P(None, clu, None, "rk"),
            P(clu, None, None, "rk"),
        ),
        check_vma=False,
    )
```

```python
import functools

import jax
import jax.numpy as jnp
from jax import lax
from jax.experimental import pallas as pl
from jax.experimental.pallas import tpu as pltpu
from jax.sharding import Mesh
from jax.sharding import PartitionSpec as P

HIGHEST = lax.Precision.HIGHEST
RANK = 64
TILE = 8
TILES = RANK // TILE


def shift(value, axis, step):
    size = lax.axis_size(axis)
    return lax.ppermute(value, axis, [(i, (i + step) % size) for i in range(size)])


def swap(value, axis, mask):
    return lax.ppermute(value, axis, [(i, i ^ mask) for i in range(lax.axis_size(axis))])


def factor_in_place(s_ref):
    batch = s_ref.shape[2]
    sub = lax.broadcasted_iota(jnp.int32, (TILE, batch), 0)
    for jb in range(TILES):
        count = TILES - jb
        base = jb * TILE
        rows = [
            [s_ref[base + k, pl.ds((jb + t) * TILE, TILE), :] for t in range(count)]
            for k in range(TILE)
        ]
        for k in range(TILE):
            scale = lax.rsqrt(rows[k][0][k : k + 1, :])
            row = [v * scale for v in rows[k]]
            row[0] = jnp.where(sub >= k, row[0], 0.0)
            rows[k] = row
            for t in range(count):
                s_ref[base + k, pl.ds((jb + t) * TILE, TILE), :] = row[t]
            for t in range(jb):
                s_ref[base + k, pl.ds(t * TILE, TILE), :] = jnp.zeros((TILE, batch), jnp.float32)
            for k2 in range(k + 1, TILE):
                s = row[0][k2 : k2 + 1, :]
                rows[k2] = [v - s * u for v, u in zip(rows[k2], row)]
        for rb in range(jb + 1, TILES):
            for r in range(rb * TILE, (rb + 1) * TILE):
                heads = [s_ref[base + k, pl.ds(r, 1), :] for k in range(TILE)]
                for ct in range(rb, TILES):
                    total = s_ref[r, pl.ds(ct * TILE, TILE), :]
                    for k in range(TILE):
                        total = total - heads[k] * rows[k][ct - jb]
                    s_ref[r, pl.ds(ct * TILE, TILE), :] = total


def to_lanes(g_ref, s_ref):
    for a in range(RANK):
        s_ref[a] = g_ref[:, a, :].T


def column_of(s_ref, c):
    return s_ref[:, c, :].T


def packed_rows(matrix):
    half = matrix.shape[0] // 2
    return jnp.concatenate([matrix[:half], matrix[half:]], axis=1)


def unpacked(rows):
    half = rows.shape[-1] // 2
    return jnp.concatenate([rows[..., :half], rows[..., half:]], axis=-2)


def leaf_kernel(x_ref, move_ref, packed_ref, gram_ref, s_ref):
    sources, leaves = x_ref.shape[0], x_ref.shape[1]
    term = None
    for m in range(leaves):
        x = jnp.concatenate([x_ref[s, m] for s in range(sources)], axis=0)
        gram_ref[m] = lax.dot_general(
            x, x, (((1,), (1,)), ((), ())), precision=HIGHEST, preferred_element_type=jnp.float32
        )
    to_lanes(gram_ref, s_ref)
    for m in range(leaves):
        move = move_ref[m]
        moved = jnp.dot(gram_ref[m], move, precision=HIGHEST, preferred_element_type=jnp.float32)
        last = jnp.dot(move.T, moved, precision=HIGHEST, preferred_element_type=jnp.float32)
        term = last if term is None else term + last
    packed_ref[leaves] = packed_rows(term)
    factor_in_place(s_ref)
    half = RANK // 2
    for c in range(half):
        packed_ref[:leaves, c, :] = jnp.concatenate(
            [column_of(s_ref, c), column_of(s_ref, c + half)], axis=1
        )


def leaf_factors(x, moves):
    leaves = x.shape[1]
    vmem = pl.BlockSpec(memory_space=pltpu.VMEM)
    return pl.pallas_call(
        leaf_kernel,
        out_shape=jax.ShapeDtypeStruct((leaves + 1, RANK // 2, 2 * RANK), jnp.float32),
        in_specs=[vmem, vmem],
        out_specs=vmem,
        scratch_shapes=[
            pltpu.VMEM((leaves, RANK, RANK), jnp.float32),
            pltpu.VMEM((RANK, RANK, leaves), jnp.float32),
        ],
        compiler_params=pltpu.CompilerParams(vmem_limit_bytes=10 * 2**20),
        name="leaf_factors",
    )(x, moves)


def level_term(level, transfer):
    moved = jnp.dot(level, transfer, precision=HIGHEST, preferred_element_type=jnp.float32)
    return jnp.dot(transfer.T, moved, precision=HIGHEST, preferred_element_type=jnp.float32)


def first_level_kernel(packed_ref, move_ref, gram_ref, term_ref):
    leaves = packed_ref.shape[1] - 1
    gram = unpacked(jnp.sum(packed_ref[:, leaves], axis=0))
    gram_ref[...] = gram
    term_ref[...] = level_term(gram, move_ref[...])


def next_level_kernel(mine_ref, other_ref, move_ref, gram_ref, term_ref):
    gram = mine_ref[...] + other_ref[...]
    gram_ref[...] = gram
    term_ref[...] = level_term(gram, move_ref[...])


def level(kernel, *arrays):
    vmem = pl.BlockSpec(memory_space=pltpu.VMEM)
    return pl.pallas_call(
        kernel,
        in_specs=[vmem] * len(arrays),
        out_specs=(vmem, vmem),
        out_shape=(jax.ShapeDtypeStruct((RANK, RANK), jnp.float32),) * 2,
        compiler_params=pltpu.CompilerParams(vmem_limit_bytes=4 * 2**20),
        name=kernel.__name__,
    )(*arrays)


def node_kernel(me_ref, g1_ref, g2_ref, g3_ref, mine_ref, other_ref, out_ref, s_ref, l_ref):
    g_ref = l_ref
    for t, ref in enumerate((g1_ref, g2_ref, g3_ref)):
        g_ref[t] = ref[...]
    g_ref[3] = mine_ref[...] + other_ref[...]
    to_lanes(g_ref, s_ref)
    factor_in_place(s_ref)
    for c in range(RANK):
        l_ref[:, c, :] = column_of(s_ref, c)
    width = out_ref.shape[1]
    out_ref[...] = l_ref[:, pl.ds(pl.multiple_of(me_ref[0] * width, width), width), :]


def node_lower(me, grams, width):
    vmem = pl.BlockSpec(memory_space=pltpu.VMEM)
    count = len(grams) - 1
    return pl.pallas_call(
        node_kernel,
        out_shape=jax.ShapeDtypeStruct((count, width, RANK), jnp.float32),
        in_specs=[pl.BlockSpec(memory_space=pltpu.SMEM)] + [vmem] * len(grams),
        out_specs=vmem,
        scratch_shapes=[
            pltpu.VMEM((RANK, RANK, count), jnp.float32),
            pltpu.VMEM((count, RANK, RANK), jnp.float32),
        ],
        compiler_params=pltpu.CompilerParams(vmem_limit_bytes=10 * 2**20),
        name="node_factors",
    )(me, *grams)


def split(value):
    high = value.astype(jnp.bfloat16)
    return high, (value - high.astype(jnp.float32)).astype(jnp.bfloat16)


def block_products(blocks, packed):
    listed, width, rank = blocks.shape
    top = width // 2
    zero = jnp.zeros((rank, rank), jnp.bfloat16)
    high, low = split(unpacked(packed))
    wide = jnp.concatenate(
        [
            blocks[:, :top, :].reshape(listed * top, rank),
            blocks[:, top:, :].reshape(listed * top, rank),
        ],
        axis=1,
    )
    w_high = jnp.concatenate(
        [jnp.concatenate([high, zero], axis=1), jnp.concatenate([zero, high], axis=1)], axis=0
    )
    w_low = jnp.concatenate(
        [jnp.concatenate([low, zero], axis=1), jnp.concatenate([zero, low], axis=1)], axis=0
    )
    c_high, c_low = split(wide)
    total = jnp.dot(
        jnp.concatenate([c_high, c_low], axis=1),
        jnp.concatenate([w_high, w_high], axis=0),
        preferred_element_type=jnp.float32,
    )
    return total + jnp.dot(c_high, w_low, preferred_element_type=jnp.float32)


def product_kernel(
    me_ref, place_ref, c_hbm, l_ref, o0_ref, o1_ref, o2_ref, o3_ref, rows_ref,
    acc_ref, c_ref, sems,
):
    leaves, listed, width, _ = c_hbm.shape
    slots, group = c_ref.shape[0], c_ref.shape[1]
    steps = leaves // group
    top = width // 2
    share = l_ref.shape[1] - 1

    def fetch(step, slot):
        return pltpu.make_async_copy(
            c_hbm.at[pl.ds(step * group, group)], c_ref.at[slot], sems.at[slot]
        )

    for step in range(slots - 1):
        fetch(step, step).start()
    acc_ref[...] = jnp.zeros_like(acc_ref)

    me = me_ref[0]
    at = pl.multiple_of(lax.rem(me, 2) * width, width)
    for j in range(leaves):
        rows = l_ref[j // share, j % share, pl.ds(at, width), :]
        rows_ref[j] = jnp.where(me < 2, rows[:, :RANK], rows[:, RANK:])

    def body(step, carry):
        slot = lax.rem(step, slots)
        ahead = step + slots - 1

        @pl.when(ahead < steps)
        def _():
            fetch(ahead, lax.rem(ahead, slots)).start()

        fetch(step, slot).wait()
        source = lax.div(step * group, share)
        first_leaf = step * group - source * share
        totals = [
            block_products(c_ref[slot, u], l_ref[source, first_leaf + u]) for u in range(group)
        ]
        for u in range(group):
            for k in range(listed):
                place = place_ref[(step * group + u) * listed + k]
                acc_ref[place] = acc_ref[place] + totals[u][k * top : (k + 1) * top, :]
        return carry

    lax.fori_loop(0, steps, body, 0)
    at = 0
    for ref in (o0_ref, o1_ref, o2_ref, o3_ref):
        ref[...] = acc_ref[at : at + ref.shape[0]]
        at += ref.shape[0]


def weighted_sums(me, place, blocks, packed, parts):
    leaves, listed, width, rank = blocks.shape
    top = width // 2
    group, slots = 4, 4
    vmem = pl.BlockSpec(memory_space=pltpu.VMEM)
    hbm = pl.BlockSpec(memory_space=pltpu.HBM)

    def out(rows):
        return jax.ShapeDtypeStruct((rows, top, 2 * rank), jnp.float32)

    return pl.pallas_call(
        product_kernel,
        in_specs=[
            pl.BlockSpec(memory_space=pltpu.SMEM),
            pl.BlockSpec(memory_space=pltpu.SMEM),
            hbm,
            vmem,
        ],
        out_specs=(vmem,) * (len(parts) + 1),
        scratch_shapes=[
            pltpu.VMEM((sum(parts) + TILE, top, 2 * rank), jnp.float32),
            pltpu.VMEM((slots, group, listed, width, rank), jnp.float32),
            pltpu.SemaphoreType.DMA((slots,)),
        ],
        out_shape=tuple(out(rows) for rows in parts)
        + (jax.ShapeDtypeStruct((leaves, width, rank), jnp.float32),),
        compiler_params=pltpu.CompilerParams(vmem_limit_bytes=16 * 2**20),
        name="weighted_sums",
    )(me, place, pltpu.with_memory_space_constraint(blocks, pltpu.HBM), packed)


class Plan:
    def __init__(self, n_y, n_z, slots):
        self.n_y, self.n_z = n_y, n_z
        self.cut = 3 * slots // 8
        self.rest = slots - self.cut
        self.rows = {"y": n_z * self.cut, "z": n_y * self.rest}
        self.base = {}
        at = 0
        for group in (
            ("y", 2), ("z", 4), ("y", 1), ("y", 3), ("z", 3), ("z", 5), ("y", 0), ("z", 2),
            ("z", 6), ("z", 1), ("z", 7), ("z", 0),
        ):
            if group == ("y", 1):
                self.near = at
            self.base[group] = at
            at += self.rows[group[0]]
        self.total = at

    def places(self, rel_y, rel_z, slot):
        base_y = sum(jnp.where(rel_y == r, self.base["y", r], 0) for r in range(self.n_y))
        base_z = sum(jnp.where(rel_z == r, self.base["z", r], 0) for r in range(self.n_z))
        by_y = base_y + rel_z * self.cut + slot
        by_z = base_z + rel_y * self.rest + slot - self.cut
        return jnp.where(slot < self.cut, by_y, by_z)

    def part(self, ref, group):
        at = self.base[group] - (0 if self.base[group] < self.near else self.near)
        return ref[at : at + self.rows[group[0]]]

    def both(self, keep, got, group):
        return self.part(keep, group) + self.part(got, group)


def low_add(whole, extra):
    rows = extra.shape[0]
    return jnp.concatenate([whole[:rows] + extra, whole[rows:]], axis=0)


def high_add(whole, extra):
    rows = whole.shape[0] - extra.shape[0]
    return jnp.concatenate([whole[:rows], whole[rows:] + extra], axis=0)


def round1_kernel(plan, keep, got, y_two, z_up, z_down):
    y_two[...] = plan.both(keep, got, ("y", 2))
    z = plan.both(keep, got, ("z", 4))
    half = z.shape[0] // 2
    z_up[...] = z[:half]
    z_down[...] = z[half:]


def round2_kernel(plan, keep, got, rz_up, rz_down, y_up, y_down, z_up, z_down):
    y_up[...] = plan.both(keep, got, ("y", 1))
    y_down[...] = plan.both(keep, got, ("y", 3))
    z_up[...] = low_add(plan.both(keep, got, ("z", 3)), rz_up[...])
    z_down[...] = high_add(plan.both(keep, got, ("z", 5)), rz_down[...])


def round3_kernel(plan, keep, got, ry_two, ry_up, ry_down, rz_up, rz_down, ey, z_up, z_down):
    ey[...] = plan.both(keep, got, ("y", 0)) + ry_two[...] + ry_up[...] + ry_down[...]
    rows, cut = plan.rows["z"], plan.cut
    half = cut // 2
    z_up[:rows] = plan.both(keep, got, ("z", 2)) + rz_up[...]
    z_up[rows : rows + half] = ey[4 * cut : 4 * cut + half]
    z_up[rows + half :] = ey[cut : 2 * cut]
    z_down[:rows] = plan.both(keep, got, ("z", 6)) + rz_down[...]
    z_down[rows : rows + half] = ey[4 * cut + half : 5 * cut]
    z_down[rows + half :] = ey[7 * cut :]


def round4_kernel(plan, keep, got, ey, rz_up, rz_down, z_up, z_down):
    rows, cut = plan.rows["z"], plan.cut
    half = cut // 2
    z_up[:rows] = plan.both(keep, got, ("z", 1)) + rz_up[:rows]
    z_up[rows:] = low_add(ey[3 * cut : 4 * cut], rz_up[rows : rows + half])
    z_down[:rows] = plan.both(keep, got, ("z", 7)) + rz_down[:rows]
    z_down[rows:] = high_add(ey[5 * cut : 6 * cut], rz_down[rows : rows + half])


def round5_kernel(plan, keep, got, ey, rz_up, rz_down, own, y_one, y_two, y_three, z_two, z_six):
    rows, cut, rest = plan.rows["z"], plan.cut, plan.rest
    ez = plan.both(keep, got, ("z", 0)) + rz_up[:rows] + rz_down[:rows]
    for r, ref in enumerate((own, y_one, y_two, y_three)):
        ref[...] = ez[r * rest : (r + 1) * rest]
    z_two[...] = ey[2 * cut : 3 * cut] + rz_up[rows:]
    z_six[...] = ey[6 * cut : 7 * cut] + rz_down[rows:]


def run_round(kernel, plan, rows, *arrays):
    vmem = pl.BlockSpec(memory_space=pltpu.VMEM)
    tail = arrays[0].shape[1:]
    return pl.pallas_call(
        functools.partial(kernel, plan),
        in_specs=[vmem] * len(arrays),
        out_specs=(vmem,) * len(rows),
        out_shape=tuple(jax.ShapeDtypeStruct((r,) + tail, jnp.float32) for r in rows),
        compiler_params=pltpu.CompilerParams(vmem_limit_bytes=12 * 2**20),
        name=kernel.__name__,
    )(*arrays)


def pack_kernel(
    me_ref, ey, z_up, z_down, z_two, z_six, ez, y_one, y_two, y_three,
    o0_ref, o1_ref, o2_ref, o3_ref, g_ref, m_ref,
):
    slots = g_ref.shape[0]
    cut = z_two.shape[0]
    skip = z_up.shape[0] - cut
    g_ref[:cut] = ey[:cut] + z_up[skip:] + z_down[skip:] + z_two[...] + z_six[...]
    g_ref[cut:] = ez[...] + y_one[...] + y_two[...] + y_three[...]
    chunks = m_ref.shape[0]
    piece = RANK // chunks
    batch = 2 * RANK // piece
    for g in range(slots // batch):
        rows = [g_ref[g * batch + q] for q in range(batch)]
        for c in range(chunks):
            for h in range(2):
                at = h * RANK + c * piece
                m_ref[c, 2 * g + h] = jnp.concatenate([r[:, at : at + piece] for r in rows], axis=1)
    for step, o_ref in enumerate((o0_ref, o1_ref, o2_ref, o3_ref)):
        o_ref[...] = m_ref[lax.rem(me_ref[0] + step, chunks)]


def pack(me, *arrays):
    vmem = pl.BlockSpec(memory_space=pltpu.VMEM)
    slots = arrays[4].shape[0] + arrays[5].shape[0]
    top, lanes = arrays[0].shape[1:]
    tiles = slots * RANK // 4 * top * 2 // (top * lanes)
    message = jax.ShapeDtypeStruct((tiles, top, lanes), jnp.float32)
    return pl.pallas_call(
        pack_kernel,
        in_specs=[pl.BlockSpec(memory_space=pltpu.SMEM)] + [vmem] * len(arrays),
        out_specs=(vmem,) * 4,
        out_shape=(message,) * 4,
        scratch_shapes=[
            pltpu.VMEM((slots, top, lanes), jnp.float32),
            pltpu.VMEM((4, tiles, top, lanes), jnp.float32),
        ],
        compiler_params=pltpu.CompilerParams(vmem_limit_bytes=8 * 2**20),
        name="pack",
    )(me, *arrays)


def final_kernel(me_ref, l_ref, m0_ref, m1_ref, m2_ref, m3_ref, out_ref, m_ref):
    chunks, tiles = m_ref.shape[0], m_ref.shape[1]
    for step, ref in enumerate((m0_ref, m1_ref, m2_ref, m3_ref)):
        m_ref[lax.rem(me_ref[0] + chunks - step, chunks)] = ref[...]
    share = l_ref.shape[1] - 1
    piece = RANK // chunks
    batch = 2 * RANK // piece
    for g in range(tiles // 2):
        rows = [m_ref[c, 2 * g + h] for c in range(chunks) for h in range(2)]
        turned = jnp.concatenate(rows, axis=0).T
        for q in range(batch):
            j = g * batch + q
            out_ref[j] = jnp.dot(
                turned[q * piece : (q + 1) * piece, :],
                unpacked(l_ref[j // share, j % share]),
                precision=HIGHEST,
                preferred_element_type=jnp.float32,
            )


def final(me, packed, messages, slots):
    vmem = pl.BlockSpec(memory_space=pltpu.VMEM)
    return pl.pallas_call(
        final_kernel,
        in_specs=[pl.BlockSpec(memory_space=pltpu.SMEM)] + [vmem] * 5,
        out_specs=vmem,
        out_shape=jax.ShapeDtypeStruct((slots, RANK // 4, RANK), jnp.float32),
        scratch_shapes=[pltpu.VMEM((4,) + messages[0].shape, jnp.float32)],
        compiler_params=pltpu.CompilerParams(vmem_limit_bytes=8 * 2**20),
        name="left_factor",
    )(me, packed, *messages)


def tie(*values):
    return lax.optimization_barrier(values)


def shards(
    bases,
    leaf_transfer,
    node_transfer,
    pair_transfer,
    quad_transfer,
    coupling,
    row_device,
    row_slot,
    block_count,
):
    n_rank = lax.axis_size("rk")
    rank_index = lax.axis_index("rk")
    me = rank_index.astype(jnp.int32).reshape(1)
    n_y, n_z, n_core = (lax.axis_size(axis) for axis in ("y", "z", "core"))
    core = lax.axis_index("core")
    local = jnp.swapaxes(bases[0], 1, 2)
    leaves, width, points = local.shape
    share = leaves // n_rank

    blocks = coupling[0]
    listed = blocks.shape[1]
    plan = Plan(n_y, n_z, leaves)
    dest = row_device[0, :, :, 0]
    valid = jnp.arange(listed, dtype=jnp.int32)[None, :] < block_count[0][:, None]
    rel_z = (dest // n_core - lax.axis_index("z")) % n_z
    rel_y = (dest // (n_core * n_z) - lax.axis_index("y")) % n_y
    place = plan.places(rel_y, rel_z, row_slot[0])
    place = place + jnp.where(dest % n_core == core, plan.total, 0)
    place = jnp.where(valid, place, n_core * plan.total).reshape(-1).astype(jnp.int32)

    pieces = lax.all_to_all(local, "rk", split_axis=0, concat_axis=0, tiled=True)
    moves = lax.dynamic_slice_in_dim(leaf_transfer[0], rank_index * share, share, 0)
    mine = leaf_factors(pieces.reshape(n_rank, share, width, points), moves)
    packed = lax.all_gather(mine, "rk", axis=0, tiled=False)

    near, far = plan.near, plan.total - plan.near
    away_near, away_far, keep_near, keep_far, leaf_weights = weighted_sums(
        me, place, blocks, packed, (near, far, near, far)
    )
    got_near = swap(away_near, "core", 1)
    got_near, away_far = tie(got_near, away_far)
    got_far = swap(away_far, "core", 1)

    def along(axis, up, down):
        return shift(up, axis, 1), shift(down, axis, -1)

    y_rows, z_rows, cut, rest = plan.rows["y"], plan.rows["z"], plan.cut, plan.rest
    y_two, z_up, z_down = run_round(
        round1_kernel, plan, (y_rows, z_rows // 2, z_rows // 2), keep_near, got_near
    )
    y_two, z_up, z_down, shared = tie(y_two, z_up, z_down, packed)
    rz_up, rz_down = along("z", z_up, z_down)
    ry_two = shift(y_two, "y", 2)
    gram1, term = level(first_level_kernel, shared, node_transfer[0])
    other = swap(term, "core", 1)
    rz_up, rz_down, got_far, other = tie(rz_up, rz_down, got_far, other)
    sums = (keep_far, got_far)

    y_up, y_down, z_up, z_down = run_round(
        round2_kernel, plan, (y_rows,) * 2 + (z_rows,) * 2, *sums, rz_up, rz_down
    )
    y_up, y_down, z_up, z_down, term = tie(y_up, y_down, z_up, z_down, term)
    rz_up, rz_down = along("z", z_up, z_down)
    ry_up, ry_down = along("y", y_up, y_down)
    gram2, term = level(next_level_kernel, term, other, pair_transfer[0])
    other = swap(term, "z", 1)
    ry_two, ry_up, ry_down, rz_up, rz_down, other = tie(
        ry_two, ry_up, ry_down, rz_up, rz_down, other
    )

    ride = z_rows + cut // 2 + cut
    ey, up, down = run_round(
        round3_kernel, plan, (y_rows, ride, ride), *sums, ry_two, ry_up, ry_down, rz_up, rz_down
    )
    up, down, term = tie(up, down, term)
    ride_up, ride_down = along("z", up, down)
    gram3, term = level(next_level_kernel, term, other, quad_transfer[0])
    other = swap(term, "z", 2)
    ride_up, ride_down, other = tie(ride_up, ride_down, other)

    both = z_rows + cut
    up, down = run_round(round4_kernel, plan, (both, both), *sums, ey, ride_up, ride_down)
    up, down, term = tie(up, down, term)
    rz_up, rz_down = along("z", up, down)
    node_weights = node_lower(me, (gram1, gram2, gram3, term, other), width)
    rz_up, rz_down, node_weights = tie(rz_up, rz_down, node_weights)

    ez, y_one, y_two, y_three, z_two, z_six = run_round(
        round5_kernel, plan, (rest,) * 4 + (cut,) * 2, *sums, ey, rz_up, rz_down
    )
    z_two = shift(z_two, "z", 2)
    z_six = shift(z_six, "z", -2)
    y_one, y_three = along("y", y_one, y_three)
    y_two = shift(y_two, "y", 2)
    messages = pack(me, ey, ride_up, ride_down, z_two, z_six, ez, y_one, y_two, y_three)
    arrived = [messages[0]] + [shift(messages[s], "rk", s) for s in range(1, n_rank)]
    coupled = final(me, packed, arrived, leaves)

    return (
        jnp.swapaxes(leaf_weights, 1, 2)[None],
        jnp.swapaxes(node_weights, 1, 2)[:, None],
        jnp.swapaxes(coupled, 1, 2)[None],
    )


def solution(mesh):
    devices = mesh.devices
    fine = Mesh(devices.reshape(4, 8, 2, devices.shape[1]), ("y", "z", "core", "rk"))
    clu = ("y", "z", "core")
    placed = (
        P(clu, None, None, "rk"),
        P(clu, None, None, None),
        P(clu, None, None),
        P(clu, None, None),
        P(clu, None, None),
        P(clu, None, None, "rk", None),
        P(clu, None, None, None),
        P(clu, None, None),
        P(clu, None),
    )
    return jax.shard_map(
        shards,
        mesh=fine,
        in_specs=placed,
        out_specs=(
            P(clu, None, None, "rk"),
            P(None, clu, None, "rk"),
            P(clu, None, None, "rk"),
        ),
        check_vma=False,
    )
```

```python
import functools

import jax
import jax.numpy as jnp
from jax import lax
from jax.experimental import pallas as pl
from jax.experimental.pallas import tpu as pltpu
from jax.sharding import Mesh
from jax.sharding import PartitionSpec as P

HIGHEST = lax.Precision.HIGHEST
RANK = 64
TILE = 8
TILES = RANK // TILE


def shift(value, axis, step):
    size = lax.axis_size(axis)
    return lax.ppermute(value, axis, [(i, (i + step) % size) for i in range(size)])


def swap(value, axis, mask):
    return lax.ppermute(value, axis, [(i, i ^ mask) for i in range(lax.axis_size(axis))])


def factor_in_place(s_ref):
    batch = s_ref.shape[2]
    sub = lax.broadcasted_iota(jnp.int32, (TILE, batch), 0)
    for jb in range(TILES):
        count = TILES - jb
        base = jb * TILE
        rows = [
            [s_ref[base + k, pl.ds((jb + t) * TILE, TILE), :] for t in range(count)]
            for k in range(TILE)
        ]
        for k in range(TILE):
            scale = lax.rsqrt(rows[k][0][k : k + 1, :])
            row = [v * scale for v in rows[k]]
            row[0] = jnp.where(sub >= k, row[0], 0.0)
            rows[k] = row
            for t in range(count):
                s_ref[base + k, pl.ds((jb + t) * TILE, TILE), :] = row[t]
            for t in range(jb):
                s_ref[base + k, pl.ds(t * TILE, TILE), :] = jnp.zeros((TILE, batch), jnp.float32)
            for k2 in range(k + 1, TILE):
                s = row[0][k2 : k2 + 1, :]
                rows[k2] = [v - s * u for v, u in zip(rows[k2], row)]
        for rb in range(jb + 1, TILES):
            for r in range(rb * TILE, (rb + 1) * TILE):
                heads = [s_ref[base + k, pl.ds(r, 1), :] for k in range(TILE)]
                for ct in range(rb, TILES):
                    total = s_ref[r, pl.ds(ct * TILE, TILE), :]
                    for k in range(TILE):
                        total = total - heads[k] * rows[k][ct - jb]
                    s_ref[r, pl.ds(ct * TILE, TILE), :] = total


def to_lanes(g_ref, s_ref):
    for a in range(RANK):
        s_ref[a] = g_ref[:, a, :].T


def column_of(s_ref, c):
    return s_ref[:, c, :].T


def packed_rows(matrix):
    half = matrix.shape[0] // 2
    return jnp.concatenate([matrix[:half], matrix[half:]], axis=1)


def unpacked(rows):
    half = rows.shape[-1] // 2
    return jnp.concatenate([rows[..., :half], rows[..., half:]], axis=-2)


def leaf_kernel(x_ref, move_ref, packed_ref, gram_ref, s_ref):
    sources, leaves = x_ref.shape[0], x_ref.shape[1]
    term = None
    for m in range(leaves):
        x = jnp.concatenate([x_ref[s, m] for s in range(sources)], axis=0)
        gram_ref[m] = lax.dot_general(
            x, x, (((1,), (1,)), ((), ())), precision=HIGHEST, preferred_element_type=jnp.float32
        )
    to_lanes(gram_ref, s_ref)
    for m in range(leaves):
        move = move_ref[m]
        moved = jnp.dot(gram_ref[m], move, precision=HIGHEST, preferred_element_type=jnp.float32)
        last = jnp.dot(move.T, moved, precision=HIGHEST, preferred_element_type=jnp.float32)
        term = last if term is None else term + last
    packed_ref[leaves] = packed_rows(term)
    factor_in_place(s_ref)
    half = RANK // 2
    for c in range(half):
        packed_ref[:leaves, c, :] = jnp.concatenate(
            [column_of(s_ref, c), column_of(s_ref, c + half)], axis=1
        )


def leaf_factors(x, moves):
    leaves = x.shape[1]
    vmem = pl.BlockSpec(memory_space=pltpu.VMEM)
    return pl.pallas_call(
        leaf_kernel,
        out_shape=jax.ShapeDtypeStruct((leaves + 1, RANK // 2, 2 * RANK), jnp.float32),
        in_specs=[vmem, vmem],
        out_specs=vmem,
        scratch_shapes=[
            pltpu.VMEM((leaves, RANK, RANK), jnp.float32),
            pltpu.VMEM((RANK, RANK, leaves), jnp.float32),
        ],
        compiler_params=pltpu.CompilerParams(vmem_limit_bytes=10 * 2**20),
        name="leaf_factors",
    )(x, moves)


def level_term(level, transfer):
    moved = jnp.dot(level, transfer, precision=HIGHEST, preferred_element_type=jnp.float32)
    return jnp.dot(transfer.T, moved, precision=HIGHEST, preferred_element_type=jnp.float32)


def first_level_kernel(packed_ref, move_ref, gram_ref, term_ref):
    leaves = packed_ref.shape[1] - 1
    gram = unpacked(jnp.sum(packed_ref[:, leaves], axis=0))
    gram_ref[...] = gram
    term_ref[...] = level_term(gram, move_ref[...])


def next_level_kernel(mine_ref, other_ref, move_ref, gram_ref, term_ref):
    gram = mine_ref[...] + other_ref[...]
    gram_ref[...] = gram
    term_ref[...] = level_term(gram, move_ref[...])


def level(kernel, *arrays):
    vmem = pl.BlockSpec(memory_space=pltpu.VMEM)
    return pl.pallas_call(
        kernel,
        in_specs=[vmem] * len(arrays),
        out_specs=(vmem, vmem),
        out_shape=(jax.ShapeDtypeStruct((RANK, RANK), jnp.float32),) * 2,
        compiler_params=pltpu.CompilerParams(vmem_limit_bytes=4 * 2**20),
        name=kernel.__name__,
    )(*arrays)


def node_kernel(me_ref, g1_ref, g2_ref, g3_ref, mine_ref, other_ref, out_ref, s_ref, l_ref):
    g_ref = l_ref
    for t, ref in enumerate((g1_ref, g2_ref, g3_ref)):
        g_ref[t] = ref[...]
    g_ref[3] = mine_ref[...] + other_ref[...]
    to_lanes(g_ref, s_ref)
    factor_in_place(s_ref)
    for c in range(RANK):
        l_ref[:, c, :] = column_of(s_ref, c)
    width = out_ref.shape[1]
    out_ref[...] = l_ref[:, pl.ds(pl.multiple_of(me_ref[0] * width, width), width), :]


def node_lower(me, grams, width):
    vmem = pl.BlockSpec(memory_space=pltpu.VMEM)
    count = len(grams) - 1
    return pl.pallas_call(
        node_kernel,
        out_shape=jax.ShapeDtypeStruct((count, width, RANK), jnp.float32),
        in_specs=[pl.BlockSpec(memory_space=pltpu.SMEM)] + [vmem] * len(grams),
        out_specs=vmem,
        scratch_shapes=[
            pltpu.VMEM((RANK, RANK, count), jnp.float32),
            pltpu.VMEM((count, RANK, RANK), jnp.float32),
        ],
        compiler_params=pltpu.CompilerParams(vmem_limit_bytes=10 * 2**20),
        name="node_factors",
    )(me, *grams)


def split(value):
    high = value.astype(jnp.bfloat16)
    return high, (value - high.astype(jnp.float32)).astype(jnp.bfloat16)


def block_products(blocks, packed):
    listed, width, rank = blocks.shape
    top = width // 2
    zero = jnp.zeros((rank, rank), jnp.bfloat16)
    high, low = split(unpacked(packed))
    wide = jnp.concatenate(
        [
            blocks[:, :top, :].reshape(listed * top, rank),
            blocks[:, top:, :].reshape(listed * top, rank),
        ],
        axis=1,
    )
    w_high = jnp.concatenate(
        [jnp.concatenate([high, zero], axis=1), jnp.concatenate([zero, high], axis=1)], axis=0
    )
    w_low = jnp.concatenate(
        [jnp.concatenate([low, zero], axis=1), jnp.concatenate([zero, low], axis=1)], axis=0
    )
    c_high, c_low = split(wide)
    total = jnp.dot(
        jnp.concatenate([c_high, c_low], axis=1),
        jnp.concatenate([w_high, w_high], axis=0),
        preferred_element_type=jnp.float32,
    )
    return total + jnp.dot(c_high, w_low, preferred_element_type=jnp.float32)


def product_kernel(
    me_ref, place_ref, c_hbm, l_ref, o0_ref, o1_ref, o2_ref, o3_ref, rows_ref,
    acc_ref, c_ref, sems,
):
    leaves, listed, width, _ = c_hbm.shape
    slots, group = c_ref.shape[0], c_ref.shape[1]
    steps = leaves // group
    top = width // 2
    share = l_ref.shape[1] - 1

    def fetch(step, slot):
        return pltpu.make_async_copy(
            c_hbm.at[pl.ds(step * group, group)], c_ref.at[slot], sems.at[slot]
        )

    for step in range(slots - 1):
        fetch(step, step).start()
    acc_ref[...] = jnp.zeros_like(acc_ref)

    me = me_ref[0]
    at = pl.multiple_of(lax.rem(me, 2) * width, width)
    for j in range(leaves):
        rows = l_ref[j // share, j % share, pl.ds(at, width), :]
        rows_ref[j] = jnp.where(me < 2, rows[:, :RANK], rows[:, RANK:])

    def body(step, carry):
        slot = lax.rem(step, slots)
        ahead = step + slots - 1

        @pl.when(ahead < steps)
        def _():
            fetch(ahead, lax.rem(ahead, slots)).start()

        fetch(step, slot).wait()
        source = lax.div(step * group, share)
        first_leaf = step * group - source * share
        totals = [
            block_products(c_ref[slot, u], l_ref[source, first_leaf + u]) for u in range(group)
        ]
        for u in range(group):
            for k in range(listed):
                place = place_ref[(step * group + u) * listed + k]
                acc_ref[place] = acc_ref[place] + totals[u][k * top : (k + 1) * top, :]
        return carry

    lax.fori_loop(0, steps, body, 0)
    at = 0
    for ref in (o0_ref, o1_ref, o2_ref, o3_ref):
        ref[...] = acc_ref[at : at + ref.shape[0]]
        at += ref.shape[0]


def weighted_sums(me, place, blocks, packed, parts):
    leaves, listed, width, rank = blocks.shape
    top = width // 2
    group, slots = 4, 4
    vmem = pl.BlockSpec(memory_space=pltpu.VMEM)
    hbm = pl.BlockSpec(memory_space=pltpu.HBM)

    def out(rows):
        return jax.ShapeDtypeStruct((rows, top, 2 * rank), jnp.float32)

    return pl.pallas_call(
        product_kernel,
        in_specs=[
            pl.BlockSpec(memory_space=pltpu.SMEM),
            pl.BlockSpec(memory_space=pltpu.SMEM),
            hbm,
            vmem,
        ],
        out_specs=(vmem,) * (len(parts) + 1),
        scratch_shapes=[
            pltpu.VMEM((sum(parts) + TILE, top, 2 * rank), jnp.float32),
            pltpu.VMEM((slots, group, listed, width, rank), jnp.float32),
            pltpu.SemaphoreType.DMA((slots,)),
        ],
        out_shape=tuple(out(rows) for rows in parts)
        + (jax.ShapeDtypeStruct((leaves, width, rank), jnp.float32),),
        compiler_params=pltpu.CompilerParams(vmem_limit_bytes=16 * 2**20),
        name="weighted_sums",
    )(me, place, pltpu.with_memory_space_constraint(blocks, pltpu.HBM), packed)


class Plan:
    def __init__(self, n_y, n_z, slots):
        self.n_y, self.n_z = n_y, n_z
        self.cut = 3 * slots // 8
        self.rest = slots - self.cut
        self.rows = {"y": n_z * self.cut, "z": n_y * self.rest}
        self.base = {}
        at = 0
        for group in (
            ("y", 2), ("z", 4), ("y", 1), ("y", 3), ("z", 3), ("z", 5), ("y", 0), ("z", 2),
            ("z", 6), ("z", 1), ("z", 7), ("z", 0),
        ):
            if group == ("y", 1):
                self.near = at
            self.base[group] = at
            at += self.rows[group[0]]
        self.total = at

    def places(self, rel_y, rel_z, slot):
        base_y = sum(jnp.where(rel_y == r, self.base["y", r], 0) for r in range(self.n_y))
        base_z = sum(jnp.where(rel_z == r, self.base["z", r], 0) for r in range(self.n_z))
        by_y = base_y + rel_z * self.cut + slot
        by_z = base_z + rel_y * self.rest + slot - self.cut
        return jnp.where(slot < self.cut, by_y, by_z)

    def part(self, ref, group):
        at = self.base[group] - (0 if self.base[group] < self.near else self.near)
        return ref[at : at + self.rows[group[0]]]

    def both(self, keep, got, group):
        return self.part(keep, group) + self.part(got, group)


def low_add(whole, extra):
    rows = extra.shape[0]
    return jnp.concatenate([whole[:rows] + extra, whole[rows:]], axis=0)


def high_add(whole, extra):
    rows = whole.shape[0] - extra.shape[0]
    return jnp.concatenate([whole[:rows], whole[rows:] + extra], axis=0)


def round1_kernel(plan, keep, got, y_two, z_up, z_down):
    y_two[...] = plan.both(keep, got, ("y", 2))
    z = plan.both(keep, got, ("z", 4))
    half = z.shape[0] // 2
    z_up[...] = z[:half]
    z_down[...] = z[half:]


def round2_kernel(plan, keep, got, rz_up, rz_down, y_up, y_down, z_up, z_down):
    y_up[...] = plan.both(keep, got, ("y", 1))
    y_down[...] = plan.both(keep, got, ("y", 3))
    z_up[...] = low_add(plan.both(keep, got, ("z", 3)), rz_up[...])
    z_down[...] = high_add(plan.both(keep, got, ("z", 5)), rz_down[...])


def round3_kernel(plan, keep, got, ry_two, ry_up, ry_down, rz_up, rz_down, ey, z_up, z_down):
    ey[...] = plan.both(keep, got, ("y", 0)) + ry_two[...] + ry_up[...] + ry_down[...]
    rows, cut = plan.rows["z"], plan.cut
    half = cut // 2
    z_up[:rows] = plan.both(keep, got, ("z", 2)) + rz_up[...]
    z_up[rows : rows + half] = ey[4 * cut : 4 * cut + half]
    z_up[rows + half :] = ey[cut : 2 * cut]
    z_down[:rows] = plan.both(keep, got, ("z", 6)) + rz_down[...]
    z_down[rows : rows + half] = ey[4 * cut + half : 5 * cut]
    z_down[rows + half :] = ey[7 * cut :]


def round4_kernel(plan, keep, got, ey, rz_up, rz_down, z_up, z_down):
    rows, cut = plan.rows["z"], plan.cut
    half = cut // 2
    z_up[:rows] = plan.both(keep, got, ("z", 1)) + rz_up[:rows]
    z_up[rows:] = low_add(ey[3 * cut : 4 * cut], rz_up[rows : rows + half])
    z_down[:rows] = plan.both(keep, got, ("z", 7)) + rz_down[:rows]
    z_down[rows:] = high_add(ey[5 * cut : 6 * cut], rz_down[rows : rows + half])


def round5_kernel(plan, keep, got, ey, rz_up, rz_down, own, y_one, y_two, y_three, z_two, z_six):
    rows, cut, rest = plan.rows["z"], plan.cut, plan.rest
    ez = plan.both(keep, got, ("z", 0)) + rz_up[:rows] + rz_down[:rows]
    for r, ref in enumerate((own, y_one, y_two, y_three)):
        ref[...] = ez[r * rest : (r + 1) * rest]
    z_two[...] = ey[2 * cut : 3 * cut] + rz_up[rows:]
    z_six[...] = ey[6 * cut : 7 * cut] + rz_down[rows:]


def run_round(kernel, plan, rows, *arrays):
    vmem = pl.BlockSpec(memory_space=pltpu.VMEM)
    tail = arrays[0].shape[1:]
    return pl.pallas_call(
        functools.partial(kernel, plan),
        in_specs=[vmem] * len(arrays),
        out_specs=(vmem,) * len(rows),
        out_shape=tuple(jax.ShapeDtypeStruct((r,) + tail, jnp.float32) for r in rows),
        compiler_params=pltpu.CompilerParams(vmem_limit_bytes=12 * 2**20),
        name=kernel.__name__,
    )(*arrays)


def pack_kernel(
    me_ref, ey, z_up, z_down, z_two, z_six, ez, y_one, y_two, y_three,
    o0_ref, o1_ref, o2_ref, o3_ref, g_ref, m_ref,
):
    slots = g_ref.shape[0]
    cut = z_two.shape[0]
    skip = z_up.shape[0] - cut
    g_ref[:cut] = ey[:cut] + z_up[skip:] + z_down[skip:] + z_two[...] + z_six[...]
    g_ref[cut:] = ez[...] + y_one[...] + y_two[...] + y_three[...]
    chunks = m_ref.shape[0]
    piece = RANK // chunks
    batch = 2 * RANK // piece
    for g in range(slots // batch):
        rows = [g_ref[g * batch + q] for q in range(batch)]
        for c in range(chunks):
            for h in range(2):
                at = h * RANK + c * piece
                m_ref[c, 2 * g + h] = jnp.concatenate([r[:, at : at + piece] for r in rows], axis=1)
    for step, o_ref in enumerate((o0_ref, o1_ref, o2_ref, o3_ref)):
        o_ref[...] = m_ref[lax.rem(me_ref[0] + step, chunks)]


def pack(me, *arrays):
    vmem = pl.BlockSpec(memory_space=pltpu.VMEM)
    slots = arrays[4].shape[0] + arrays[5].shape[0]
    top, lanes = arrays[0].shape[1:]
    tiles = slots * RANK // 4 * top * 2 // (top * lanes)
    message = jax.ShapeDtypeStruct((tiles, top, lanes), jnp.float32)
    return pl.pallas_call(
        pack_kernel,
        in_specs=[pl.BlockSpec(memory_space=pltpu.SMEM)] + [vmem] * len(arrays),
        out_specs=(vmem,) * 4,
        out_shape=(message,) * 4,
        scratch_shapes=[
            pltpu.VMEM((slots, top, lanes), jnp.float32),
            pltpu.VMEM((4, tiles, top, lanes), jnp.float32),
        ],
        compiler_params=pltpu.CompilerParams(vmem_limit_bytes=8 * 2**20),
        name="pack",
    )(me, *arrays)


def final_kernel(me_ref, l_ref, m0_ref, m1_ref, m2_ref, m3_ref, out_ref, m_ref):
    chunks, tiles = m_ref.shape[0], m_ref.shape[1]
    for step, ref in enumerate((m0_ref, m1_ref, m2_ref, m3_ref)):
        m_ref[lax.rem(me_ref[0] + chunks - step, chunks)] = ref[...]
    share = l_ref.shape[1] - 1
    piece = RANK // chunks
    batch = 2 * RANK // piece
    for g in range(tiles // 2):
        rows = [m_ref[c, 2 * g + h] for c in range(chunks) for h in range(2)]
        turned = jnp.concatenate(rows, axis=0).T
        for q in range(batch):
            j = g * batch + q
            high, low = split(turned[q * piece : (q + 1) * piece, :])
            w_high, w_low = split(unpacked(l_ref[j // share, j % share]))
            total = jnp.dot(high, w_high, preferred_element_type=jnp.float32)
            total = total + jnp.dot(low, w_high, preferred_element_type=jnp.float32)
            out_ref[j] = total + jnp.dot(high, w_low, preferred_element_type=jnp.float32)


def final(me, packed, messages, slots):
    vmem = pl.BlockSpec(memory_space=pltpu.VMEM)
    return pl.pallas_call(
        final_kernel,
        in_specs=[pl.BlockSpec(memory_space=pltpu.SMEM)] + [vmem] * 5,
        out_specs=vmem,
        out_shape=jax.ShapeDtypeStruct((slots, RANK // 4, RANK), jnp.float32),
        scratch_shapes=[pltpu.VMEM((4,) + messages[0].shape, jnp.float32)],
        compiler_params=pltpu.CompilerParams(vmem_limit_bytes=8 * 2**20),
        name="left_factor",
    )(me, packed, *messages)


def tie(*values):
    return lax.optimization_barrier(values)


def shards(
    bases,
    leaf_transfer,
    node_transfer,
    pair_transfer,
    quad_transfer,
    coupling,
    row_device,
    row_slot,
    block_count,
):
    n_rank = lax.axis_size("rk")
    rank_index = lax.axis_index("rk")
    me = rank_index.astype(jnp.int32).reshape(1)
    n_y, n_z, n_core = (lax.axis_size(axis) for axis in ("y", "z", "core"))
    core = lax.axis_index("core")
    local = jnp.swapaxes(bases[0], 1, 2)
    leaves, width, points = local.shape
    share = leaves // n_rank

    blocks = coupling[0]
    listed = blocks.shape[1]
    plan = Plan(n_y, n_z, leaves)
    dest = row_device[0, :, :, 0]
    valid = jnp.arange(listed, dtype=jnp.int32)[None, :] < block_count[0][:, None]
    rel_z = (dest // n_core - lax.axis_index("z")) % n_z
    rel_y = (dest // (n_core * n_z) - lax.axis_index("y")) % n_y
    place = plan.places(rel_y, rel_z, row_slot[0])
    place = place + jnp.where(dest % n_core == core, plan.total, 0)
    place = jnp.where(valid, place, n_core * plan.total).reshape(-1).astype(jnp.int32)

    pieces = lax.all_to_all(local, "rk", split_axis=0, concat_axis=0, tiled=True)
    moves = lax.dynamic_slice_in_dim(leaf_transfer[0], rank_index * share, share, 0)
    mine = leaf_factors(pieces.reshape(n_rank, share, width, points), moves)
    packed = lax.all_gather(mine, "rk", axis=0, tiled=False)

    near, far = plan.near, plan.total - plan.near
    away_near, away_far, keep_near, keep_far, leaf_weights = weighted_sums(
        me, place, blocks, packed, (near, far, near, far)
    )
    got_near = swap(away_near, "core", 1)
    got_near, away_far = tie(got_near, away_far)
    got_far = swap(away_far, "core", 1)

    def along(axis, up, down):
        return shift(up, axis, 1), shift(down, axis, -1)

    y_rows, z_rows, cut, rest = plan.rows["y"], plan.rows["z"], plan.cut, plan.rest
    y_two, z_up, z_down = run_round(
        round1_kernel, plan, (y_rows, z_rows // 2, z_rows // 2), keep_near, got_near
    )
    y_two, z_up, z_down, shared = tie(y_two, z_up, z_down, packed)
    rz_up, rz_down = along("z", z_up, z_down)
    ry_two = shift(y_two, "y", 2)
    gram1, term = level(first_level_kernel, shared, node_transfer[0])
    other = swap(term, "core", 1)
    ry_two, rz_up, rz_down, got_far, other = tie(ry_two, rz_up, rz_down, got_far, other)
    sums = (keep_far, got_far)

    y_up, y_down, z_up, z_down = run_round(
        round2_kernel, plan, (y_rows,) * 2 + (z_rows,) * 2, *sums, rz_up, rz_down
    )
    y_up, y_down, z_up, z_down, term = tie(y_up, y_down, z_up, z_down, term)
    rz_up, rz_down = along("z", z_up, z_down)
    ry_up, ry_down = along("y", y_up, y_down)
    gram2, term = level(next_level_kernel, term, other, pair_transfer[0])
    other = swap(term, "z", 1)
    ry_up, ry_down, rz_up, rz_down, other = tie(ry_up, ry_down, rz_up, rz_down, other)

    ride = z_rows + cut // 2 + cut
    ey, up, down = run_round(
        round3_kernel, plan, (y_rows, ride, ride), *sums, ry_two, ry_up, ry_down, rz_up, rz_down
    )
    up, down, term = tie(up, down, term)
    ride_up, ride_down = along("z", up, down)
    gram3, term = level(next_level_kernel, term, other, quad_transfer[0])
    other = swap(term, "z", 2)
    ride_up, ride_down, other = tie(ride_up, ride_down, other)

    both = z_rows + cut
    up, down = run_round(round4_kernel, plan, (both, both), *sums, ey, ride_up, ride_down)
    up, down, term = tie(up, down, term)
    rz_up, rz_down = along("z", up, down)
    node_weights = node_lower(me, (gram1, gram2, gram3, term, other), width)
    rz_up, rz_down, node_weights = tie(rz_up, rz_down, node_weights)

    ez, y_one, y_two, y_three, z_two, z_six = run_round(
        round5_kernel, plan, (rest,) * 4 + (cut,) * 2, *sums, ey, rz_up, rz_down
    )
    z_two = shift(z_two, "z", 2)
    z_six = shift(z_six, "z", -2)
    y_one, y_three = along("y", y_one, y_three)
    y_two = shift(y_two, "y", 2)
    messages = pack(me, ey, ride_up, ride_down, z_two, z_six, ez, y_one, y_two, y_three)
    arrived = [messages[0]] + [shift(messages[s], "rk", s) for s in range(1, n_rank)]
    coupled = final(me, packed, arrived, leaves)

    return (
        jnp.swapaxes(leaf_weights, 1, 2)[None],
        jnp.swapaxes(node_weights, 1, 2)[:, None],
        jnp.swapaxes(coupled, 1, 2)[None],
    )


def solution(mesh):
    devices = mesh.devices
    fine = Mesh(devices.reshape(4, 8, 2, devices.shape[1]), ("y", "z", "core", "rk"))
    clu = ("y", "z", "core")
    placed = (
        P(clu, None, None, "rk"),
        P(clu, None, None, None),
        P(clu, None, None),
        P(clu, None, None),
        P(clu, None, None),
        P(clu, None, None, "rk", None),
        P(clu, None, None, None),
        P(clu, None, None),
        P(clu, None),
    )
    return jax.shard_map(
        shards,
        mesh=fine,
        in_specs=placed,
        out_specs=(
            P(clu, None, None, "rk"),
            P(None, clu, None, "rk"),
            P(clu, None, None, "rk"),
        ),
        check_vma=False,
    )
```

```python
import functools

import jax
import jax.numpy as jnp
from jax import lax
from jax.experimental import pallas as pl
from jax.experimental.pallas import tpu as pltpu
from jax.sharding import Mesh
from jax.sharding import PartitionSpec as P

HIGHEST = lax.Precision.HIGHEST
RANK = 64
TILE = 8
TILES = RANK // TILE


def shift(value, axis, step):
    size = lax.axis_size(axis)
    return lax.ppermute(value, axis, [(i, (i + step) % size) for i in range(size)])


def swap(value, axis, mask):
    return lax.ppermute(value, axis, [(i, i ^ mask) for i in range(lax.axis_size(axis))])


def factor_in_place(s_ref):
    batch = s_ref.shape[2]
    sub = lax.broadcasted_iota(jnp.int32, (TILE, batch), 0)
    for jb in range(TILES):
        count = TILES - jb
        base = jb * TILE
        rows = [
            [s_ref[base + k, pl.ds((jb + t) * TILE, TILE), :] for t in range(count)]
            for k in range(TILE)
        ]
        for k in range(TILE):
            scale = lax.rsqrt(rows[k][0][k : k + 1, :])
            row = [v * scale for v in rows[k]]
            row[0] = jnp.where(sub >= k, row[0], 0.0)
            rows[k] = row
            for t in range(count):
                s_ref[base + k, pl.ds((jb + t) * TILE, TILE), :] = row[t]
            for t in range(jb):
                s_ref[base + k, pl.ds(t * TILE, TILE), :] = jnp.zeros((TILE, batch), jnp.float32)
            for k2 in range(k + 1, TILE):
                s = row[0][k2 : k2 + 1, :]
                rows[k2] = [v - s * u for v, u in zip(rows[k2], row)]
        for rb in range(jb + 1, TILES):
            for r in range(rb * TILE, (rb + 1) * TILE):
                heads = [s_ref[base + k, pl.ds(r, 1), :] for k in range(TILE)]
                for ct in range(rb, TILES):
                    total = s_ref[r, pl.ds(ct * TILE, TILE), :]
                    for k in range(TILE):
                        total = total - heads[k] * rows[k][ct - jb]
                    s_ref[r, pl.ds(ct * TILE, TILE), :] = total


def to_lanes(g_ref, s_ref):
    for a in range(RANK):
        s_ref[a] = g_ref[:, a, :].T


def column_of(s_ref, c):
    return s_ref[:, c, :].T


def packed_rows(matrix):
    half = matrix.shape[0] // 2
    return jnp.concatenate([matrix[:half], matrix[half:]], axis=1)


def unpacked(rows):
    half = rows.shape[-1] // 2
    return jnp.concatenate([rows[..., :half], rows[..., half:]], axis=-2)


def leaf_kernel(x_ref, move_ref, packed_ref, gram_ref, s_ref):
    sources, leaves = x_ref.shape[0], x_ref.shape[1]
    term = None
    for m in range(leaves):
        x = jnp.concatenate([x_ref[s, m] for s in range(sources)], axis=0)
        gram_ref[m] = lax.dot_general(
            x, x, (((1,), (1,)), ((), ())), precision=HIGHEST, preferred_element_type=jnp.float32
        )
    to_lanes(gram_ref, s_ref)
    for m in range(leaves):
        move = move_ref[m]
        moved = jnp.dot(gram_ref[m], move, precision=HIGHEST, preferred_element_type=jnp.float32)
        last = jnp.dot(move.T, moved, precision=HIGHEST, preferred_element_type=jnp.float32)
        term = last if term is None else term + last
    packed_ref[leaves] = packed_rows(term)
    factor_in_place(s_ref)
    half = RANK // 2
    for c in range(half):
        packed_ref[:leaves, c, :] = jnp.concatenate(
            [column_of(s_ref, c), column_of(s_ref, c + half)], axis=1
        )


def leaf_factors(x, moves):
    leaves = x.shape[1]
    vmem = pl.BlockSpec(memory_space=pltpu.VMEM)
    return pl.pallas_call(
        leaf_kernel,
        out_shape=jax.ShapeDtypeStruct((leaves + 1, RANK // 2, 2 * RANK), jnp.float32),
        in_specs=[vmem, vmem],
        out_specs=vmem,
        scratch_shapes=[
            pltpu.VMEM((leaves, RANK, RANK), jnp.float32),
            pltpu.VMEM((RANK, RANK, leaves), jnp.float32),
        ],
        compiler_params=pltpu.CompilerParams(vmem_limit_bytes=10 * 2**20),
        name="leaf_factors",
    )(x, moves)


def level_term(level, transfer):
    moved = jnp.dot(level, transfer, precision=HIGHEST, preferred_element_type=jnp.float32)
    return jnp.dot(transfer.T, moved, precision=HIGHEST, preferred_element_type=jnp.float32)


def first_level_kernel(packed_ref, move_ref, gram_ref, term_ref):
    leaves = packed_ref.shape[1] - 1
    gram = unpacked(jnp.sum(packed_ref[:, leaves], axis=0))
    gram_ref[...] = gram
    term_ref[...] = level_term(gram, move_ref[...])


def next_level_kernel(mine_ref, other_ref, move_ref, gram_ref, term_ref):
    gram = mine_ref[...] + other_ref[...]
    gram_ref[...] = gram
    term_ref[...] = level_term(gram, move_ref[...])


def level(kernel, *arrays):
    vmem = pl.BlockSpec(memory_space=pltpu.VMEM)
    return pl.pallas_call(
        kernel,
        in_specs=[vmem] * len(arrays),
        out_specs=(vmem, vmem),
        out_shape=(jax.ShapeDtypeStruct((RANK, RANK), jnp.float32),) * 2,
        compiler_params=pltpu.CompilerParams(vmem_limit_bytes=4 * 2**20),
        name=kernel.__name__,
    )(*arrays)


def node_kernel(me_ref, g1_ref, g2_ref, g3_ref, mine_ref, other_ref, out_ref, s_ref, l_ref):
    g_ref = l_ref
    for t, ref in enumerate((g1_ref, g2_ref, g3_ref)):
        g_ref[t] = ref[...]
    g_ref[3] = mine_ref[...] + other_ref[...]
    to_lanes(g_ref, s_ref)
    factor_in_place(s_ref)
    for c in range(RANK):
        l_ref[:, c, :] = column_of(s_ref, c)
    width = out_ref.shape[1]
    out_ref[...] = l_ref[:, pl.ds(pl.multiple_of(me_ref[0] * width, width), width), :]


def node_lower(me, grams, width):
    vmem = pl.BlockSpec(memory_space=pltpu.VMEM)
    count = len(grams) - 1
    return pl.pallas_call(
        node_kernel,
        out_shape=jax.ShapeDtypeStruct((count, width, RANK), jnp.float32),
        in_specs=[pl.BlockSpec(memory_space=pltpu.SMEM)] + [vmem] * len(grams),
        out_specs=vmem,
        scratch_shapes=[
            pltpu.VMEM((RANK, RANK, count), jnp.float32),
            pltpu.VMEM((count, RANK, RANK), jnp.float32),
        ],
        compiler_params=pltpu.CompilerParams(vmem_limit_bytes=10 * 2**20),
        name="node_factors",
    )(me, *grams)


def split(value):
    high = value.astype(jnp.bfloat16)
    return high, (value - high.astype(jnp.float32)).astype(jnp.bfloat16)


def block_products(blocks, packed):
    listed, width, rank = blocks.shape
    top = width // 2
    zero = jnp.zeros((rank, rank), jnp.bfloat16)
    high, low = split(unpacked(packed))
    wide = jnp.concatenate(
        [
            blocks[:, :top, :].reshape(listed * top, rank),
            blocks[:, top:, :].reshape(listed * top, rank),
        ],
        axis=1,
    )
    w_high = jnp.concatenate(
        [jnp.concatenate([high, zero], axis=1), jnp.concatenate([zero, high], axis=1)], axis=0
    )
    w_low = jnp.concatenate(
        [jnp.concatenate([low, zero], axis=1), jnp.concatenate([zero, low], axis=1)], axis=0
    )
    c_high, c_low = split(wide)
    total = jnp.dot(
        jnp.concatenate([c_high, c_low], axis=1),
        jnp.concatenate([w_high, w_high], axis=0),
        preferred_element_type=jnp.float32,
    )
    return total + jnp.dot(c_high, w_low, preferred_element_type=jnp.float32)


def product_kernel(
    me_ref, place_ref, c_hbm, l_ref, o0_ref, o1_ref, o2_ref, o3_ref, rows_ref,
    acc_ref, c_ref, sems,
):
    leaves, listed, width, _ = c_hbm.shape
    slots, group = c_ref.shape[0], c_ref.shape[1]
    steps = leaves // group
    top = width // 2
    share = l_ref.shape[1] - 1

    def fetch(step, slot):
        return pltpu.make_async_copy(
            c_hbm.at[pl.ds(step * group, group)], c_ref.at[slot], sems.at[slot]
        )

    for step in range(slots - 1):
        fetch(step, step).start()
    acc_ref[...] = jnp.zeros_like(acc_ref)

    me = me_ref[0]
    at = pl.multiple_of(lax.rem(me, 2) * width, width)
    for j in range(leaves):
        rows = l_ref[j // share, j % share, pl.ds(at, width), :]
        rows_ref[j] = jnp.where(me < 2, rows[:, :RANK], rows[:, RANK:])

    def body(step, carry):
        slot = lax.rem(step, slots)
        ahead = step + slots - 1

        @pl.when(ahead < steps)
        def _():
            fetch(ahead, lax.rem(ahead, slots)).start()

        fetch(step, slot).wait()
        source = lax.div(step * group, share)
        first_leaf = step * group - source * share
        totals = [
            block_products(c_ref[slot, u], l_ref[source, first_leaf + u]) for u in range(group)
        ]
        for u in range(group):
            for k in range(listed):
                place = place_ref[(step * group + u) * listed + k]
                acc_ref[place] = acc_ref[place] + totals[u][k * top : (k + 1) * top, :]
        return carry

    lax.fori_loop(0, steps, body, 0)
    at = 0
    for ref in (o0_ref, o1_ref, o2_ref, o3_ref):
        ref[...] = acc_ref[at : at + ref.shape[0]]
        at += ref.shape[0]


def weighted_sums(me, place, blocks, packed, parts):
    leaves, listed, width, rank = blocks.shape
    top = width // 2
    group, slots = 4, 4
    vmem = pl.BlockSpec(memory_space=pltpu.VMEM)
    hbm = pl.BlockSpec(memory_space=pltpu.HBM)

    def out(rows):
        return jax.ShapeDtypeStruct((rows, top, 2 * rank), jnp.float32)

    return pl.pallas_call(
        product_kernel,
        in_specs=[
            pl.BlockSpec(memory_space=pltpu.SMEM),
            pl.BlockSpec(memory_space=pltpu.SMEM),
            hbm,
            vmem,
        ],
        out_specs=(vmem,) * (len(parts) + 1),
        scratch_shapes=[
            pltpu.VMEM((sum(parts) + TILE, top, 2 * rank), jnp.float32),
            pltpu.VMEM((slots, group, listed, width, rank), jnp.float32),
            pltpu.SemaphoreType.DMA((slots,)),
        ],
        out_shape=tuple(out(rows) for rows in parts)
        + (jax.ShapeDtypeStruct((leaves, width, rank), jnp.float32),),
        compiler_params=pltpu.CompilerParams(vmem_limit_bytes=16 * 2**20),
        name="weighted_sums",
    )(me, place, pltpu.with_memory_space_constraint(blocks, pltpu.HBM), packed)


class Plan:
    def __init__(self, n_y, n_z, slots):
        self.n_y, self.n_z = n_y, n_z
        self.cut = 7 * slots // 16
        self.rest = slots - self.cut
        self.rows = {"y": n_z * self.cut, "z": n_y * self.rest}
        self.base = {}
        at = 0
        for group in (
            ("y", 2), ("z", 4), ("y", 1), ("y", 3), ("z", 3), ("z", 5), ("y", 0), ("z", 2),
            ("z", 6), ("z", 1), ("z", 7), ("z", 0),
        ):
            if group == ("y", 1):
                self.near = at
            self.base[group] = at
            at += self.rows[group[0]]
        self.total = at

    def places(self, rel_y, rel_z, slot):
        base_y = sum(jnp.where(rel_y == r, self.base["y", r], 0) for r in range(self.n_y))
        base_z = sum(jnp.where(rel_z == r, self.base["z", r], 0) for r in range(self.n_z))
        by_y = base_y + rel_z * self.cut + slot
        by_z = base_z + rel_y * self.rest + slot - self.cut
        return jnp.where(slot < self.cut, by_y, by_z)

    def part(self, ref, group):
        at = self.base[group] - (0 if self.base[group] < self.near else self.near)
        return ref[at : at + self.rows[group[0]]]

    def both(self, keep, got, group):
        return self.part(keep, group) + self.part(got, group)


def low_add(whole, extra):
    rows = extra.shape[0]
    return jnp.concatenate([whole[:rows] + extra, whole[rows:]], axis=0)


def high_add(whole, extra):
    rows = whole.shape[0] - extra.shape[0]
    return jnp.concatenate([whole[:rows], whole[rows:] + extra], axis=0)


def round1_kernel(plan, keep, got, y_two, z_up, z_down):
    y_two[...] = plan.both(keep, got, ("y", 2))
    z = plan.both(keep, got, ("z", 4))
    half = z.shape[0] // 2
    z_up[...] = z[:half]
    z_down[...] = z[half:]


def round2_kernel(plan, keep, got, rz_up, rz_down, y_up, y_down, z_up, z_down):
    y_up[...] = plan.both(keep, got, ("y", 1))
    y_down[...] = plan.both(keep, got, ("y", 3))
    z_up[...] = low_add(plan.both(keep, got, ("z", 3)), rz_up[...])
    z_down[...] = high_add(plan.both(keep, got, ("z", 5)), rz_down[...])


def round3_kernel(plan, keep, got, ry_two, ry_up, ry_down, rz_up, rz_down, ey, z_up, z_down):
    ey[...] = plan.both(keep, got, ("y", 0)) + ry_two[...] + ry_up[...] + ry_down[...]
    rows, cut = plan.rows["z"], plan.cut
    half = cut // 2
    z_up[:rows] = plan.both(keep, got, ("z", 2)) + rz_up[...]
    z_up[rows : rows + half] = ey[4 * cut : 4 * cut + half]
    z_up[rows + half :] = ey[cut : 2 * cut]
    z_down[:rows] = plan.both(keep, got, ("z", 6)) + rz_down[...]
    z_down[rows : rows + half] = ey[4 * cut + half : 5 * cut]
    z_down[rows + half :] = ey[7 * cut :]


def round4_kernel(plan, keep, got, ey, rz_up, rz_down, z_up, z_down):
    rows, cut = plan.rows["z"], plan.cut
    half = cut // 2
    z_up[:rows] = plan.both(keep, got, ("z", 1)) + rz_up[:rows]
    z_up[rows:] = low_add(ey[3 * cut : 4 * cut], rz_up[rows : rows + half])
    z_down[:rows] = plan.both(keep, got, ("z", 7)) + rz_down[:rows]
    z_down[rows:] = high_add(ey[5 * cut : 6 * cut], rz_down[rows : rows + half])


def round5_kernel(plan, keep, got, ey, rz_up, rz_down, own, y_one, y_two, y_three, z_two, z_six):
    rows, cut, rest = plan.rows["z"], plan.cut, plan.rest
    ez = plan.both(keep, got, ("z", 0)) + rz_up[:rows] + rz_down[:rows]
    for r, ref in enumerate((own, y_one, y_two, y_three)):
        ref[...] = ez[r * rest : (r + 1) * rest]
    z_two[...] = ey[2 * cut : 3 * cut] + rz_up[rows:]
    z_six[...] = ey[6 * cut : 7 * cut] + rz_down[rows:]


def run_round(kernel, plan, rows, *arrays):
    vmem = pl.BlockSpec(memory_space=pltpu.VMEM)
    tail = arrays[0].shape[1:]
    return pl.pallas_call(
        functools.partial(kernel, plan),
        in_specs=[vmem] * len(arrays),
        out_specs=(vmem,) * len(rows),
        out_shape=tuple(jax.ShapeDtypeStruct((r,) + tail, jnp.float32) for r in rows),
        compiler_params=pltpu.CompilerParams(vmem_limit_bytes=12 * 2**20),
        name=kernel.__name__,
    )(*arrays)


def pack_kernel(
    me_ref, ey, z_up, z_down, z_two, z_six, ez, y_one, y_two, y_three,
    o0_ref, o1_ref, o2_ref, o3_ref, g_ref, m_ref,
):
    slots = g_ref.shape[0]
    cut = z_two.shape[0]
    skip = z_up.shape[0] - cut
    g_ref[:cut] = ey[:cut] + z_up[skip:] + z_down[skip:] + z_two[...] + z_six[...]
    g_ref[cut:] = ez[...] + y_one[...] + y_two[...] + y_three[...]
    chunks = m_ref.shape[0]
    piece = RANK // chunks
    batch = 2 * RANK // piece
    for g in range(slots // batch):
        rows = [g_ref[g * batch + q] for q in range(batch)]
        for c in range(chunks):
            for h in range(2):
                at = h * RANK + c * piece
                m_ref[c, 2 * g + h] = jnp.concatenate([r[:, at : at + piece] for r in rows], axis=1)
    for step, o_ref in enumerate((o0_ref, o1_ref, o2_ref, o3_ref)):
        o_ref[...] = m_ref[lax.rem(me_ref[0] + step, chunks)]


def pack(me, *arrays):
    vmem = pl.BlockSpec(memory_space=pltpu.VMEM)
    slots = arrays[4].shape[0] + arrays[5].shape[0]
    top, lanes = arrays[0].shape[1:]
    tiles = slots * RANK // 4 * top * 2 // (top * lanes)
    message = jax.ShapeDtypeStruct((tiles, top, lanes), jnp.float32)
    return pl.pallas_call(
        pack_kernel,
        in_specs=[pl.BlockSpec(memory_space=pltpu.SMEM)] + [vmem] * len(arrays),
        out_specs=(vmem,) * 4,
        out_shape=(message,) * 4,
        scratch_shapes=[
            pltpu.VMEM((slots, top, lanes), jnp.float32),
            pltpu.VMEM((4, tiles, top, lanes), jnp.float32),
        ],
        compiler_params=pltpu.CompilerParams(vmem_limit_bytes=8 * 2**20),
        name="pack",
    )(me, *arrays)


def final_kernel(me_ref, l_ref, m0_ref, m1_ref, m2_ref, m3_ref, out_ref, m_ref):
    chunks, tiles = m_ref.shape[0], m_ref.shape[1]
    for step, ref in enumerate((m0_ref, m1_ref, m2_ref, m3_ref)):
        m_ref[lax.rem(me_ref[0] + chunks - step, chunks)] = ref[...]
    share = l_ref.shape[1] - 1
    piece = RANK // chunks
    batch = 2 * RANK // piece
    for g in range(tiles // 2):
        rows = [m_ref[c, 2 * g + h] for c in range(chunks) for h in range(2)]
        turned = jnp.concatenate(rows, axis=0).T
        for q in range(batch):
            j = g * batch + q
            high, low = split(turned[q * piece : (q + 1) * piece, :])
            w_high, w_low = split(unpacked(l_ref[j // share, j % share]))
            total = jnp.dot(high, w_high, preferred_element_type=jnp.float32)
            total = total + jnp.dot(low, w_high, preferred_element_type=jnp.float32)
            out_ref[j] = total + jnp.dot(high, w_low, preferred_element_type=jnp.float32)


def final(me, packed, messages, slots):
    vmem = pl.BlockSpec(memory_space=pltpu.VMEM)
    return pl.pallas_call(
        final_kernel,
        in_specs=[pl.BlockSpec(memory_space=pltpu.SMEM)] + [vmem] * 5,
        out_specs=vmem,
        out_shape=jax.ShapeDtypeStruct((slots, RANK // 4, RANK), jnp.float32),
        scratch_shapes=[pltpu.VMEM((4,) + messages[0].shape, jnp.float32)],
        compiler_params=pltpu.CompilerParams(vmem_limit_bytes=8 * 2**20),
        name="left_factor",
    )(me, packed, *messages)


def tie(*values):
    return lax.optimization_barrier(values)


def shards(
    bases,
    leaf_transfer,
    node_transfer,
    pair_transfer,
    quad_transfer,
    coupling,
    row_device,
    row_slot,
    block_count,
):
    n_rank = lax.axis_size("rk")
    rank_index = lax.axis_index("rk")
    me = rank_index.astype(jnp.int32).reshape(1)
    n_y, n_z, n_core = (lax.axis_size(axis) for axis in ("y", "z", "core"))
    core = lax.axis_index("core")
    local = jnp.swapaxes(bases[0], 1, 2)
    leaves, width, points = local.shape
    share = leaves // n_rank

    blocks = coupling[0]
    listed = blocks.shape[1]
    plan = Plan(n_y, n_z, leaves)
    dest = row_device[0, :, :, 0]
    valid = jnp.arange(listed, dtype=jnp.int32)[None, :] < block_count[0][:, None]
    rel_z = (dest // n_core - lax.axis_index("z")) % n_z
    rel_y = (dest // (n_core * n_z) - lax.axis_index("y")) % n_y
    place = plan.places(rel_y, rel_z, row_slot[0])
    place = place + jnp.where(dest % n_core == core, plan.total, 0)
    place = jnp.where(valid, place, n_core * plan.total).reshape(-1).astype(jnp.int32)

    pieces = lax.all_to_all(local, "rk", split_axis=0, concat_axis=0, tiled=True)
    moves = lax.dynamic_slice_in_dim(leaf_transfer[0], rank_index * share, share, 0)
    mine = leaf_factors(pieces.reshape(n_rank, share, width, points), moves)
    packed = lax.all_gather(mine, "rk", axis=0, tiled=False)

    near, far = plan.near, plan.total - plan.near
    away_near, away_far, keep_near, keep_far, leaf_weights = weighted_sums(
        me, place, blocks, packed, (near, far, near, far)
    )
    got_near = swap(away_near, "core", 1)
    got_near, away_far = tie(got_near, away_far)
    got_far = swap(away_far, "core", 1)

    def along(axis, up, down):
        return shift(up, axis, 1), shift(down, axis, -1)

    y_rows, z_rows, cut, rest = plan.rows["y"], plan.rows["z"], plan.cut, plan.rest
    y_two, z_up, z_down = run_round(
        round1_kernel, plan, (y_rows, z_rows // 2, z_rows // 2), keep_near, got_near
    )
    y_two, z_up, z_down, shared = tie(y_two, z_up, z_down, packed)
    rz_up, rz_down = along("z", z_up, z_down)
    ry_two = shift(y_two, "y", 2)
    gram1, term = level(first_level_kernel, shared, node_transfer[0])
    other = swap(term, "core", 1)
    ry_two, rz_up, rz_down, got_far, other = tie(ry_two, rz_up, rz_down, got_far, other)
    sums = (keep_far, got_far)

    y_up, y_down, z_up, z_down = run_round(
        round2_kernel, plan, (y_rows,) * 2 + (z_rows,) * 2, *sums, rz_up, rz_down
    )
    y_up, y_down, z_up, z_down, term = tie(y_up, y_down, z_up, z_down, term)
    rz_up, rz_down = along("z", z_up, z_down)
    ry_up, ry_down = along("y", y_up, y_down)
    gram2, term = level(next_level_kernel, term, other, pair_transfer[0])
    other = swap(term, "z", 1)
    ry_up, ry_down, rz_up, rz_down, other = tie(ry_up, ry_down, rz_up, rz_down, other)

    ride = z_rows + cut // 2 + cut
    ey, up, down = run_round(
        round3_kernel, plan, (y_rows, ride, ride), *sums, ry_two, ry_up, ry_down, rz_up, rz_down
    )
    up, down, term = tie(up, down, term)
    ride_up, ride_down = along("z", up, down)
    gram3, term = level(next_level_kernel, term, other, quad_transfer[0])
    other = swap(term, "z", 2)
    ride_up, ride_down, other = tie(ride_up, ride_down, other)

    both = z_rows + cut
    up, down = run_round(round4_kernel, plan, (both, both), *sums, ey, ride_up, ride_down)
    up, down, term = tie(up, down, term)
    rz_up, rz_down = along("z", up, down)
    node_weights = node_lower(me, (gram1, gram2, gram3, term, other), width)
    rz_up, rz_down, node_weights = tie(rz_up, rz_down, node_weights)

    ez, y_one, y_two, y_three, z_two, z_six = run_round(
        round5_kernel, plan, (rest,) * 4 + (cut,) * 2, *sums, ey, rz_up, rz_down
    )
    z_two = shift(z_two, "z", 2)
    z_six = shift(z_six, "z", -2)
    y_one, y_three = along("y", y_one, y_three)
    y_two = shift(y_two, "y", 2)
    messages = pack(me, ey, ride_up, ride_down, z_two, z_six, ez, y_one, y_two, y_three)
    arrived = [messages[0]] + [shift(messages[s], "rk", s) for s in range(1, n_rank)]
    coupled = final(me, packed, arrived, leaves)

    return (
        jnp.swapaxes(leaf_weights, 1, 2)[None],
        jnp.swapaxes(node_weights, 1, 2)[:, None],
        jnp.swapaxes(coupled, 1, 2)[None],
    )


def solution(mesh):
    devices = mesh.devices
    fine = Mesh(devices.reshape(4, 8, 2, devices.shape[1]), ("y", "z", "core", "rk"))
    clu = ("y", "z", "core")
    placed = (
        P(clu, None, None, "rk"),
        P(clu, None, None, None),
        P(clu, None, None),
        P(clu, None, None),
        P(clu, None, None),
        P(clu, None, None, "rk", None),
        P(clu, None, None, None),
        P(clu, None, None),
        P(clu, None),
    )
    return jax.shard_map(
        shards,
        mesh=fine,
        in_specs=placed,
        out_specs=(
            P(clu, None, None, "rk"),
            P(None, clu, None, "rk"),
            P(clu, None, None, "rk"),
        ),
        check_vma=False,
    )
```

```python
import functools

import jax
import jax.numpy as jnp
from jax import lax
from jax.experimental import pallas as pl
from jax.experimental.pallas import tpu as pltpu
from jax.sharding import Mesh
from jax.sharding import PartitionSpec as P

HIGHEST = lax.Precision.HIGHEST
RANK = 64
TILE = 8
TILES = RANK // TILE


def shift(value, axis, step):
    size = lax.axis_size(axis)
    return lax.ppermute(value, axis, [(i, (i + step) % size) for i in range(size)])


def swap(value, axis, mask):
    return lax.ppermute(value, axis, [(i, i ^ mask) for i in range(lax.axis_size(axis))])


def factor_in_place(s_ref):
    batch = s_ref.shape[2]
    sub = lax.broadcasted_iota(jnp.int32, (TILE, batch), 0)
    for jb in range(TILES):
        count = TILES - jb
        base = jb * TILE
        rows = [
            [s_ref[base + k, pl.ds((jb + t) * TILE, TILE), :] for t in range(count)]
            for k in range(TILE)
        ]
        for k in range(TILE):
            scale = lax.rsqrt(rows[k][0][k : k + 1, :])
            row = [v * scale for v in rows[k]]
            row[0] = jnp.where(sub >= k, row[0], 0.0)
            rows[k] = row
            for t in range(count):
                s_ref[base + k, pl.ds((jb + t) * TILE, TILE), :] = row[t]
            for t in range(jb):
                s_ref[base + k, pl.ds(t * TILE, TILE), :] = jnp.zeros((TILE, batch), jnp.float32)
            for k2 in range(k + 1, TILE):
                s = row[0][k2 : k2 + 1, :]
                rows[k2] = [v - s * u for v, u in zip(rows[k2], row)]
        for rb in range(jb + 1, TILES):
            for r in range(rb * TILE, (rb + 1) * TILE):
                heads = [s_ref[base + k, pl.ds(r, 1), :] for k in range(TILE)]
                for ct in range(rb, TILES):
                    total = s_ref[r, pl.ds(ct * TILE, TILE), :]
                    for k in range(TILE):
                        total = total - heads[k] * rows[k][ct - jb]
                    s_ref[r, pl.ds(ct * TILE, TILE), :] = total


def to_lanes(g_ref, s_ref):
    for a in range(RANK):
        s_ref[a] = g_ref[:, a, :].T


def column_of(s_ref, c):
    return s_ref[:, c, :].T


def packed_rows(matrix):
    half = matrix.shape[0] // 2
    return jnp.concatenate([matrix[:half], matrix[half:]], axis=1)


def unpacked(rows):
    half = rows.shape[-1] // 2
    return jnp.concatenate([rows[..., :half], rows[..., half:]], axis=-2)


def leaf_kernel(x_ref, move_ref, packed_ref, gram_ref, s_ref):
    sources, leaves = x_ref.shape[0], x_ref.shape[1]
    term = None
    for m in range(leaves):
        x = jnp.concatenate([x_ref[s, m] for s in range(sources)], axis=0)
        gram_ref[m] = lax.dot_general(
            x, x, (((1,), (1,)), ((), ())), precision=HIGHEST, preferred_element_type=jnp.float32
        )
    to_lanes(gram_ref, s_ref)
    for m in range(leaves):
        move = move_ref[m]
        moved = jnp.dot(gram_ref[m], move, precision=HIGHEST, preferred_element_type=jnp.float32)
        last = jnp.dot(move.T, moved, precision=HIGHEST, preferred_element_type=jnp.float32)
        term = last if term is None else term + last
    packed_ref[leaves] = packed_rows(term)
    factor_in_place(s_ref)
    half = RANK // 2
    for c in range(half):
        packed_ref[:leaves, c, :] = jnp.concatenate(
            [column_of(s_ref, c), column_of(s_ref, c + half)], axis=1
        )


def leaf_factors(x, moves):
    leaves = x.shape[1]
    vmem = pl.BlockSpec(memory_space=pltpu.VMEM)
    return pl.pallas_call(
        leaf_kernel,
        out_shape=jax.ShapeDtypeStruct((leaves + 1, RANK // 2, 2 * RANK), jnp.float32),
        in_specs=[vmem, vmem],
        out_specs=vmem,
        scratch_shapes=[
            pltpu.VMEM((leaves, RANK, RANK), jnp.float32),
            pltpu.VMEM((RANK, RANK, leaves), jnp.float32),
        ],
        compiler_params=pltpu.CompilerParams(vmem_limit_bytes=10 * 2**20),
        name="leaf_factors",
    )(x, moves)


def level_term(level, transfer):
    moved = jnp.dot(level, transfer, precision=HIGHEST, preferred_element_type=jnp.float32)
    return jnp.dot(transfer.T, moved, precision=HIGHEST, preferred_element_type=jnp.float32)


def first_level_kernel(packed_ref, move_ref, gram_ref, term_ref):
    leaves = packed_ref.shape[1] - 1
    gram = unpacked(jnp.sum(packed_ref[:, leaves], axis=0))
    gram_ref[...] = gram
    term_ref[...] = level_term(gram, move_ref[...])


def next_level_kernel(mine_ref, other_ref, move_ref, gram_ref, term_ref):
    gram = mine_ref[...] + other_ref[...]
    gram_ref[...] = gram
    term_ref[...] = level_term(gram, move_ref[...])


def level(kernel, *arrays):
    vmem = pl.BlockSpec(memory_space=pltpu.VMEM)
    return pl.pallas_call(
        kernel,
        in_specs=[vmem] * len(arrays),
        out_specs=(vmem, vmem),
        out_shape=(jax.ShapeDtypeStruct((RANK, RANK), jnp.float32),) * 2,
        compiler_params=pltpu.CompilerParams(vmem_limit_bytes=4 * 2**20),
        name=kernel.__name__,
    )(*arrays)


def node_kernel(me_ref, g1_ref, g2_ref, g3_ref, mine_ref, other_ref, out_ref, s_ref, l_ref):
    g_ref = l_ref
    for t, ref in enumerate((g1_ref, g2_ref, g3_ref)):
        g_ref[t] = ref[...]
    g_ref[3] = mine_ref[...] + other_ref[...]
    to_lanes(g_ref, s_ref)
    factor_in_place(s_ref)
    for c in range(RANK):
        l_ref[:, c, :] = column_of(s_ref, c)
    width = out_ref.shape[1]
    out_ref[...] = l_ref[:, pl.ds(pl.multiple_of(me_ref[0] * width, width), width), :]


def node_lower(me, grams, width):
    vmem = pl.BlockSpec(memory_space=pltpu.VMEM)
    count = len(grams) - 1
    return pl.pallas_call(
        node_kernel,
        out_shape=jax.ShapeDtypeStruct((count, width, RANK), jnp.float32),
        in_specs=[pl.BlockSpec(memory_space=pltpu.SMEM)] + [vmem] * len(grams),
        out_specs=vmem,
        scratch_shapes=[
            pltpu.VMEM((RANK, RANK, count), jnp.float32),
            pltpu.VMEM((count, RANK, RANK), jnp.float32),
        ],
        compiler_params=pltpu.CompilerParams(vmem_limit_bytes=10 * 2**20),
        name="node_factors",
    )(me, *grams)


def split(value):
    high = value.astype(jnp.bfloat16)
    return high, (value - high.astype(jnp.float32)).astype(jnp.bfloat16)


def block_products(blocks, packed):
    listed, width, rank = blocks.shape
    top = width // 2
    zero = jnp.zeros((rank, rank), jnp.bfloat16)
    high, low = split(unpacked(packed))
    wide = jnp.concatenate(
        [
            blocks[:, :top, :].reshape(listed * top, rank),
            blocks[:, top:, :].reshape(listed * top, rank),
        ],
        axis=1,
    )
    w_high = jnp.concatenate(
        [jnp.concatenate([high, zero], axis=1), jnp.concatenate([zero, high], axis=1)], axis=0
    )
    w_low = jnp.concatenate(
        [jnp.concatenate([low, zero], axis=1), jnp.concatenate([zero, low], axis=1)], axis=0
    )
    c_high, c_low = split(wide)
    total = jnp.dot(
        jnp.concatenate([c_high, c_low], axis=1),
        jnp.concatenate([w_high, w_high], axis=0),
        preferred_element_type=jnp.float32,
    )
    return total + jnp.dot(c_high, w_low, preferred_element_type=jnp.float32)


def product_kernel(
    me_ref, place_ref, c_hbm, l_ref, o0_ref, o1_ref, o2_ref, o3_ref, rows_ref,
    acc_ref, c_ref, sems,
):
    leaves, listed, width, _ = c_hbm.shape
    slots, group = c_ref.shape[0], c_ref.shape[1]
    steps = leaves // group
    top = width // 2
    share = l_ref.shape[1] - 1

    def fetch(step, slot):
        return pltpu.make_async_copy(
            c_hbm.at[pl.ds(step * group, group)], c_ref.at[slot], sems.at[slot]
        )

    for step in range(slots - 1):
        fetch(step, step).start()
    acc_ref[...] = jnp.zeros_like(acc_ref)

    me = me_ref[0]
    at = pl.multiple_of(lax.rem(me, 2) * width, width)
    for j in range(leaves):
        rows = l_ref[j // share, j % share, pl.ds(at, width), :]
        rows_ref[j] = jnp.where(me < 2, rows[:, :RANK], rows[:, RANK:])

    def body(step, carry):
        slot = lax.rem(step, slots)
        ahead = step + slots - 1

        @pl.when(ahead < steps)
        def _():
            fetch(ahead, lax.rem(ahead, slots)).start()

        fetch(step, slot).wait()
        source = lax.div(step * group, share)
        first_leaf = step * group - source * share
        totals = [
            block_products(c_ref[slot, u], l_ref[source, first_leaf + u]) for u in range(group)
        ]
        for u in range(group):
            for k in range(listed):
                place = place_ref[(step * group + u) * listed + k]
                acc_ref[place] = acc_ref[place] + totals[u][k * top : (k + 1) * top, :]
        return carry

    lax.fori_loop(0, steps, body, 0)
    at = 0
    for ref in (o0_ref, o1_ref, o2_ref, o3_ref):
        ref[...] = acc_ref[at : at + ref.shape[0]]
        at += ref.shape[0]


def weighted_sums(me, place, blocks, packed, parts):
    leaves, listed, width, rank = blocks.shape
    top = width // 2
    group, slots = 4, 4
    vmem = pl.BlockSpec(memory_space=pltpu.VMEM)
    hbm = pl.BlockSpec(memory_space=pltpu.HBM)

    def out(rows):
        return jax.ShapeDtypeStruct((rows, top, 2 * rank), jnp.float32)

    return pl.pallas_call(
        product_kernel,
        in_specs=[
            pl.BlockSpec(memory_space=pltpu.SMEM),
            pl.BlockSpec(memory_space=pltpu.SMEM),
            hbm,
            vmem,
        ],
        out_specs=(vmem,) * (len(parts) + 1),
        scratch_shapes=[
            pltpu.VMEM((sum(parts) + TILE, top, 2 * rank), jnp.float32),
            pltpu.VMEM((slots, group, listed, width, rank), jnp.float32),
            pltpu.SemaphoreType.DMA((slots,)),
        ],
        out_shape=tuple(out(rows) for rows in parts)
        + (jax.ShapeDtypeStruct((leaves, width, rank), jnp.float32),),
        compiler_params=pltpu.CompilerParams(vmem_limit_bytes=16 * 2**20),
        name="weighted_sums",
    )(me, place, pltpu.with_memory_space_constraint(blocks, pltpu.HBM), packed)


class Plan:
    def __init__(self, n_y, n_z, slots):
        self.n_y, self.n_z = n_y, n_z
        self.cut = 5 * slots // 16
        self.rest = slots - self.cut
        self.rows = {"y": n_z * self.cut, "z": n_y * self.rest}
        self.base = {}
        at = 0
        for group in (
            ("y", 2), ("z", 4), ("y", 1), ("y", 3), ("z", 3), ("z", 5), ("y", 0), ("z", 2),
            ("z", 6), ("z", 1), ("z", 7), ("z", 0),
        ):
            if group == ("y", 1):
                self.near = at
            self.base[group] = at
            at += self.rows[group[0]]
        self.total = at

    def places(self, rel_y, rel_z, slot):
        base_y = sum(jnp.where(rel_y == r, self.base["y", r], 0) for r in range(self.n_y))
        base_z = sum(jnp.where(rel_z == r, self.base["z", r], 0) for r in range(self.n_z))
        by_y = base_y + rel_z * self.cut + slot
        by_z = base_z + rel_y * self.rest + slot - self.cut
        return jnp.where(slot < self.cut, by_y, by_z)

    def part(self, ref, group):
        at = self.base[group] - (0 if self.base[group] < self.near else self.near)
        return ref[at : at + self.rows[group[0]]]

    def both(self, keep, got, group):
        return self.part(keep, group) + self.part(got, group)


def low_add(whole, extra):
    rows = extra.shape[0]
    return jnp.concatenate([whole[:rows] + extra, whole[rows:]], axis=0)


def high_add(whole, extra):
    rows = whole.shape[0] - extra.shape[0]
    return jnp.concatenate([whole[:rows], whole[rows:] + extra], axis=0)


def round1_kernel(plan, keep, got, y_two, z_up, z_down):
    y_two[...] = plan.both(keep, got, ("y", 2))
    z = plan.both(keep, got, ("z", 4))
    half = z.shape[0] // 2
    z_up[...] = z[:half]
    z_down[...] = z[half:]


def round2_kernel(plan, keep, got, rz_up, rz_down, y_up, y_down, z_up, z_down):
    y_up[...] = plan.both(keep, got, ("y", 1))
    y_down[...] = plan.both(keep, got, ("y", 3))
    z_up[...] = low_add(plan.both(keep, got, ("z", 3)), rz_up[...])
    z_down[...] = high_add(plan.both(keep, got, ("z", 5)), rz_down[...])


def round3_kernel(plan, keep, got, ry_two, ry_up, ry_down, rz_up, rz_down, ey, z_up, z_down):
    ey[...] = plan.both(keep, got, ("y", 0)) + ry_two[...] + ry_up[...] + ry_down[...]
    rows, cut = plan.rows["z"], plan.cut
    half = cut // 2
    z_up[:rows] = plan.both(keep, got, ("z", 2)) + rz_up[...]
    z_up[rows : rows + half] = ey[4 * cut : 4 * cut + half]
    z_up[rows + half :] = ey[cut : 2 * cut]
    z_down[:rows] = plan.both(keep, got, ("z", 6)) + rz_down[...]
    z_down[rows : rows + half] = ey[4 * cut + half : 5 * cut]
    z_down[rows + half :] = ey[7 * cut :]


def round4_kernel(plan, keep, got, ey, rz_up, rz_down, z_up, z_down):
    rows, cut = plan.rows["z"], plan.cut
    half = cut // 2
    z_up[:rows] = plan.both(keep, got, ("z", 1)) + rz_up[:rows]
    z_up[rows:] = low_add(ey[3 * cut : 4 * cut], rz_up[rows : rows + half])
    z_down[:rows] = plan.both(keep, got, ("z", 7)) + rz_down[:rows]
    z_down[rows:] = high_add(ey[5 * cut : 6 * cut], rz_down[rows : rows + half])


def round5_kernel(plan, keep, got, ey, rz_up, rz_down, own, y_one, y_two, y_three, z_two, z_six):
    rows, cut, rest = plan.rows["z"], plan.cut, plan.rest
    ez = plan.both(keep, got, ("z", 0)) + rz_up[:rows] + rz_down[:rows]
    for r, ref in enumerate((own, y_one, y_two, y_three)):
        ref[...] = ez[r * rest : (r + 1) * rest]
    z_two[...] = ey[2 * cut : 3 * cut] + rz_up[rows:]
    z_six[...] = ey[6 * cut : 7 * cut] + rz_down[rows:]


def run_round(kernel, plan, rows, *arrays):
    vmem = pl.BlockSpec(memory_space=pltpu.VMEM)
    tail = arrays[0].shape[1:]
    return pl.pallas_call(
        functools.partial(kernel, plan),
        in_specs=[vmem] * len(arrays),
        out_specs=(vmem,) * len(rows),
        out_shape=tuple(jax.ShapeDtypeStruct((r,) + tail, jnp.float32) for r in rows),
        compiler_params=pltpu.CompilerParams(vmem_limit_bytes=12 * 2**20),
        name=kernel.__name__,
    )(*arrays)


def pack_kernel(
    me_ref, ey, z_up, z_down, z_two, z_six, ez, y_one, y_two, y_three,
    o0_ref, o1_ref, o2_ref, o3_ref, g_ref, m_ref,
):
    slots = g_ref.shape[0]
    cut = z_two.shape[0]
    skip = z_up.shape[0] - cut
    g_ref[:cut] = ey[:cut] + z_up[skip:] + z_down[skip:] + z_two[...] + z_six[...]
    g_ref[cut:] = ez[...] + y_one[...] + y_two[...] + y_three[...]
    chunks = m_ref.shape[0]
    piece = RANK // chunks
    batch = 2 * RANK // piece
    for g in range(slots // batch):
        rows = [g_ref[g * batch + q] for q in range(batch)]
        for c in range(chunks):
            for h in range(2):
                at = h * RANK + c * piece
                m_ref[c, 2 * g + h] = jnp.concatenate([r[:, at : at + piece] for r in rows], axis=1)
    for step, o_ref in enumerate((o0_ref, o1_ref, o2_ref, o3_ref)):
        o_ref[...] = m_ref[lax.rem(me_ref[0] + step, chunks)]


def pack(me, *arrays):
    vmem = pl.BlockSpec(memory_space=pltpu.VMEM)
    slots = arrays[4].shape[0] + arrays[5].shape[0]
    top, lanes = arrays[0].shape[1:]
    tiles = slots * RANK // 4 * top * 2 // (top * lanes)
    message = jax.ShapeDtypeStruct((tiles, top, lanes), jnp.float32)
    return pl.pallas_call(
        pack_kernel,
        in_specs=[pl.BlockSpec(memory_space=pltpu.SMEM)] + [vmem] * len(arrays),
        out_specs=(vmem,) * 4,
        out_shape=(message,) * 4,
        scratch_shapes=[
            pltpu.VMEM((slots, top, lanes), jnp.float32),
            pltpu.VMEM((4, tiles, top, lanes), jnp.float32),
        ],
        compiler_params=pltpu.CompilerParams(vmem_limit_bytes=8 * 2**20),
        name="pack",
    )(me, *arrays)


def final_kernel(me_ref, l_ref, m0_ref, m1_ref, m2_ref, m3_ref, out_ref, m_ref):
    chunks, tiles = m_ref.shape[0], m_ref.shape[1]
    for step, ref in enumerate((m0_ref, m1_ref, m2_ref, m3_ref)):
        m_ref[lax.rem(me_ref[0] + chunks - step, chunks)] = ref[...]
    share = l_ref.shape[1] - 1
    piece = RANK // chunks
    batch = 2 * RANK // piece
    for g in range(tiles // 2):
        rows = [m_ref[c, 2 * g + h] for c in range(chunks) for h in range(2)]
        turned = jnp.concatenate(rows, axis=0).T
        for q in range(batch):
            j = g * batch + q
            high, low = split(turned[q * piece : (q + 1) * piece, :])
            w_high, w_low = split(unpacked(l_ref[j // share, j % share]))
            total = jnp.dot(high, w_high, preferred_element_type=jnp.float32)
            total = total + jnp.dot(low, w_high, preferred_element_type=jnp.float32)
            out_ref[j] = total + jnp.dot(high, w_low, preferred_element_type=jnp.float32)


def final(me, packed, messages, slots):
    vmem = pl.BlockSpec(memory_space=pltpu.VMEM)
    return pl.pallas_call(
        final_kernel,
        in_specs=[pl.BlockSpec(memory_space=pltpu.SMEM)] + [vmem] * 5,
        out_specs=vmem,
        out_shape=jax.ShapeDtypeStruct((slots, RANK // 4, RANK), jnp.float32),
        scratch_shapes=[pltpu.VMEM((4,) + messages[0].shape, jnp.float32)],
        compiler_params=pltpu.CompilerParams(vmem_limit_bytes=8 * 2**20),
        name="left_factor",
    )(me, packed, *messages)


def tie(*values):
    return lax.optimization_barrier(values)


def shards(
    bases,
    leaf_transfer,
    node_transfer,
    pair_transfer,
    quad_transfer,
    coupling,
    row_device,
    row_slot,
    block_count,
):
    n_rank = lax.axis_size("rk")
    rank_index = lax.axis_index("rk")
    me = rank_index.astype(jnp.int32).reshape(1)
    n_y, n_z, n_core = (lax.axis_size(axis) for axis in ("y", "z", "core"))
    core = lax.axis_index("core")
    local = jnp.swapaxes(bases[0], 1, 2)
    leaves, width, points = local.shape
    share = leaves // n_rank

    blocks = coupling[0]
    listed = blocks.shape[1]
    plan = Plan(n_y, n_z, leaves)
    dest = row_device[0, :, :, 0]
    valid = jnp.arange(listed, dtype=jnp.int32)[None, :] < block_count[0][:, None]
    rel_z = (dest // n_core - lax.axis_index("z")) % n_z
    rel_y = (dest // (n_core * n_z) - lax.axis_index("y")) % n_y
    place = plan.places(rel_y, rel_z, row_slot[0])
    place = place + jnp.where(dest % n_core == core, plan.total, 0)
    place = jnp.where(valid, place, n_core * plan.total).reshape(-1).astype(jnp.int32)

    pieces = lax.all_to_all(local, "rk", split_axis=0, concat_axis=0, tiled=True)
    moves = lax.dynamic_slice_in_dim(leaf_transfer[0], rank_index * share, share, 0)
    mine = leaf_factors(pieces.reshape(n_rank, share, width, points), moves)
    packed = lax.all_gather(mine, "rk", axis=0, tiled=False)

    near, far = plan.near, plan.total - plan.near
    away_near, away_far, keep_near, keep_far, leaf_weights = weighted_sums(
        me, place, blocks, packed, (near, far, near, far)
    )
    got_near = swap(away_near, "core", 1)
    got_near, away_far = tie(got_near, away_far)
    got_far = swap(away_far, "core", 1)

    def along(axis, up, down):
        return shift(up, axis, 1), shift(down, axis, -1)

    y_rows, z_rows, cut, rest = plan.rows["y"], plan.rows["z"], plan.cut, plan.rest
    y_two, z_up, z_down = run_round(
        round1_kernel, plan, (y_rows, z_rows // 2, z_rows // 2), keep_near, got_near
    )
    y_two, z_up, z_down, shared = tie(y_two, z_up, z_down, packed)
    rz_up, rz_down = along("z", z_up, z_down)
    ry_two = shift(y_two, "y", 2)
    gram1, term = level(first_level_kernel, shared, node_transfer[0])
    other = swap(term, "core", 1)
    ry_two, rz_up, rz_down, got_far, other = tie(ry_two, rz_up, rz_down, got_far, other)
    sums = (keep_far, got_far)

    y_up, y_down, z_up, z_down = run_round(
        round2_kernel, plan, (y_rows,) * 2 + (z_rows,) * 2, *sums, rz_up, rz_down
    )
    y_up, y_down, z_up, z_down, term = tie(y_up, y_down, z_up, z_down, term)
    rz_up, rz_down = along("z", z_up, z_down)
    ry_up, ry_down = along("y", y_up, y_down)
    gram2, term = level(next_level_kernel, term, other, pair_transfer[0])
    other = swap(term, "z", 1)
    ry_up, ry_down, rz_up, rz_down, other = tie(ry_up, ry_down, rz_up, rz_down, other)

    ride = z_rows + cut // 2 + cut
    ey, up, down = run_round(
        round3_kernel, plan, (y_rows, ride, ride), *sums, ry_two, ry_up, ry_down, rz_up, rz_down
    )
    up, down, term = tie(up, down, term)
    ride_up, ride_down = along("z", up, down)
    gram3, term = level(next_level_kernel, term, other, quad_transfer[0])
    other = swap(term, "z", 2)
    ride_up, ride_down, other = tie(ride_up, ride_down, other)

    both = z_rows + cut
    up, down = run_round(round4_kernel, plan, (both, both), *sums, ey, ride_up, ride_down)
    up, down, term = tie(up, down, term)
    rz_up, rz_down = along("z", up, down)
    node_weights = node_lower(me, (gram1, gram2, gram3, term, other), width)
    rz_up, rz_down, node_weights = tie(rz_up, rz_down, node_weights)

    ez, y_one, y_two, y_three, z_two, z_six = run_round(
        round5_kernel, plan, (rest,) * 4 + (cut,) * 2, *sums, ey, rz_up, rz_down
    )
    z_two = shift(z_two, "z", 2)
    z_six = shift(z_six, "z", -2)
    y_one, y_three = along("y", y_one, y_three)
    y_two = shift(y_two, "y", 2)
    messages = pack(me, ey, ride_up, ride_down, z_two, z_six, ez, y_one, y_two, y_three)
    arrived = [messages[0]] + [shift(messages[s], "rk", s) for s in range(1, n_rank)]
    coupled = final(me, packed, arrived, leaves)

    return (
        jnp.swapaxes(leaf_weights, 1, 2)[None],
        jnp.swapaxes(node_weights, 1, 2)[:, None],
        jnp.swapaxes(coupled, 1, 2)[None],
    )


def solution(mesh):
    devices = mesh.devices
    fine = Mesh(devices.reshape(4, 8, 2, devices.shape[1]), ("y", "z", "core", "rk"))
    clu = ("y", "z", "core")
    placed = (
        P(clu, None, None, "rk"),
        P(clu, None, None, None),
        P(clu, None, None),
        P(clu, None, None),
        P(clu, None, None),
        P(clu, None, None, "rk", None),
        P(clu, None, None, None),
        P(clu, None, None),
        P(clu, None),
    )
    return jax.shard_map(
        shards,
        mesh=fine,
        in_specs=placed,
        out_specs=(
            P(clu, None, None, "rk"),
            P(None, clu, None, "rk"),
            P(clu, None, None, "rk"),
        ),
        check_vma=False,
    )
```
